256 devices in a mesh: ctx: 16 (over y_lo, z), tp: 8 (over x, core), role: 2 (over y_hi).
Axes of the slice: x: 4, y: 4 (y_hi: 2, y_lo: 2; y = y_hi * 2 + y_lo), z: 8, core: 2. Of those that a mesh axis runs over, the one named last changes fastest.
Arguments:
- token_ids: int32 [2, 2048], P('role', 'ctx'), may hold values from 0 to 65535
- embed_table: bfloat16 [65536, 7168], P(('ctx', 'role'), 'tp'), may hold values from -6 to 6
- latent_down: bfloat16 [7168, 576], P('tp'), may hold values from -0.0625 to 0.0625
- latent_gain: float32 [512], replicated, may hold values from 0.1 to 1.9
- prefill_query: bfloat16 [2048, 64, 576], P('ctx', 'tp'), may hold values from -120 to 120
- decode_query: bfloat16 [1024, 2, 64, 576], P(('ctx', 'tp')), may hold values from -120 to 120
- latent_cache: bfloat16 [1024, 512, 576], P(('ctx', 'tp')), may hold values from -6 to 6
- cache_length: int32 [1024], P(('ctx', 'tp')), may hold values from 1 to 512, as said below
- prompt_owner: int32 [2], replicated, may hold values from 0 to 15
Outputs:
- attended: bfloat16 [2, 2048, 32768], P('role', 'ctx', 'tp')
The draws below stay inside these ranges and needn't reach their ends.
Inputs may be any that keep to these rules, and one draw needn't show every extreme that they name: `cache_length`: some row has exactly 512.
All inputs are finite; a program needn't handle non-finite values.
Results may differ from the reference program's by a relative error of at most 0.0099.
Values may be sent and summed in bfloat16 or wider, within the bound.
No kernel may reach another device: no remote copies, remote signals or barrier semaphores. Data moves between devices by JAX's collectives and lax.ppermute only.
A program may use at most 128 MiB of HBM per device.

```python
import math
import jax
import jax.numpy as jnp
import numpy as np
from jax import lax

D = 7168
LAT = 512
HEADS = 64
ROW_DEV = 8
STEPS = 2
PROMPTS = 2
CACHE = 512
KVW = 576
VOCAB = 65536
SEC_ROWS = 2048
LEN = 1024
ROWS = 1024
N_CTX = 16
N_TP = 8


def draw_prefill_query(key, part):
    key = jax.random.fold_in(key, 11)
    shape = (SEC_ROWS, HEADS, KVW)
    values = jax.random.truncated_normal(key, -6.0, 6.0, shape, jnp.float32)
    return values.astype(jnp.bfloat16)


def draw_decode_query(key, part):
    key = jax.random.fold_in(key, 13)
    shape = (ROWS, STEPS, HEADS, KVW)
    values = jax.random.truncated_normal(key, -6.0, 6.0, shape, jnp.float32)
    return values.astype(jnp.bfloat16)


def draw_cache_length(key, part):
    key = jax.random.fold_in(key, 17)
    lengths = jax.random.randint(key, (ROWS,), 1, CACHE + 1, dtype=jnp.int32)
    chosen = jax.random.randint(jax.random.fold_in(key, 3), (), 0, ROWS, dtype=jnp.int32)
    return lengths.at[chosen].set(CACHE)


def with_ends(drawn, stream_key, least, top_value):
    longest = drawn.shape.index(max(drawn.shape))
    spots = []
    for shift in (0, 1):
        where = [jax.random.randint(jax.random.fold_in(stream_key, axis), (), 0, length) for axis, length in enumerate(drawn.shape)]
        where[longest] = (where[longest] + shift) % drawn.shape[longest]
        spots.append(tuple(where))
    return drawn.at[spots[0]].set(least).at[spots[1]].set(top_value)


def block_levels(rng, dims, cuts, low, top_value):
    gain = 1.0
    for dim, blocks in cuts:
        draws = jax.random.uniform(jax.random.fold_in(jax.random.fold_in(rng, 6), dim), (blocks,), jnp.float32, low / len(cuts), top_value / len(cuts))
        gain = gain * jnp.repeat(jnp.exp(draws), dims[dim] // blocks).reshape((-1,) + (1,) * (len(dims) - 1 - dim))
    return gain


def rank_table(number_of, lean):
    portions = [(1 << 20) // math.isqrt(grade ** lean) + 1 for grade in range(1, number_of + 1)]
    deviation = 1 + sum(portions) // (1 << 30)
    return np.cumsum(np.array([max(1, weight // deviation) for weight in portions]))


def ranked_ids(key, extent, number_of, slope):
    table = rank_table(number_of, slope)
    ticket = jax.random.randint(jax.random.fold_in(key, 1), extent, 0, int(table[number_of - 1]))
    grade = jnp.searchsorted(jnp.asarray(table, jnp.int32), ticket, side="right")
    return jax.random.permutation(jax.random.fold_in(key, 2), number_of)[grade].astype(jnp.int32)


def scatter_about(rng, dims, deviation, reach, split=(), kind=jnp.bfloat16):
    values = jax.random.normal(rng, dims, jnp.float32) * deviation
    if len(split) > 0:
        values = block_levels(rng, dims, split, -0.22, 0.18) * values
    return jnp.clip(values, min=-reach, max=reach).astype(kind)


def setup_inputs(seed: int = 0) -> dict:
    key_list = jax.random.split(jax.random.key(seed), 10)
    token_ids = with_ends(ranked_ids(key_list[0], (2, SEC_ROWS), VOCAB, 2), jax.random.fold_in(key_list[0], 3), 0, VOCAB - 1).astype(jnp.int32)
    embed_table = scatter_about(key_list[1], (VOCAB, D), 1.0, 6.0, ((0, 32), (1, 8)))
    latent_down = scatter_about(key_list[2], (D, KVW), D ** -0.5, 0.0625, ((0, 8),))
    latent_gain = jnp.clip(1.0 + 0.18 * jax.random.normal(key_list[3], (LAT,), jnp.float32), 0.1, 1.9)
    prefill_query = draw_prefill_query(jax.random.fold_in(key_list[9], 71), 0)
    decode_query = draw_decode_query(jax.random.fold_in(key_list[9], 71), 0)
    latent_cache = scatter_about(key_list[6], (ROWS, CACHE, KVW), 1.0, 6.0, ((0, 128),))
    cache_length = draw_cache_length(jax.random.fold_in(key_list[9], 71), 0)
    prompt_owner = jax.random.randint(key_list[8], (PROMPTS,), 0, N_CTX).astype(jnp.int32)
    return dict(token_ids=token_ids, embed_table=embed_table, latent_down=latent_down, latent_gain=latent_gain, prefill_query=prefill_query, decode_query=decode_query, latent_cache=latent_cache, cache_length=cache_length, prompt_owner=prompt_owner)


score_scale = 0.07216878364870322
masked_fill = -1e+30
norm_eps = 1e-06
rope_base = 10000.0

def finish_keys(latent, latent_gain, position):
    plain = latent[:, :LAT]
    scaled = plain * lax.rsqrt(lax.optimization_barrier(jnp.mean(plain * plain, axis=-1, keepdims=True)) + norm_eps) * latent_gain
    rotary = latent[:, LAT:]
    half_width = rotary.shape[-1] // 2
    frequency = rope_base ** (-jnp.arange(half_width, dtype=jnp.float32) / half_width)
    angles = position.astype(jnp.float32)[:, None] * frequency[None, :]
    first_half = rotary[:, :half_width]
    second_half = rotary[:, half_width:]
    turned = jnp.concatenate([first_half * jnp.cos(angles) - second_half * jnp.sin(angles), first_half * jnp.sin(angles) + second_half * jnp.cos(angles)], axis=-1)
    return lax.optimization_barrier(jnp.concatenate([scaled, turned], axis=-1).astype(jnp.bfloat16))

def rounded_weights(weights):
    return lax.optimization_barrier(weights.astype(jnp.bfloat16)).astype(jnp.float32)

def reference(token_ids, embed_table, latent_down, latent_gain, prefill_query, decode_query, latent_cache, cache_length, prompt_owner):
    rows_total = token_ids.shape[1]
    embedded = embed_table[token_ids.reshape(-1)]
    latent = jnp.dot(embedded, latent_down, preferred_element_type=jnp.float32).reshape(2, rows_total, -1)
    row_index = jnp.arange(rows_total, dtype=jnp.int32)
    prompt_keys = finish_keys(latent[0], latent_gain, row_index // PROMPTS)
    decode_pos = cache_length[row_index // STEPS] + row_index % STEPS
    decode_keys = finish_keys(latent[1], latent_gain, decode_pos)
    causal = row_index[:LEN, None] >= row_index[None, :LEN]
    outputs = []
    for prompt in range(PROMPTS):
        query = prefill_query[prompt::PROMPTS].astype(jnp.float32)
        block_keys = prompt_keys[prompt::PROMPTS].astype(jnp.float32)
        scores = jnp.einsum('qhc,kc->hqk', query, block_keys) * score_scale
        scores = jnp.where(causal[None], scores, masked_fill)
        highest = lax.optimization_barrier(jnp.max(scores, axis=-1, keepdims=True))
        weights = jnp.where(causal[None], jnp.exp(scores - highest), 0.0)
        total = lax.optimization_barrier(jnp.sum(weights, axis=-1))
        mixed = jnp.einsum('hqk,kc->hqc', rounded_weights(weights), block_keys[:, :LAT])
        outputs.append(jnp.transpose(mixed / total[:, :, None], (1, 0, 2)))
    prefill_out = jnp.stack(outputs, axis=1).reshape(rows_total, HEADS, LAT).astype(jnp.bfloat16)
    group_rows = ROW_DEV * N_TP
    all_prompt = prompt_keys.astype(jnp.float32)
    key_owner = prompt_owner[jnp.arange(PROMPTS * LEN, dtype=jnp.int32) % PROMPTS]
    step_index = jnp.arange(STEPS, dtype=jnp.int32)
    fresh_ok = (step_index[None, :] <= step_index[:, None])[None, :, None, :]

    def one_group(inputs):
        group, query, cached, lengths, newest = inputs
        query = query.astype(jnp.float32)
        cached = cached.astype(jnp.float32)
        newest = newest.astype(jnp.float32)
        cache_scores = jnp.einsum('rshc,rkc->rshk', query, cached) * score_scale
        cache_ok = (jnp.arange(CACHE, dtype=jnp.int32)[None, :] < lengths[:, None])[:, None, None, :]
        cache_scores = jnp.where(cache_ok, cache_scores, masked_fill)
        prompt_scores = jnp.einsum('rshc,kc->rshk', query, all_prompt) * score_scale
        prompt_ok = (key_owner == group)[None, None, None, :]
        prompt_scores = jnp.where(prompt_ok, prompt_scores, masked_fill)
        fresh_scores = jnp.einsum('rshc,rtc->rsht', query, newest) * score_scale
        fresh_scores = jnp.where(fresh_ok, fresh_scores, masked_fill)
        highest = jnp.maximum(jnp.maximum(lax.optimization_barrier(jnp.max(cache_scores, axis=-1)), lax.optimization_barrier(jnp.max(prompt_scores, axis=-1))), lax.optimization_barrier(jnp.max(fresh_scores, axis=-1)))
        cache_w = jnp.where(cache_ok, jnp.exp(cache_scores - highest[..., None]), 0.0)
        prompt_w = jnp.where(prompt_ok, jnp.exp(prompt_scores - highest[..., None]), 0.0)
        fresh_w = jnp.where(fresh_ok, jnp.exp(fresh_scores - highest[..., None]), 0.0)
        total = lax.optimization_barrier(jnp.sum(cache_w, axis=-1)) + lax.optimization_barrier(jnp.sum(prompt_w, axis=-1)) + lax.optimization_barrier(jnp.sum(fresh_w, axis=-1))
        mixed = jnp.einsum('rshk,rkc->rshc', rounded_weights(cache_w), cached[..., :LAT])
        mixed = mixed + jnp.einsum('rshk,kc->rshc', rounded_weights(prompt_w), all_prompt[:, :LAT])
        mixed = mixed + jnp.einsum('rsht,rtc->rshc', rounded_weights(fresh_w), newest[..., :LAT])
        return (mixed / total[..., None]).astype(jnp.bfloat16)
    decode_out = lax.map(one_group, (jnp.arange(N_CTX, dtype=jnp.int32), decode_query.reshape(N_CTX, group_rows, STEPS, HEADS, -1), latent_cache.reshape(N_CTX, group_rows, CACHE, -1), cache_length.reshape(N_CTX, group_rows), decode_keys.reshape(N_CTX, group_rows, STEPS, -1)))
    decode_out = decode_out.reshape(rows_total, HEADS, LAT)
    return jnp.stack([prefill_out, decode_out]).reshape(2, rows_total, HEADS * LAT)
```

```python
import jax
import jax.numpy as jnp
import numpy as np
from jax import lax
from jax.experimental import pallas as pl
from jax.experimental.pallas import tpu as pltpu
from jax.sharding import Mesh
from jax.sharding import PartitionSpec as P

LAT = 512
KVW = 576
STEPS = 2
WIDE = 640
SLOTS = 16
KEPT = 48
SIDE = 16 * KEPT
KEYS = 2048

score_scale = 0.07216878364870322
masked_fill = -1e30
norm_eps = 1e-06
rope_base = 10000.0
bf16 = jnp.bfloat16
f32 = jnp.float32
SMEM = pltpu.SMEM
VMEM = pltpu.VMEM

HOLDERS = ("ylo", "z", "role")
PLANE = ("ylo", "role", "x")
TP = ("x", "core")


def iota(shape, axis):
    return lax.broadcasted_iota(jnp.int32, shape, axis)


def ones_where(flags):
    return jnp.where(flags, 1.0, 0.0).astype(bf16)


def dot(left, right):
    return lax.dot_general(left, right, (((1,), (0,)), ((), ())), preferred_element_type=f32)


def dot_nt(left, right):
    return lax.dot_general(left, right, (((1,), (1,)), ((), ())), preferred_element_type=f32)


def whole_loop(count, body, unroll=1):
    def step(index, carry):
        body(index)
        return carry

    lax.fori_loop(0, count, step, 0, unroll=unroll)


def aligned(index, size):
    return pl.ds(pl.multiple_of(index * size, size), size)


def select_kernel(place, ids, table, down, partial, hots, lows, chosen, table_here, down_here, sems):
    holder = place[0]
    table_copy = pltpu.make_async_copy(table, table_here, sems.at[0])
    down_copy = pltpu.make_async_copy(down, down_here, sems.at[1])
    table_copy.start()
    down_copy.start()

    def mark(block):
        tokens = ids[pl.ds(block, 1), :]
        span = aligned(block, 128)
        hots[:, span] = ones_where(iota((16, 128), 0) == (tokens >> 7) - holder * 16)
        lows[:, span] = ones_where(iota((128, 128), 0) == (tokens & 127))

    whole_loop(32, mark, 8)
    odd = ((iota((16, 4096), 1) >> 7) & 1) == 1
    both = hots[...]
    decodes = jnp.where(odd, both, jnp.zeros_like(both))
    in_prompt = dot_nt(both - decodes, lows[...]) > 0.5
    alone = (dot_nt(decodes, lows[...]) > 0.5) & jnp.logical_not(in_prompt)
    upper = ones_where(iota((128, 128), 0) < iota((128, 128), 1))
    all_ones = jnp.ones((128, 128), bf16)
    row = iota((8 * SLOTS, 128), 0)
    wanted = ((row & 15) * 8 + (((row >> 4) - holder) & 7)).astype(f32)
    before = jnp.zeros((1, 128), f32)
    ranks = []
    for present in (in_prompt, alone):
        flags = ones_where(present)
        within = dot(flags, upper)
        totals = dot(flags, all_ones)
        lines = []
        for step in range(16):
            lines.append(within[step : step + 1, :] + before)
            before = before + totals[step : step + 1, :]
        ranks.append(lines)
    for step in range(16):
        rank = jnp.where(alone[step : step + 1, :], ranks[1][step], -1.0)
        rank = jnp.where(in_prompt[step : step + 1, :], ranks[0][step], rank)
        chosen[:, step * 128 : (step + 1) * 128] = ones_where(wanted == rank)
    table_copy.wait()
    rows = dot(chosen[...], table_here[...]).astype(bf16)
    down_copy.wait()
    partial[...] = dot_nt(rows, down_here[...]).reshape(partial.shape)


def place_kernel(place, ids, columns, kept, fits, highs, lows, quads, holders, sheet, sheet_b):
    ylo, zed, ex, core, section = place[0], place[1], place[2], place[3], place[4]
    square = (128, 128)
    lane = iota((8, 128), 1)
    target = iota(square, 1)
    mover = ones_where(iota(square, 0) == jnp.where(target < 64, 2 * target, 2 * target - 127))
    plain = ids[pl.ds(0, 16, stride=2), :]
    coarse = (plain >> 8).astype(f32).astype(bf16)
    fine = (plain & 255).astype(f32).astype(bf16)
    moved = dot(coarse, mover) * 256.0 + dot(fine, mover)
    sheet[0:16, :] = moved.astype(jnp.int32)
    even = sheet[pl.ds(0, 8, stride=2), :]
    odd = sheet[pl.ds(1, 8, stride=2), :]
    first = jnp.where(lane < 64, even, pltpu.roll(odd, 64, 1))
    second = jnp.where(lane < 64, pltpu.roll(even, 64, 1), odd)
    tokens = jnp.concatenate([first, second, ids[pl.ds(1, 16, stride=2), :]], axis=0)
    sheet[0:32, :] = tokens

    def mark(block):
        line = sheet[pl.ds(block, 1), :]
        span = aligned(block, 128)
        highs[:, span] = ones_where(iota((512, 128), 0) == (line >> 7))
        lows[:, span] = ones_where(iota(square, 0) == (line & 127))

    whole_loop(32, mark, 8)
    in_prompt = dot_nt(lows[:, :KEYS], highs[:, :KEYS]) > 0.5
    alone = (dot_nt(lows[:, KEYS:], highs[:, KEYS:]) > 0.5) & jnp.logical_not(in_prompt)
    below = ones_where(iota(square, 1) < iota(square, 0))
    all_ones = jnp.ones(square, bf16)
    wide = (512, 512)
    same = (iota(wide, 0) // 16) == (iota(wide, 1) // 16)
    in_holder = ones_where(same & (iota(wide, 0) < iota(wide, 1)))
    prompt_flags = ones_where(in_prompt)
    alone_flags = ones_where(alone)
    prompt_columns = dot(all_ones, prompt_flags).astype(bf16)
    alone_columns = dot(all_ones, alone_flags).astype(bf16)
    prompt_rank = dot(below, prompt_flags) + dot(prompt_columns, in_holder)
    alone_rank = (
        dot(below, alone_flags) + dot(alone_columns, in_holder) + dot(prompt_columns, ones_where(same))
    )
    rank = jnp.where(in_prompt, prompt_rank, jnp.where(alone, alone_rank, 0.0))
    top_rank = jnp.max(jnp.max(rank, axis=0, keepdims=True), axis=1, keepdims=True)
    coded = (jnp.minimum(rank, 127.0) + jnp.where(in_prompt, 128.0, 0.0)).astype(bf16)
    pieces = []
    for chunk in range(4):
        span = slice(chunk * 1024, (chunk + 1) * 1024)
        looked = dot(coded, highs[:, span]) * lows[:, span].astype(f32)
        line = jnp.sum(looked, axis=0, keepdims=True)
        for part in range(8):
            pieces.append(line[:, part * 128 : (part + 1) * 128])
    value = jnp.concatenate(pieces, axis=0).astype(jnp.int32)
    ranks = value & 127
    holder = tokens >> 11
    tp_of = (ranks + holder) & 7
    quad = tp_of * 16 + (ranks >> 3)
    sheet[0:32, :] = quad
    sheet[32:64, :] = holder
    sheet[64:96, :] = jnp.where(value >= 128, -1, tp_of)

    def spot(block, source):
        span = aligned(block, 128)
        quads[:, span] = ones_where(iota(square, 0) == sheet[pl.ds(source, 1), :])
        holders[:, span] = ones_where(iota(square, 0) == sheet[pl.ds(source + 32, 1), :])

    whole_loop(16, lambda block: spot(block, block), 8)
    for part in range(2):
        spot(16 + part, 16 + part * 8 + zed)
    spot(18, 16 + ylo * 8 + zed)
    counted = dot_nt(quads[:, :KEYS], holders[:, :KEYS])
    newest = dot_nt(quads[:, KEYS : KEYS + 256], holders[:, KEYS : KEYS + 256])
    held = (counted + newest) > 0.5
    held_flags = ones_where(held)
    up, down = iota(square, 0), iota(square, 1)
    same_tp = (up // 16) == (down // 16)
    same_pool = ((up >> 4) == (down >> 4)) & ((up & 1) == (down & 1))
    pool = ones_where(same_pool)
    before = ones_where(same_pool & (up < down))
    in_tp = ones_where(same_tp & (down < up))
    position = dot(in_tp, held_flags) + dot(dot(ones_where(same_tp), held_flags).astype(bf16), before)
    position = jnp.where(held, jnp.minimum(position, 255.0), 255.0)
    gather_tp = ones_where(up == (down >> 4))
    sheet_b[...] = dot(dot(gather_tp, ones_where(counted > 0.5)).astype(bf16), pool)

    def extras(plane, worst):
        fresh = []
        owners = []
        for part in range(2):
            source = 16 + part * 8 + plane
            fresh.append(ones_where(iota(square, 0) == sheet[pl.ds(source + 64, 1), :]))
            owners.append(ones_where(iota(square, 0) == sheet[pl.ds(source + 32, 1), :]))
        added = dot_nt(jnp.concatenate(fresh, axis=1), jnp.concatenate(owners, axis=1))
        needed = sheet_b[...] + dot(added.astype(bf16), pool)
        return jnp.maximum(worst, needed)

    needed = lax.fori_loop(0, 8, extras, jnp.zeros(square, f32), unroll=4)
    needed = jnp.max(jnp.max(needed, axis=0, keepdims=True), axis=1, keepdims=True)
    enough = (top_rank < 8.0 * SLOTS) & (needed <= float(KEPT))
    fits[0, 0] = jnp.max(jnp.where(enough, 1, 0))
    position_b = position.astype(bf16)
    looked = dot(position_b, holders[...]) * quads[...].astype(f32)
    line = jnp.sum(looked, axis=0, keepdims=True)
    found = [line[:, block * 128 : (block + 1) * 128] for block in range(19)]
    found = jnp.concatenate(found + [jnp.zeros((5, 128), f32)], axis=0)
    own = 16 + ylo * 8 + zed
    quad_rows = jnp.concatenate(
        [sheet[0:16, :], jnp.zeros((2, 128), jnp.int32), sheet[pl.ds(own, 1), :], jnp.zeros((5, 128), jnp.int32)], axis=0
    )
    holder_rows = jnp.concatenate(
        [sheet[32:48, :], jnp.zeros((2, 128), jnp.int32), sheet[pl.ds(own + 32, 1), :], jnp.zeros((5, 128), jnp.int32)],
        axis=0,
    )
    tp_rows = quad_rows >> 4
    source = ((holder_rows >> 4) * 2 + (holder_rows & 1)) * 4 + (tp_rows >> 1)
    side = jnp.where((tp_rows & 1) == core, 0, SIDE)
    final = found + (source * KEPT + side).astype(f32)
    tp_index = ex * 2 + core
    turned = pltpu.roll(final, (128 - tp_index * 16) % 128, 1)
    turned = jnp.where(iota((24, 128), 1) < 16, turned, -1.0)
    final = jnp.where(iota((24, 128), 0) == 18, turned, final)
    final = jnp.concatenate([final, jnp.zeros((104, 128), f32)], axis=0)
    columns[...] = jnp.transpose(final).astype(jnp.int32)
    sheet_b[...] = position
    mine = sheet_b[pl.ds(pl.multiple_of(tp_index * 16, 16), 16), :].astype(bf16)
    spread = dot(mine, ones_where(up == (ylo * 8 + (down >> 4)) * 2 + section))
    few = (16, 128)
    spread = jnp.where((iota(few, 1) & 15) == iota(few, 0), spread, 0.0)
    kept[...] = jnp.broadcast_to(jnp.sum(spread, axis=0, keepdims=True), kept.shape)


def finish_kernel(parts, gain, sent):
    latent = parts[0]
    for tp in range(1, parts.shape[0]):
        latent = latent + parts[tp]
    plain = latent[:, :LAT]
    scaled = plain * lax.rsqrt(jnp.mean(plain * plain, axis=-1, keepdims=True) + norm_eps) * gain[...]
    rotary = latent[:, LAT:]
    coarse = rotary.astype(bf16)
    fine = (rotary - coarse.astype(f32)).astype(bf16)
    row = jnp.concatenate([scaled.astype(bf16), coarse, fine], axis=-1)
    for peer in range(sent.shape[0]):
        sent[peer] = row


def keep_kernel(kept, rows, sent):
    chosen = iota((KEPT, 128), 0).astype(f32) == kept[0:1, :]
    row = dot(ones_where(chosen), rows[...]).astype(bf16)
    for peer in range(sent.shape[0]):
        sent[peer] = row


def cache_kernel(lengths, query, cache, out, level):
    length = lengths[pl.program_id(0)]
    scores = dot(query[0], cache[0]) * score_scale
    scores = jnp.where(iota(scores.shape, 1) < length, scores, masked_fill)
    highest = jnp.max(scores, axis=-1, keepdims=True)
    weights = jnp.exp(scores - highest)
    total = jnp.sum(weights, axis=-1, keepdims=True)
    out[...] = (dot_nt(weights.astype(bf16), cache[0, :LAT, :]) / total).astype(bf16)
    level[...] = jnp.broadcast_to(highest + jnp.log(total), level.shape)


def hot_rows(hot, columns, prompt, side):
    for block in range(8):
        wanted = jnp.sum(jnp.where(iota((128, 128), 1) == prompt * 8 + block, columns[...], 0), axis=1, keepdims=True)
        hot[block * 128 : (block + 1) * 128, :] = ones_where(iota((128, SIDE), 1) == wanted - side * SIDE)


def fresh_hot(columns, side):
    return ones_where(iota((128, SIDE), 1) == columns[:, 18:19] - side * SIDE)


def put_keys(keys, span, found, factor):
    turning = found[:, LAT:]
    turning = turning + pltpu.roll(turning, 64, 1)
    turned = turning * factor + pltpu.roll(turning, 32, 1) * pltpu.roll(factor, 64, 1)
    keys[span, :LAT] = found[:, :LAT].astype(bf16)
    keys[span, LAT:] = turned[:, : KVW - LAT].astype(bf16)


def copy_in(source, target, sem):
    copy = pltpu.make_async_copy(source, target, sem)
    copy.start()
    copy.wait()


def fold(query, some, allowed, highest, total, mixed, span):
    scores = dot_nt(query, some[:, :]) * score_scale
    if allowed is not None:
        scores = jnp.where(allowed(scores.shape), scores, masked_fill)
    old = highest[span, 0:1]
    new = jnp.maximum(old, jnp.max(scores, axis=-1, keepdims=True))
    weights = jnp.exp(scores - new)
    factor = jnp.exp(old - new)
    summed = total[span, 0:1] * factor + jnp.sum(weights, axis=-1, keepdims=True)
    mixed[span, :] = mixed[span, :] * factor + dot(weights.astype(bf16), some[:, :LAT])
    highest[span, :] = jnp.broadcast_to(new, (scores.shape[0], 128))
    total[span, :] = jnp.broadcast_to(summed, (scores.shape[0], 128))


def near_kernel(place, owner, slots, columns, near, hot):
    group = place[0] * 8 + place[1]

    @pl.when(place[4] == 1)
    def _():
        near[KEYS : KEYS + 128, :] = dot(fresh_hot(columns, 0), slots[...]).astype(bf16)

        def open_prompt(prompt):
            @pl.when(owner[prompt] == group)
            def _():
                hot_rows(hot, columns, prompt, 0)

                def open_part(part):
                    near[aligned(prompt * 2 + part, 512), :] = dot(hot[aligned(part, 512), :], slots[...]).astype(bf16)

                whole_loop(2, open_part)

        whole_loop(2, open_prompt)


def decode_kernel(
    place, owner, fits, near, others, columns, factors, new_factors, query, earlier, level, spare, spare_new,
    out, keys, hot, highest, total, mixed, lines, sem
):
    group = place[0] * 8 + place[1]
    fitting = fits[0, 0] == 1

    @pl.when(place[4] == 1)
    def _():
        @pl.when(fitting)
        def _():
            found = near[KEYS : KEYS + 128, :].astype(f32) + dot(fresh_hot(columns, 1), others[...])
            put_keys(keys, slice(KEYS, KEYS + 128), found, new_factors[...])

        @pl.when(jnp.logical_not(fitting))
        def _():
            copy_in(spare_new, keys.at[pl.ds(KEYS, 128)], sem)

        newest = keys[KEYS : KEYS + 128, :]

        def begin(piece):
            span = aligned(piece, 512)
            scores = dot_nt(query[span, :], newest) * score_scale
            key = iota(scores.shape, 1)
            row = iota(scores.shape, 0) + piece * 512
            allowed = ((key >> 1) == (row >> 7)) & ((key & 1) <= ((row >> 6) & 1))
            scores = jnp.where(allowed, scores, masked_fill)
            old = level[span, 0:1]
            new = jnp.maximum(old, jnp.max(scores, axis=-1, keepdims=True))
            weights = jnp.exp(scores - new)
            factor = jnp.exp(old - new)
            summed = factor + jnp.sum(weights, axis=-1, keepdims=True)
            mixed[span, :] = earlier[span, :].astype(f32) * factor + dot(weights.astype(bf16), newest[:, :LAT])
            highest[span, :] = jnp.broadcast_to(new, (512, 128))
            total[span, :] = jnp.broadcast_to(summed, (512, 128))

        whole_loop(2, begin)

        def add_prompt(prompt):
            @pl.when(owner[prompt] == group)
            def _():
                @pl.when(fitting)
                def _():
                    hot_rows(hot, columns, prompt, 1)

                    def open_part(part):
                        span = aligned(prompt * 2 + part, 512)
                        found = near[span, :].astype(f32) + dot(hot[aligned(part, 512), :], others[...])
                        put_keys(keys, span, found, factors[aligned(part, 512), :])

                    whole_loop(2, open_part)

                @pl.when(jnp.logical_not(fitting))
                def _():
                    copy_in(spare.at[pl.ds(prompt * 1024, 1024)], keys.at[pl.ds(prompt * 1024, 1024)], sem)

                def add_part(piece):
                    span = aligned(piece, 512)
                    fold(query[span, :], keys[aligned(prompt, 1024), :], None, highest, total, mixed, span)

                whole_loop(2, add_part)

        whole_loop(2, add_prompt)

        for piece in range(4):
            span = slice(piece * 256, (piece + 1) * 256)
            quotient = mixed[span, :] / total[span, 0:1]
            for column in range(4):
                lines[column, span, :] = quotient[:, column * 128 : (column + 1) * 128]

        def tp_rows(tp):
            for head in range(8):
                for column in range(4):
                    some = lines[column, pl.ds(tp * 8 + head, 16, stride=64), :]
                    start = head * LAT + column * 128
                    out[aligned(tp, 16), start : start + 128] = some.astype(bf16)

        whole_loop(8, tp_rows)


def prefill_kernel(
    place, fits, slots, others, columns, factors, query, spare, out, keys, hot, highest, total, mixed, lines, sem
):
    group = place[0] * 8 + place[1]
    fitting = fits[0, 0] == 1

    @pl.when(place[4] == 0)
    def _():
        highest[...] = jnp.full(highest.shape, masked_fill, f32)
        total[...] = jnp.zeros(total.shape, f32)
        mixed[...] = jnp.zeros(mixed.shape, f32)

        def add_prompt(prompt):
            @pl.when(fitting)
            def _():
                for side in range(2):
                    hot_rows(hot, columns, prompt, side)

                    def open_part(part, side=side):
                        span = aligned(part, 512)
                        if side == 0:
                            lines[span, :] = dot(hot[span, :], slots[...])
                        else:
                            found = lines[span, :] + dot(hot[span, :], others[...])
                            put_keys(keys, span, found, factors[span, :])

                    whole_loop(2, open_part)

            @pl.when(jnp.logical_not(fitting))
            def _():
                copy_in(spare.at[pl.ds(prompt * 1024, 1024)], keys, sem)

            def causal(shape):
                last = (iota((shape[0], 1), 0) & 63) + group * 64
                return iota(shape, 1) <= last

            span = aligned(prompt, 512)
            fold(query[span, :], keys[...], causal, highest, total, mixed, span)
            mixed[span, :] = mixed[span, :] / total[span, 0:1]

        whole_loop(2, add_prompt)

        def head_rows(head):
            for column in range(4):
                for prompt in range(2):
                    some = mixed[pl.ds(pl.multiple_of(prompt * 512 + head * 64, 64), 64), column * 128 : (column + 1) * 128]
                    highest[pl.ds(prompt, 64, stride=2), :] = some
                out[:, pl.ds(pl.multiple_of(head * LAT + column * 128, 128), 128)] = highest[0:128, :].astype(bf16)

        whole_loop(8, head_rows)


def rope_factors(position):
    frequency = np.float32(rope_base) ** (-np.arange(32, dtype=np.float32) / np.float32(32))
    angles = position[:, None] * frequency[None, :]
    if isinstance(position, np.ndarray):
        angles = angles.astype(np.float32).astype(np.float64)
        cosine, sine = np.cos(angles), np.sin(angles)
        return np.concatenate([cosine, cosine, -sine, sine], axis=-1).astype(np.float32)
    cosine, sine = jnp.cos(angles), jnp.sin(angles)
    return jnp.concatenate([cosine, cosine, -sine, sine], axis=-1)


def finish_keys(latent, latent_gain, position):
    plain = latent[:, :LAT]
    scaled = plain * lax.rsqrt(jnp.mean(plain * plain, axis=-1, keepdims=True) + norm_eps) * latent_gain
    factors = rope_factors(position.astype(f32))
    rotary = latent[:, LAT:]
    swapped = jnp.concatenate([rotary[:, 32:], rotary[:, :32]], axis=-1)
    turned = rotary * factors[:, :64] + swapped * factors[:, 64:]
    return jnp.concatenate([scaled, turned], axis=-1).astype(bf16)


def dense_keys(every, place, embed_table, down, latent_gain, cache_length):
    group = place[0] * 8 + place[1]
    tp_index = place[2] * 2 + place[3]
    local_row = every.reshape(-1) - (group * 2 + place[4]) * 2048
    inside = (local_row >= 0) & (local_row < 2048)
    picked = jnp.take(embed_table, jnp.clip(local_row, 0, 2047), axis=0)
    picked = jnp.where(inside[:, None], picked, jnp.zeros_like(picked)).reshape(32, 128, 896)
    embedded = jnp.sum(lax.all_to_all(picked, HOLDERS, 0, 0, tiled=True).astype(f32), axis=0).astype(bf16)
    partial = dot_nt(embedded, down)
    spread = jnp.broadcast_to(partial[None], (8, 128, KVW))
    latent = jnp.sum(lax.all_to_all(spread, TP, 0, 0, tiled=True), axis=0)
    index = jnp.arange(128, dtype=jnp.int32)
    mine = finish_keys(latent, latent_gain, group * 64 + index // 2)
    spread = jnp.broadcast_to(mine[None], (32, 128, KVW))
    prompts = lax.all_to_all(spread, HOLDERS, 0, 0, tiled=True).reshape(16, 2, 64, 2, KVW)[:, 0]
    prompts = jnp.transpose(prompts, (2, 0, 1, 3)).reshape(KEYS, KVW)
    own = lax.dynamic_slice_in_dim(latent, tp_index * 16, 16, 0)
    fresh = finish_keys(own, latent_gain, (cache_length[:, None] + jnp.arange(2, dtype=jnp.int32)[None]).reshape(-1))
    return prompts, jnp.concatenate([fresh, jnp.zeros((112, KVW), bf16)], axis=0)


def params(mebibytes):
    return pltpu.CompilerParams(vmem_limit_bytes=mebibytes * 1024 * 1024)


def cache_attention(cache_length, decode_query, latent_cache):
    return pl.pallas_call(
        cache_kernel,
        grid_spec=pltpu.PrefetchScalarGridSpec(
            num_scalar_prefetch=1,
            grid=(8,),
            in_specs=[
                pl.BlockSpec((1, 128, KVW), lambda row, lengths: (row, 0, 0)),
                pl.BlockSpec((1, KVW, 512), lambda row, lengths: (row, 0, 0)),
            ],
            out_specs=[
                pl.BlockSpec((128, LAT), lambda row, lengths: (row, 0)),
                pl.BlockSpec((128, 128), lambda row, lengths: (row, 0)),
            ],
        ),
        out_shape=(jax.ShapeDtypeStruct((1024, LAT), bf16), jax.ShapeDtypeStruct((1024, 128), f32)),
        compiler_params=params(12),
        cost_estimate=pl.CostEstimate(flops=12 * 10**8, bytes_accessed=7 * 10**6, transcendentals=524288),
        name="cache_rows",
    )(cache_length, decode_query.reshape(8, 128, KVW), jnp.swapaxes(latent_cache, 1, 2))


def shards(
    token_ids,
    embed_table,
    latent_down,
    latent_gain,
    prefill_query,
    decode_query,
    latent_cache,
    cache_length,
    prompt_owner,
):
    place = jnp.stack([lax.axis_index(name) for name in ("ylo", "z", "x", "core", "role")]).astype(jnp.int32)
    section = place[4]
    group = place[0] * 8 + place[1]
    down = jnp.transpose(latent_down)
    whole = pl.BlockSpec(memory_space=VMEM)
    scalars = pl.BlockSpec(memory_space=SMEM)
    anywhere = pl.BlockSpec(memory_space=pl.ANY)

    every = lax.all_to_all(jnp.broadcast_to(token_ids, (32, 128)).reshape(32, 1, 128), HOLDERS, 0, 0, tiled=True)
    every = every.reshape(32, 128)
    earlier, level = cache_attention(cache_length, decode_query, latent_cache)
    every, earlier, level = lax.optimization_barrier((every, earlier, level))

    partial = pl.pallas_call(
        select_kernel,
        out_shape=jax.ShapeDtypeStruct((8, SLOTS, KVW), f32),
        in_specs=[scalars, whole, anywhere, anywhere],
        out_specs=whole,
        scratch_shapes=[
            VMEM((16, 4096), bf16),
            VMEM((128, 4096), bf16),
            VMEM((8 * SLOTS, 2048), bf16),
            VMEM((2048, 896), bf16),
            VMEM((KVW, 896), bf16),
            pltpu.SemaphoreType.DMA((2,)),
        ],
        compiler_params=params(16),
        cost_estimate=pl.CostEstimate(flops=3 * 10**9, bytes_accessed=5 * 10**6, transcendentals=0),
        name="select_rows",
    )((group * 2 + section).reshape(1), every, embed_table, down)
    parts = lax.all_to_all(partial, TP, 0, 0, tiled=True)

    columns, kept, fits = pl.pallas_call(
        place_kernel,
        out_shape=(
            jax.ShapeDtypeStruct((128, 128), jnp.int32),
            jax.ShapeDtypeStruct((8, 128), f32),
            jax.ShapeDtypeStruct((1, 1), jnp.int32),
        ),
        in_specs=[scalars, whole],
        out_specs=(whole, whole, scalars),
        scratch_shapes=[
            VMEM((512, 4096), bf16),
            VMEM((128, 4096), bf16),
            VMEM((128, 19 * 128), bf16),
            VMEM((128, 19 * 128), bf16),
            VMEM((96, 128), jnp.int32),
            VMEM((128, 128), f32),
        ],
        compiler_params=params(20),
        cost_estimate=pl.CostEstimate(flops=3 * 10**9, bytes_accessed=10**6, transcendentals=0),
        name="place_rows",
    )(place, every)

    parts, columns, kept, fits = lax.optimization_barrier((parts, columns, kept, fits))
    sent = pl.pallas_call(
        finish_kernel,
        out_shape=jax.ShapeDtypeStruct((8, SLOTS, WIDE), bf16),
        in_specs=[whole, whole],
        out_specs=whole,
        compiler_params=params(8),
        name="finish_rows",
    )(parts, latent_gain.reshape(1, LAT))
    arrived = lax.all_to_all(sent, "z", 0, 0, tiled=True)
    handed = pl.pallas_call(
        keep_kernel,
        out_shape=jax.ShapeDtypeStruct((16, KEPT, WIDE), bf16),
        in_specs=[whole, whole],
        out_specs=whole,
        compiler_params=params(8),
        name="keep_rows",
    )(kept, arrived.reshape(8 * SLOTS, WIDE))
    slots = lax.all_to_all(handed, PLANE, 0, 0, tiled=True).reshape(SIDE, WIDE)
    prompt_query = jnp.transpose(prefill_query.reshape(64, 2, 8, KVW), (1, 2, 0, 3)).reshape(1024, KVW)
    new_position = (cache_length[:, None] + jnp.arange(2, dtype=jnp.int32)[None]).reshape(-1)
    new_factors = jnp.pad(rope_factors(new_position.astype(f32)), ((0, 112), (0, 0)))
    slots, prompt_query, new_factors = lax.optimization_barrier((slots, prompt_query, new_factors))
    others = lax.ppermute(slots, "core", [(0, 1), (1, 0)])

    spare, spare_new = lax.cond(
        fits[0, 0] == 1,
        lambda *unused: (jnp.zeros((KEYS, KVW), bf16), jnp.zeros((128, KVW), bf16)),
        dense_keys,
        every,
        place,
        embed_table,
        down,
        latent_gain,
        cache_length,
    )
    near = pl.pallas_call(
        near_kernel,
        out_shape=jax.ShapeDtypeStruct((KEYS + 128, WIDE), bf16),
        in_specs=[scalars, scalars, whole, whole],
        out_specs=whole,
        scratch_shapes=[VMEM((1024, SIDE), bf16)],
        compiler_params=params(16),
        cost_estimate=pl.CostEstimate(flops=2 * 10**9, bytes_accessed=10**6, transcendentals=0),
        name="near_keys",
    )(place, prompt_owner, slots, columns)
    factors = jnp.asarray(rope_factors(np.arange(1024, dtype=np.float32)))
    decoded = pl.pallas_call(
        decode_kernel,
        out_shape=jax.ShapeDtypeStruct((128, 4096), bf16),
        in_specs=[scalars] * 3 + [whole] * 8 + [anywhere] * 2,
        out_specs=whole,
        scratch_shapes=[
            VMEM((KEYS + 128, KVW), bf16),
            VMEM((1024, SIDE), bf16),
            VMEM((1024, 128), f32),
            VMEM((1024, 128), f32),
            VMEM((1024, LAT), f32),
            VMEM((4, 1024, 128), f32),
            pltpu.SemaphoreType.DMA,
        ],
        compiler_params=params(28),
        cost_estimate=pl.CostEstimate(flops=5 * 10**9, bytes_accessed=7 * 10**6, transcendentals=10**6),
        name="decode_rows",
    )(
        place, prompt_owner, fits, near, others, columns, factors, new_factors, decode_query.reshape(1024, KVW),
        earlier, level, spare, spare_new,
    )
    turned = lax.all_to_all(decoded.reshape(8, 16, 4096), TP, 0, 0, tiled=True).reshape(128, 4096)
    prefilled = pl.pallas_call(
        prefill_kernel,
        out_shape=jax.ShapeDtypeStruct((128, 4096), bf16),
        in_specs=[scalars] * 2 + [whole] * 5 + [anywhere],
        out_specs=whole,
        scratch_shapes=[
            VMEM((1024, KVW), bf16),
            VMEM((1024, SIDE), bf16),
            VMEM((1024, 128), f32),
            VMEM((1024, 128), f32),
            VMEM((1024, LAT), f32),
            VMEM((1024, WIDE), f32),
            pltpu.SemaphoreType.DMA,
        ],
        compiler_params=params(28),
        cost_estimate=pl.CostEstimate(flops=7 * 10**9, bytes_accessed=7 * 10**6, transcendentals=10**6),
        name="prefill_rows",
    )(place, fits, slots, others, columns, factors, prompt_query, spare)
    return jnp.where(section == 0, prefilled, turned)[None]


def solution(mesh):
    fine_mesh = Mesh(mesh.devices.reshape(2, 8, 4, 2, 2), ("ylo", "z", "x", "core", "role"))
    ctx, tp = ("ylo", "z"), ("x", "core")
    in_specs = (
        P("role", ctx),
        P(ctx + ("role",), tp),
        P(tp, None),
        P(),
        P(ctx, tp, None),
        P(ctx + tp, None, None, None),
        P(ctx + tp, None, None),
        P(ctx + tp),
        P(),
    )
    out_specs = P("role", ctx, tp)
    return jax.shard_map(shards, mesh=fine_mesh, in_specs=in_specs, out_specs=out_specs, check_vma=False)
```

```python
import jax
import jax.numpy as jnp
import numpy as np
from jax import lax
from jax.experimental import pallas as pl
from jax.experimental.pallas import tpu as pltpu
from jax.sharding import Mesh
from jax.sharding import PartitionSpec as P

LAT = 512
KVW = 576
STEPS = 2
WIDE = 640
SLOTS = 16
KEPT = 48
SIDE = 16 * KEPT
KEYS = 2048

score_scale = 0.07216878364870322
base_two = score_scale * 1.4426950408889634
masked_fill = -1e30
norm_eps = 1e-06
rope_base = 10000.0
bf16 = jnp.bfloat16
f32 = jnp.float32
SMEM = pltpu.SMEM
VMEM = pltpu.VMEM

HOLDERS = ("ylo", "z", "role")
PLANE = ("ylo", "role", "x")
TP = ("x", "core")


def iota(shape, axis):
    return lax.broadcasted_iota(jnp.int32, shape, axis)


def ones_where(flags):
    return jnp.where(flags, 1.0, 0.0).astype(bf16)


def dot(left, right):
    return lax.dot_general(left, right, (((1,), (0,)), ((), ())), preferred_element_type=f32)


def dot_nt(left, right):
    return lax.dot_general(left, right, (((1,), (1,)), ((), ())), preferred_element_type=f32)


def whole_loop(count, body, unroll=1):
    def step(index, carry):
        body(index)
        return carry

    lax.fori_loop(0, count, step, 0, unroll=unroll)


def aligned(index, size):
    return pl.ds(pl.multiple_of(index * size, size), size)


def select_kernel(place, ids, table, down, partial, hots, lows, chosen, table_here, down_here, sems):
    holder = (place[0] * 8 + place[1]) * 2 + place[4]
    table_copy = pltpu.make_async_copy(table, table_here, sems.at[0])
    down_copy = pltpu.make_async_copy(down, down_here, sems.at[1])
    table_copy.start()
    down_copy.start()
    for line in range(32):
        tokens = ids[line : line + 1, :]
        start = ((line & 1) * 16 + (line >> 1)) * 128
        span = slice(start, start + 128)
        hots[:, span] = ones_where(iota((16, 128), 0) == (tokens >> 7) - holder * 16)
        lows[:, span] = ones_where(iota((128, 128), 0) == (tokens & 127))
    in_prompt = dot_nt(hots[:, :KEYS], lows[:, :KEYS]) > 0.5
    alone = (dot_nt(hots[:, KEYS:], lows[:, KEYS:]) > 0.5) & jnp.logical_not(in_prompt)
    upper = ones_where(iota((128, 128), 0) < iota((128, 128), 1))
    all_ones = jnp.ones((128, 128), bf16)
    row = iota((8 * SLOTS, 128), 0)
    wanted = ((row & 15) * 8 + (((row >> 4) - holder) & 7)).astype(f32)
    before = jnp.zeros((1, 128), f32)
    ranks = []
    for present in (in_prompt, alone):
        flags = ones_where(present)
        within = dot(flags, upper)
        totals = dot(flags, all_ones)
        lines = []
        for step in range(16):
            lines.append(within[step : step + 1, :] + before)
            before = before + totals[step : step + 1, :]
        ranks.append(lines)
    for step in range(16):
        rank = jnp.where(alone[step : step + 1, :], ranks[1][step], -1.0)
        rank = jnp.where(in_prompt[step : step + 1, :], ranks[0][step], rank)
        chosen[:, step * 128 : (step + 1) * 128] = ones_where(wanted == rank)
    table_copy.wait()
    rows = dot(chosen[...], table_here[...]).astype(bf16)
    down_copy.wait()
    partial[...] = dot_nt(rows, down_here[...]).reshape(partial.shape)


def rank_kernel(ids, sheet, highs, lows):
    square = (128, 128)
    lane = iota((8, 128), 1)
    sheet[0:16, :] = ids[pl.ds(0, 16, stride=2), :]
    sheet[16:32, :] = ids[pl.ds(1, 16, stride=2), :]
    target = iota(square, 1)
    mover = ones_where(iota(square, 0) == jnp.where(target < 64, 2 * target, 2 * target - 127))
    plain = sheet[0:16, :]
    decode_tokens = sheet[16:32, :]
    coarse = (plain >> 8).astype(f32).astype(bf16)
    fine = (plain & 255).astype(f32).astype(bf16)
    moved = dot(coarse, mover) * 256.0 + dot(fine, mover)
    sheet[0:16, :] = moved.astype(jnp.int32)
    even = sheet[pl.ds(0, 8, stride=2), :]
    odd = sheet[pl.ds(1, 8, stride=2), :]
    first = jnp.where(lane < 64, even, pltpu.roll(odd, 64, 1))
    second = jnp.where(lane < 64, pltpu.roll(even, 64, 1), odd)
    tokens = jnp.concatenate([first, second, decode_tokens], axis=0)
    sheet[0:32, :] = tokens

    def mark(block):
        line = sheet[pl.ds(block, 1), :]
        span = aligned(block, 128)
        highs[:, span] = ones_where(iota((512, 128), 0) == (line >> 7))
        lows[:, span] = ones_where(iota(square, 0) == (line & 127))

    whole_loop(32, mark, 8)
    in_prompt = dot_nt(lows[:, :KEYS], highs[:, :KEYS]) > 0.5
    alone = (dot_nt(lows[:, KEYS:], highs[:, KEYS:]) > 0.5) & jnp.logical_not(in_prompt)
    below = ones_where(iota(square, 1) < iota(square, 0))
    all_ones = jnp.ones(square, bf16)
    wide = (512, 512)
    same = (iota(wide, 0) >> 4) == (iota(wide, 1) >> 4)
    in_holder = ones_where(same & (iota(wide, 0) < iota(wide, 1)))
    prompt_flags = ones_where(in_prompt)
    alone_flags = ones_where(alone)
    prompt_columns = dot(all_ones, prompt_flags).astype(bf16)
    alone_columns = dot(all_ones, alone_flags).astype(bf16)
    prompt_rank = dot(below, prompt_flags) + dot(prompt_columns, in_holder)
    alone_rank = (
        dot(below, alone_flags) + dot(alone_columns, in_holder) + dot(prompt_columns, ones_where(same))
    )
    rank = jnp.where(in_prompt, prompt_rank, jnp.where(alone, alone_rank, 0.0))
    top_rank = jnp.max(jnp.max(rank, axis=0, keepdims=True), axis=1, keepdims=True).astype(jnp.int32)
    coded = (jnp.minimum(rank, 127.0) + jnp.where(in_prompt, 128.0, 0.0)).astype(bf16)
    pieces = []
    for chunk in range(4):
        span = slice(chunk * 1024, (chunk + 1) * 1024)
        looked = dot(coded, highs[:, span]) * lows[:, span].astype(f32)
        line = jnp.sum(looked, axis=0, keepdims=True)
        for part in range(8):
            pieces.append(line[:, part * 128 : (part + 1) * 128])
    value = jnp.concatenate(pieces, axis=0).astype(jnp.int32)
    ranks = value & 127
    holder = tokens >> 11
    tp_of = (ranks + holder) & 7
    quad = tp_of * 16 + (ranks >> 3)
    sheet[0:32, :] = quad
    sheet[32:64, :] = holder
    sheet[64:96, :] = jnp.where(value >= 128, -1, tp_of)
    sheet[96:104, :] = jnp.broadcast_to(top_rank, (8, 128))


def place_kernel(place, sheet, columns, kept, fits, quads, holders, hot_tp, hot_pool, sheet_b):
    ylo, zed, ex, core, section = place[0], place[1], place[2], place[3], place[4]
    square = (128, 128)

    def spot(block, source):
        span = aligned(block, 128)
        quads[:, span] = ones_where(iota(square, 0) == sheet[pl.ds(source, 1), :])
        holders[:, span] = ones_where(iota(square, 0) == sheet[pl.ds(source + 32, 1), :])

    whole_loop(16, lambda block: spot(block, block), 8)
    for part in range(2):
        spot(16 + part, 16 + part * 8 + zed)
    spot(18, 16 + ylo * 8 + zed)
    counted = dot_nt(quads[:, :KEYS], holders[:, :KEYS])
    newest = dot_nt(quads[:, KEYS : KEYS + 256], holders[:, KEYS : KEYS + 256])
    held = (counted + newest) > 0.5
    held_flags = ones_where(held)
    up, down = iota(square, 0), iota(square, 1)
    same_tp = (up >> 4) == (down >> 4)
    same_pool = ((up >> 4) == (down >> 4)) & ((up & 1) == (down & 1))
    before = ones_where(same_pool & (up < down))
    in_tp = ones_where(same_tp & (down < up))
    position = dot(in_tp, held_flags) + dot(dot(ones_where(same_tp), held_flags).astype(bf16), before)
    position = jnp.where(held, jnp.minimum(position, 255.0), 255.0)
    def pick(block):
        span = aligned(block, 128)
        hot_tp[:, span] = ones_where(iota((16, 128), 0) == sheet[pl.ds(block + 80, 1), :])
        line = sheet[pl.ds(block + 48, 1), :] + 32 * (block & 7)
        hot_pool[:, span] = ones_where(iota((256, 128), 0) == line)

    whole_loop(16, pick, 8)
    added = dot_nt(hot_tp[...], hot_pool[...]).astype(bf16)
    gather_tp = ones_where(iota((16, 128), 0) == (iota((16, 128), 1) >> 4))
    base = dot(gather_tp, ones_where(counted > 0.5)).astype(bf16)

    def same_pools(shape):
        left, right = iota(shape, 0), iota(shape, 1)
        pools = (((left & 31) >> 4) == ((right & 31) >> 4)) & ((left & 1) == (right & 1))
        return ones_where(pools & ((left < 32) if shape[0] == 128 else ((left >> 5) == (right >> 5))))

    needed = dot(added, same_pools((256, 256))) + dot(base, same_pools((128, 256)))
    needed = jnp.max(jnp.max(needed, axis=0, keepdims=True), axis=1, keepdims=True)
    enough = (sheet[96:97, 0:1] < 8 * SLOTS) & (needed <= float(KEPT))
    fits[0, 0] = jnp.max(jnp.where(enough, 1, 0))
    position_b = position.astype(bf16)
    looked = dot(position_b, holders[...]) * quads[...].astype(f32)
    line = jnp.sum(looked, axis=0, keepdims=True)
    found = [line[:, block * 128 : (block + 1) * 128] for block in range(19)]
    found = jnp.concatenate(found + [jnp.zeros((5, 128), f32)], axis=0)
    own = 16 + ylo * 8 + zed
    quad_rows = jnp.concatenate(
        [sheet[0:16, :], jnp.zeros((2, 128), jnp.int32), sheet[pl.ds(own, 1), :], jnp.zeros((5, 128), jnp.int32)], axis=0
    )
    holder_rows = jnp.concatenate(
        [sheet[32:48, :], jnp.zeros((2, 128), jnp.int32), sheet[pl.ds(own + 32, 1), :], jnp.zeros((5, 128), jnp.int32)],
        axis=0,
    )
    tp_rows = quad_rows >> 4
    source = ((holder_rows >> 4) * 2 + (holder_rows & 1)) * 4 + (tp_rows >> 1)
    side = jnp.where((tp_rows & 1) == core, 0, SIDE)
    final = found + (source * KEPT + side).astype(f32)
    tp_index = ex * 2 + core
    turned = pltpu.roll(final, (128 - tp_index * 16) % 128, 1)
    turned = jnp.where(iota((24, 128), 1) < 16, turned, -1.0)
    final = jnp.where(iota((24, 128), 0) == 18, turned, final)
    final = jnp.concatenate([final, jnp.zeros((104, 128), f32)], axis=0)
    columns[...] = jnp.transpose(final).astype(jnp.int32)
    sheet_b[...] = position
    mine = sheet_b[pl.ds(pl.multiple_of(tp_index * 16, 16), 16), :].astype(bf16)
    spread = dot(mine, ones_where(up == (ylo * 8 + (down >> 4)) * 2 + section))
    few = (16, 128)
    spread = jnp.where((iota(few, 1) & 15) == iota(few, 0), spread, 0.0)
    kept[...] = jnp.broadcast_to(jnp.sum(spread, axis=0, keepdims=True), kept.shape)


def finish_kernel(parts, gain, sent):
    latent = parts[0]
    for tp in range(1, parts.shape[0]):
        latent = latent + parts[tp]
    plain = latent[:, :LAT]
    scaled = plain * lax.rsqrt(jnp.mean(plain * plain, axis=-1, keepdims=True) + norm_eps) * gain[...]
    rotary = latent[:, LAT:]
    coarse = rotary.astype(bf16)
    fine = (rotary - coarse.astype(f32)).astype(bf16)
    row = jnp.concatenate([scaled.astype(bf16), coarse, fine], axis=-1)
    for peer in range(sent.shape[0]):
        sent[peer] = row


def keep_kernel(kept, rows, sent):
    chosen = iota((KEPT, 128), 0).astype(f32) == kept[0:1, :]
    row = dot(ones_where(chosen), rows[...]).astype(bf16)
    for peer in range(sent.shape[0]):
        sent[peer] = row


def cache_kernel(lengths, query, cache, out, level):
    length = lengths[pl.program_id(0)]
    scores = dot(query[0], cache[0]) * base_two
    scores = jnp.where(iota(scores.shape, 1) < length, scores, masked_fill)
    highest = jnp.max(scores, axis=-1, keepdims=True)
    weights = jnp.exp2(scores - highest)
    total = jnp.sum(weights, axis=-1, keepdims=True)
    out[...] = (dot_nt(weights.astype(bf16), cache[0, :LAT, :]) * (1.0 / total)).astype(bf16)
    level[...] = jnp.broadcast_to(highest + jnp.log2(total), level.shape)


def hot_rows(hot, columns, prompt, side):
    for block in range(8):
        wanted = jnp.sum(jnp.where(iota((128, 128), 1) == prompt * 8 + block, columns[...], 0), axis=1, keepdims=True)
        hot[block * 128 : (block + 1) * 128, :] = ones_where(iota((128, SIDE), 1) == wanted - side * SIDE)


def fresh_hot(columns, side):
    return ones_where(iota((128, SIDE), 1) == columns[:, 18:19] - side * SIDE)


def put_keys(keys, span, found, factor):
    turning = found[:, LAT:]
    turning = turning + pltpu.roll(turning, 64, 1)
    turned = turning * factor + pltpu.roll(turning, 32, 1) * pltpu.roll(factor, 64, 1)
    keys[span, :LAT] = found[:, :LAT].astype(bf16)
    keys[span, LAT:] = turned[:, : KVW - LAT].astype(bf16)


def copy_in(source, target, sem):
    copy = pltpu.make_async_copy(source, target, sem)
    copy.start()
    copy.wait()


def weigh(scores, old):
    new = jnp.maximum(old, jnp.max(scores, axis=-1, keepdims=True))
    weights = jnp.exp2(scores - new)
    return new, jnp.exp2(old - new), jnp.sum(weights, axis=-1, keepdims=True), weights.astype(bf16)


def near_kernel(place, owner, slots, columns, near, hot):
    group = place[0] * 8 + place[1]

    @pl.when(place[4] == 1)
    def _():
        near[KEYS : KEYS + 128, :] = dot(fresh_hot(columns, 0), slots[...]).astype(bf16)

        def open_prompt(prompt):
            @pl.when(owner[prompt] == group)
            def _():
                hot_rows(hot, columns, prompt, 0)

                def open_part(part):
                    near[aligned(prompt * 2 + part, 512), :] = dot(hot[aligned(part, 512), :], slots[...]).astype(bf16)

                whole_loop(2, open_part)

        whole_loop(2, open_prompt)


def decode_kernel(
    place, owner, fits, near, others, columns, factors, new_factors, query, earlier, level, spare, spare_new,
    out, keys, hot, highest, total, mixed, sem
):
    group = place[0] * 8 + place[1]
    fitting = fits[0, 0] == 1

    @pl.when(place[4] == 1)
    def _():
        @pl.when(fitting)
        def _():
            span = slice(KEYS, KEYS + 128)
            found = near[span, :].astype(f32) + dot(fresh_hot(columns, 1), others[...])
            put_keys(keys, span, found, new_factors[...])

        @pl.when(jnp.logical_not(fitting))
        def _():
            copy_in(spare_new, keys.at[pl.ds(KEYS, 128)], sem)

        newest = keys[KEYS : KEYS + 128, :]

        def begin(piece):
            span = aligned(piece, 512)
            scores = dot_nt(query[span, :], newest) * base_two
            key = iota(scores.shape, 1)
            row = iota(scores.shape, 0) & 15
            allowed = ((key >> 1) == (row >> 1)) & ((key & 1) <= (row & 1))
            scores = jnp.where(allowed, scores, masked_fill)
            new, factor, summed, weights = weigh(scores, level[span, 0:1])
            mixed[span, :] = earlier[span, :].astype(f32) * factor + dot(weights, newest[:, :LAT])
            highest[span, :] = jnp.broadcast_to(new, (512, 128))
            total[span, :] = jnp.broadcast_to(factor + summed, (512, 128))

        whole_loop(2, begin)

        def add_prompt(prompt):
            @pl.when(owner[prompt] == group)
            def _():
                @pl.when(fitting)
                def _():
                    hot_rows(hot, columns, prompt, 1)

                    def open_part(part):
                        span = aligned(prompt * 2 + part, 512)
                        found = near[span, :].astype(f32) + dot(hot[aligned(part, 512), :], others[...])
                        put_keys(keys, span, found, factors[aligned(part, 512), :])

                    whole_loop(2, open_part)

                @pl.when(jnp.logical_not(fitting))
                def _():
                    copy_in(spare.at[pl.ds(prompt * 1024, 1024)], keys.at[pl.ds(prompt * 1024, 1024)], sem)

                def add_part(piece):
                    span = aligned(piece, 512)
                    some = keys[aligned(prompt, 1024), :]
                    new, factor, summed, weights = weigh(dot_nt(query[span, :], some) * base_two, highest[span, 0:1])
                    mixed[span, :] = mixed[span, :] * factor + dot(weights, some[:, :LAT])
                    highest[span, :] = jnp.broadcast_to(new, (512, 128))
                    total[span, :] = total[span, :] * factor + summed

                whole_loop(2, add_part)

        whole_loop(2, add_prompt)

        def tp_rows(tp):
            for head in range(8):
                rows = pl.ds(pl.multiple_of(tp * 128 + head * 16, 16), 16)
                some = mixed[rows, :] * (1.0 / total[rows, 0:1])
                out[aligned(tp, 16), head * LAT : (head + 1) * LAT] = some.astype(bf16)

        whole_loop(8, tp_rows)


def prefill_kernel(place, fits, slots, others, columns, factors, query, spare, out, keys, hot, mixed, lines, pairs, sem):
    group = place[0] * 8 + place[1]
    fitting = fits[0, 0] == 1

    @pl.when(place[4] == 0)
    def _():
        def add_prompt(prompt):
            @pl.when(fitting)
            def _():
                for side in range(2):
                    hot_rows(hot, columns, prompt, side)

                    def open_part(part, side=side):
                        span = aligned(part, 512)
                        if side == 0:
                            lines[span, :] = dot(hot[span, :], slots[...])
                        else:
                            found = lines[span, :] + dot(hot[span, :], others[...])
                            put_keys(keys, span, found, factors[span, :])

                    whole_loop(2, open_part)

            @pl.when(jnp.logical_not(fitting))
            def _():
                copy_in(spare.at[pl.ds(prompt * 1024, 1024)], keys, sem)

            span = aligned(prompt, 512)
            some = keys[...]
            scores = dot_nt(query[span, :], some) * base_two
            last = (iota((512, 1), 0) & 63) + group * 64
            scores = jnp.where(iota(scores.shape, 1) <= last, scores, masked_fill)
            _, _, summed, weights = weigh(scores, jnp.full((512, 1), masked_fill, f32))
            added = dot(weights, some[:, :LAT]) * (1.0 / summed)
            for column in range(4):
                mixed[column, span, :] = added[:, column * 128 : (column + 1) * 128]

        whole_loop(2, add_prompt)

        def head_rows(head):
            for column in range(4):
                for prompt in range(2):
                    start = pl.multiple_of(prompt * 512 + head * 64, 64)
                    pairs[column, pl.ds(prompt, 64, stride=2), :] = mixed[column, pl.ds(start, 64), :]
                out[:, pl.ds(pl.multiple_of(head * LAT + column * 128, 128), 128)] = pairs[column].astype(bf16)

        whole_loop(8, head_rows)


def join_kernel(place, turned, prefilled, out, sems):
    def bring(source):
        copies = []
        for part in range(4):
            span = pl.ds(part * 32, 32)
            copies.append(pltpu.make_async_copy(source.at[span], out.at[span], sems.at[part]))
        for copy in copies:
            copy.start()
        for copy in copies:
            copy.wait()

    @pl.when(place[4] == 0)
    def _():
        bring(prefilled)

    @pl.when(place[4] == 1)
    def _():
        bring(turned)


def rope_factors(position):
    frequency = np.float32(rope_base) ** (-np.arange(32, dtype=np.float32) / np.float32(32))
    angles = position[:, None] * frequency[None, :]
    if isinstance(position, np.ndarray):
        angles = angles.astype(np.float32).astype(np.float64)
        cosine, sine = np.cos(angles), np.sin(angles)
        return np.concatenate([cosine, cosine, -sine, sine], axis=-1).astype(np.float32)
    cosine, sine = jnp.cos(angles), jnp.sin(angles)
    return jnp.concatenate([cosine, cosine, -sine, sine], axis=-1)


def finish_keys(latent, latent_gain, position):
    plain = latent[:, :LAT]
    scaled = plain * lax.rsqrt(jnp.mean(plain * plain, axis=-1, keepdims=True) + norm_eps) * latent_gain
    factors = rope_factors(position.astype(f32))
    rotary = latent[:, LAT:]
    swapped = jnp.concatenate([rotary[:, 32:], rotary[:, :32]], axis=-1)
    turned = rotary * factors[:, :64] + swapped * factors[:, 64:]
    return jnp.concatenate([scaled, turned], axis=-1).astype(bf16)


def dense_keys(token_ids, place, embed_table, down, latent_gain, cache_length):
    group = place[0] * 8 + place[1]
    tp_index = place[2] * 2 + place[3]
    every = lax.all_to_all(jnp.broadcast_to(token_ids, (32, 128)).reshape(32, 1, 128), HOLDERS, 0, 0, tiled=True)
    local_row = every.reshape(-1) - (group * 2 + place[4]) * 2048
    inside = (local_row >= 0) & (local_row < 2048)
    picked = jnp.take(embed_table, jnp.clip(local_row, 0, 2047), axis=0)
    picked = jnp.where(inside[:, None], picked, jnp.zeros_like(picked)).reshape(32, 128, 896)
    embedded = jnp.sum(lax.all_to_all(picked, HOLDERS, 0, 0, tiled=True).astype(f32), axis=0).astype(bf16)
    partial = dot_nt(embedded, down)
    spread = jnp.broadcast_to(partial[None], (8, 128, KVW))
    latent = jnp.sum(lax.all_to_all(spread, TP, 0, 0, tiled=True), axis=0)
    index = jnp.arange(128, dtype=jnp.int32)
    mine = finish_keys(latent, latent_gain, group * 64 + index // 2)
    spread = jnp.broadcast_to(mine[None], (32, 128, KVW))
    prompts = lax.all_to_all(spread, HOLDERS, 0, 0, tiled=True).reshape(16, 2, 64, 2, KVW)[:, 0]
    prompts = jnp.transpose(prompts, (2, 0, 1, 3)).reshape(KEYS, KVW)
    own = lax.dynamic_slice_in_dim(latent, tp_index * 16, 16, 0)
    fresh = finish_keys(own, latent_gain, (cache_length[:, None] + jnp.arange(2, dtype=jnp.int32)[None]).reshape(-1))
    return prompts, jnp.concatenate([fresh, jnp.zeros((112, KVW), bf16)], axis=0)


def params(mebibytes):
    return pltpu.CompilerParams(vmem_limit_bytes=mebibytes * 1024 * 1024)


def shards(
    token_ids,
    embed_table,
    latent_down,
    latent_gain,
    prefill_query,
    decode_query,
    latent_cache,
    cache_length,
    prompt_owner,
):
    place = jnp.stack([lax.axis_index(name) for name in ("ylo", "z", "x", "core", "role")]).astype(jnp.int32)
    down = jnp.transpose(latent_down)
    whole = pl.BlockSpec(memory_space=VMEM)
    scalars = pl.BlockSpec(memory_space=SMEM)
    anywhere = pl.BlockSpec(memory_space=pl.ANY)
    shaped = jax.ShapeDtypeStruct

    every = lax.all_to_all(jnp.broadcast_to(token_ids, (32, 128)).reshape(32, 1, 128), HOLDERS, 0, 0, tiled=True)
    every = every.reshape(32, 128)

    earlier, level = pl.pallas_call(
        cache_kernel,
        grid_spec=pltpu.PrefetchScalarGridSpec(
            num_scalar_prefetch=1,
            grid=(8,),
            in_specs=[
                pl.BlockSpec((1, 128, KVW), lambda row, lengths: (row, 0, 0)),
                pl.BlockSpec((1, KVW, 512), lambda row, lengths: (row, 0, 0)),
            ],
            out_specs=[
                pl.BlockSpec((128, LAT), lambda row, lengths: (row, 0)),
                pl.BlockSpec((128, 128), lambda row, lengths: (row, 0)),
            ],
        ),
        out_shape=(shaped((1024, LAT), bf16), shaped((1024, 128), f32)),
        compiler_params=params(56),
        cost_estimate=pl.CostEstimate(flops=12 * 10**8, bytes_accessed=7 * 10**6, transcendentals=524288),
        name="cache_rows",
    )(cache_length, decode_query.reshape(8, 128, KVW), jnp.swapaxes(latent_cache, 1, 2))
    every, earlier, level = lax.optimization_barrier((every, earlier, level))

    partial = pl.pallas_call(
        select_kernel,
        out_shape=shaped((8, SLOTS, KVW), f32),
        in_specs=[scalars, whole, anywhere, anywhere],
        out_specs=whole,
        scratch_shapes=[
            VMEM((16, 4096), bf16),
            VMEM((128, 4096), bf16),
            VMEM((8 * SLOTS, 2048), bf16),
            VMEM((2048, 896), bf16),
            VMEM((KVW, 896), bf16),
            pltpu.SemaphoreType.DMA((2,)),
        ],
        compiler_params=params(16),
        cost_estimate=pl.CostEstimate(flops=3 * 10**9, bytes_accessed=5 * 10**6, transcendentals=0),
        name="select_rows",
    )(place, every, embed_table, down)
    parts = lax.all_to_all(partial, TP, 0, 0, tiled=True)

    sheet = pl.pallas_call(
        rank_kernel,
        out_shape=shaped((104, 128), jnp.int32),
        in_specs=[whole],
        out_specs=whole,
        scratch_shapes=[VMEM((512, 4096), bf16), VMEM((128, 4096), bf16)],
        compiler_params=params(18),
        cost_estimate=pl.CostEstimate(flops=2 * 10**9, bytes_accessed=10**6, transcendentals=0),
        name="rank_rows",
    )(every)
    parts, sheet = lax.optimization_barrier((parts, sheet))
    sent = pl.pallas_call(
        finish_kernel,
        out_shape=shaped((8, SLOTS, WIDE), bf16),
        in_specs=[whole, whole],
        out_specs=whole,
        compiler_params=params(8),
        name="finish_rows",
    )(parts, latent_gain.reshape(1, LAT))
    arrived = lax.all_to_all(sent, "z", 0, 0, tiled=True)

    columns, kept, fits = pl.pallas_call(
        place_kernel,
        out_shape=(shaped((128, 128), jnp.int32), shaped((8, 128), f32), shaped((1, 1), jnp.int32)),
        in_specs=[scalars, whole],
        out_specs=(whole, whole, scalars),
        scratch_shapes=[
            VMEM((128, 19 * 128), bf16),
            VMEM((128, 19 * 128), bf16),
            VMEM((16, 2048), bf16),
            VMEM((256, 2048), bf16),
            VMEM((128, 128), f32),
        ],
        compiler_params=params(12),
        cost_estimate=pl.CostEstimate(flops=10**9, bytes_accessed=10**6, transcendentals=0),
        name="place_rows",
    )(place, sheet)
    prompt_query = jnp.transpose(prefill_query.reshape(64, 2, 8, KVW), (1, 2, 0, 3)).reshape(1024, KVW)
    arrived, prompt_query = lax.optimization_barrier((arrived, prompt_query))
    handed = pl.pallas_call(
        keep_kernel,
        out_shape=shaped((16, KEPT, WIDE), bf16),
        in_specs=[whole, whole],
        out_specs=whole,
        compiler_params=params(8),
        name="keep_rows",
    )(kept, arrived.reshape(8 * SLOTS, WIDE))
    slots = lax.all_to_all(handed, PLANE, 0, 0, tiled=True).reshape(SIDE, WIDE)

    def by_head(rows):
        return jnp.transpose(rows.reshape(16, 64, -1), (1, 0, 2)).reshape(1024, -1)

    row_query, earlier, level = by_head(decode_query), by_head(earlier), by_head(level)
    new_position = (cache_length[:, None] + jnp.arange(2, dtype=jnp.int32)[None]).reshape(-1)
    new_factors = jnp.pad(rope_factors(new_position.astype(f32)), ((0, 112), (0, 0)))
    slots, new_factors, row_query, earlier, level = lax.optimization_barrier(
        (slots, new_factors, row_query, earlier, level)
    )
    others = lax.ppermute(slots, "core", [(0, 1), (1, 0)])

    spare, spare_new = lax.cond(
        fits[0, 0] == 1,
        lambda *unused: (jnp.zeros((KEYS, KVW), bf16), jnp.zeros((128, KVW), bf16)),
        dense_keys,
        token_ids,
        place,
        embed_table,
        down,
        latent_gain,
        cache_length,
    )
    near = pl.pallas_call(
        near_kernel,
        out_shape=shaped((KEYS + 128, WIDE), bf16),
        in_specs=[scalars, scalars, whole, whole],
        out_specs=whole,
        scratch_shapes=[VMEM((1024, SIDE), bf16)],
        compiler_params=params(12),
        cost_estimate=pl.CostEstimate(flops=2 * 10**9, bytes_accessed=10**6, transcendentals=0),
        name="near_keys",
    )(place, prompt_owner, slots, columns)
    factors = jnp.asarray(rope_factors(np.arange(1024, dtype=np.float32)))
    decoded = pl.pallas_call(
        decode_kernel,
        out_shape=shaped((128, 4096), bf16),
        in_specs=[scalars] * 3 + [whole] * 8 + [anywhere] * 2,
        out_specs=whole,
        scratch_shapes=[
            VMEM((KEYS + 128, KVW), bf16),
            VMEM((1024, SIDE), bf16),
            VMEM((1024, 128), f32),
            VMEM((1024, 128), f32),
            VMEM((1024, LAT), f32),
            pltpu.SemaphoreType.DMA,
        ],
        compiler_params=params(20),
        cost_estimate=pl.CostEstimate(flops=5 * 10**9, bytes_accessed=7 * 10**6, transcendentals=10**6),
        name="decode_rows",
    )(
        place, prompt_owner, fits, near, others, columns, factors, new_factors, row_query, earlier, level, spare, spare_new
    )
    turned = lax.all_to_all(decoded.reshape(8, 16, 4096), TP, 0, 0, tiled=True).reshape(128, 4096)
    prefilled = pl.pallas_call(
        prefill_kernel,
        out_shape=shaped((128, 4096), bf16),
        in_specs=[scalars] * 2 + [whole] * 5 + [anywhere],
        out_specs=whole,
        scratch_shapes=[
            VMEM((1024, KVW), bf16),
            VMEM((1024, SIDE), bf16),
            VMEM((4, 1024, 128), f32),
            VMEM((1024, WIDE), f32),
            VMEM((4, 128, 128), f32),
            pltpu.SemaphoreType.DMA,
        ],
        compiler_params=params(20),
        cost_estimate=pl.CostEstimate(flops=7 * 10**9, bytes_accessed=7 * 10**6, transcendentals=10**6),
        name="prefill_rows",
    )(place, fits, slots, others, columns, factors, prompt_query, spare)
    out = pl.pallas_call(
        join_kernel,
        out_shape=shaped((128, 4096), bf16),
        in_specs=[scalars] + [anywhere] * 2,
        out_specs=anywhere,
        scratch_shapes=[pltpu.SemaphoreType.DMA((4,))],
        compiler_params=params(4),
        name="join_rows",
    )(place, turned, prefilled)
    return out[None]


def solution(mesh):
    fine_mesh = Mesh(mesh.devices.reshape(2, 8, 4, 2, 2), ("ylo", "z", "x", "core", "role"))
    ctx, tp = ("ylo", "z"), ("x", "core")
    in_specs = (
        P("role", ctx),
        P(ctx + ("role",), tp),
        P(tp, None),
        P(),
        P(ctx, tp, None),
        P(ctx + tp, None, None, None),
        P(ctx + tp, None, None),
        P(ctx + tp),
        P(),
    )
    out_specs = P("role", ctx, tp)
    return jax.shard_map(shards, mesh=fine_mesh, in_specs=in_specs, out_specs=out_specs, check_vma=False)
```

```python
import jax
import jax.numpy as jnp
import numpy as np
from jax import lax
from jax.experimental import pallas as pl
from jax.experimental.pallas import tpu as pltpu
from jax.sharding import Mesh
from jax.sharding import PartitionSpec as P

LAT = 512
KVW = 576
STEPS = 2
WIDE = 640
SLOTS = 16
KEPT = 48
SIDE = 16 * KEPT
KEYS = 2048

score_scale = 0.07216878364870322
base_two = score_scale * 1.4426950408889634
masked_fill = -1e30
norm_eps = 1e-06
rope_base = 10000.0
bf16 = jnp.bfloat16
f32 = jnp.float32
SMEM = pltpu.SMEM
VMEM = pltpu.VMEM

HOLDERS = ("ylo", "z", "role")
PLANE = ("ylo", "role", "x")
TP = ("x", "core")


def iota(shape, axis):
    return lax.broadcasted_iota(jnp.int32, shape, axis)


def ones_where(flags):
    return jnp.where(flags, 1.0, 0.0).astype(bf16)


def dot(left, right):
    return lax.dot_general(left, right, (((1,), (0,)), ((), ())), preferred_element_type=f32)


def dot_nt(left, right):
    return lax.dot_general(left, right, (((1,), (1,)), ((), ())), preferred_element_type=f32)


def whole_loop(count, body, unroll=1):
    def step(index, carry):
        body(index)
        return carry

    lax.fori_loop(0, count, step, 0, unroll=unroll)


def aligned(index, size):
    return pl.ds(pl.multiple_of(index * size, size), size)


def select_kernel(place, ids, table, down, partial, hots, lows, chosen, table_here, down_here, sems):
    holder = (place[0] * 8 + place[1]) * 2 + place[4]
    table_copy = pltpu.make_async_copy(table, table_here, sems.at[0])
    down_copy = pltpu.make_async_copy(down, down_here, sems.at[1])
    table_copy.start()
    down_copy.start()
    for line in range(32):
        tokens = ids[line : line + 1, :]
        start = ((line & 1) * 16 + (line >> 1)) * 128
        span = slice(start, start + 128)
        hots[:, span] = ones_where(iota((16, 128), 0) == (tokens >> 7) - holder * 16)
        lows[:, span] = ones_where(iota((128, 128), 0) == (tokens & 127))
    in_prompt = dot_nt(hots[:, :KEYS], lows[:, :KEYS]) > 0.5
    alone = (dot_nt(hots[:, KEYS:], lows[:, KEYS:]) > 0.5) & jnp.logical_not(in_prompt)
    upper = ones_where(iota((128, 128), 0) < iota((128, 128), 1))
    all_ones = jnp.ones((128, 128), bf16)
    row = iota((8 * SLOTS, 128), 0)
    wanted = ((row & 15) * 8 + (((row >> 4) - holder) & 7)).astype(f32)
    before = jnp.zeros((1, 128), f32)
    ranks = []
    for present in (in_prompt, alone):
        flags = ones_where(present)
        within = dot(flags, upper)
        totals = dot(flags, all_ones)
        lines = []
        for step in range(16):
            lines.append(within[step : step + 1, :] + before)
            before = before + totals[step : step + 1, :]
        ranks.append(lines)
    for step in range(16):
        rank = jnp.where(alone[step : step + 1, :], ranks[1][step], -1.0)
        rank = jnp.where(in_prompt[step : step + 1, :], ranks[0][step], rank)
        chosen[:, step * 128 : (step + 1) * 128] = ones_where(wanted == rank)
    table_copy.wait()
    rows = dot(chosen[...], table_here[...]).astype(bf16)
    down_copy.wait()
    partial[...] = dot_nt(rows, down_here[...]).reshape(partial.shape)


def rank_kernel(ids, sheet, highs, lows):
    square = (128, 128)
    lane = iota((8, 128), 1)
    sheet[0:16, :] = ids[pl.ds(0, 16, stride=2), :]
    sheet[16:32, :] = ids[pl.ds(1, 16, stride=2), :]
    target = iota(square, 1)
    mover = ones_where(iota(square, 0) == jnp.where(target < 64, 2 * target, 2 * target - 127))
    plain = sheet[0:16, :]
    decode_tokens = sheet[16:32, :]
    coarse = (plain >> 8).astype(f32).astype(bf16)
    fine = (plain & 255).astype(f32).astype(bf16)
    moved = dot(coarse, mover) * 256.0 + dot(fine, mover)
    sheet[0:16, :] = moved.astype(jnp.int32)
    even = sheet[pl.ds(0, 8, stride=2), :]
    odd = sheet[pl.ds(1, 8, stride=2), :]
    first = jnp.where(lane < 64, even, pltpu.roll(odd, 64, 1))
    second = jnp.where(lane < 64, pltpu.roll(even, 64, 1), odd)
    tokens = jnp.concatenate([first, second, decode_tokens], axis=0)
    sheet[0:32, :] = tokens

    def mark(block):
        line = sheet[pl.ds(block, 1), :]
        span = aligned(block, 128)
        highs[:, span] = ones_where(iota((512, 128), 0) == (line >> 7))
        lows[:, span] = ones_where(iota(square, 0) == (line & 127))

    whole_loop(32, mark, 8)
    in_prompt = dot_nt(lows[:, :KEYS], highs[:, :KEYS]) > 0.5
    alone = (dot_nt(lows[:, KEYS:], highs[:, KEYS:]) > 0.5) & jnp.logical_not(in_prompt)
    below = ones_where(iota(square, 1) < iota(square, 0))
    all_ones = jnp.ones(square, bf16)
    wide = (512, 512)
    same = (iota(wide, 0) >> 4) == (iota(wide, 1) >> 4)
    in_holder = ones_where(same & (iota(wide, 0) < iota(wide, 1)))
    prompt_flags = ones_where(in_prompt)
    alone_flags = ones_where(alone)
    prompt_columns = dot(all_ones, prompt_flags).astype(bf16)
    alone_columns = dot(all_ones, alone_flags).astype(bf16)
    prompt_rank = dot(below, prompt_flags) + dot(prompt_columns, in_holder)
    alone_rank = (
        dot(below, alone_flags) + dot(alone_columns, in_holder) + dot(prompt_columns, ones_where(same))
    )
    rank = jnp.where(in_prompt, prompt_rank, jnp.where(alone, alone_rank, 0.0))
    top_rank = jnp.max(jnp.max(rank, axis=0, keepdims=True), axis=1, keepdims=True).astype(jnp.int32)
    coded = (jnp.minimum(rank, 127.0) + jnp.where(in_prompt, 128.0, 0.0)).astype(bf16)
    pieces = []
    for chunk in range(4):
        span = slice(chunk * 1024, (chunk + 1) * 1024)
        looked = dot(coded, highs[:, span]) * lows[:, span].astype(f32)
        line = jnp.sum(looked, axis=0, keepdims=True)
        for part in range(8):
            pieces.append(line[:, part * 128 : (part + 1) * 128])
    value = jnp.concatenate(pieces, axis=0).astype(jnp.int32)
    ranks = value & 127
    holder = tokens >> 11
    tp_of = (ranks + holder) & 7
    quad = tp_of * 16 + (ranks >> 3)
    sheet[0:32, :] = quad
    sheet[32:64, :] = holder
    sheet[64:96, :] = jnp.where(value >= 128, -1, tp_of)
    sheet[96:104, :] = jnp.broadcast_to(top_rank, (8, 128))


def place_kernel(place, sheet, columns, kept, fits, quads, holders, hot_tp, hot_pool, sheet_b):
    ylo, zed, ex, core, section = place[0], place[1], place[2], place[3], place[4]
    square = (128, 128)

    def spot(block, source):
        span = aligned(block, 128)
        quads[:, span] = ones_where(iota(square, 0) == sheet[pl.ds(source, 1), :])
        holders[:, span] = ones_where(iota(square, 0) == sheet[pl.ds(source + 32, 1), :])

    whole_loop(16, lambda block: spot(block, block), 8)
    for part in range(2):
        spot(16 + part, 16 + part * 8 + zed)
    own = 16 + ylo * 8 + zed
    spot(18, own)
    up, down = iota(square, 0), iota(square, 1)
    same_tp = (up >> 4) == (down >> 4)
    same_pool = ((up >> 4) == (down >> 4)) & ((up & 1) == (down & 1))
    tp_ones = ones_where(same_tp)
    pool = ones_where(same_pool)
    before = ones_where(same_pool & (up < down))
    in_tp = ones_where(same_tp & (down < up))
    held = dot_nt(quads[:, :KEYS], holders[:, :KEYS]) > 0.5
    flags = ones_where(held)
    sums = dot(tp_ones, flags).astype(bf16)
    prompt_position = dot(in_tp, flags) + dot(sums, before)
    prompt_count = dot(sums, pool)
    positions = []
    for part in range(2):
        span = slice(KEYS + part * 128, KEYS + (part + 1) * 128)
        added = (dot_nt(quads[:, span], holders[:, span]) > 0.5) & jnp.logical_not(held)
        added_flags = ones_where(added)
        added_sums = dot(tp_ones, added_flags).astype(bf16)
        spots = dot(in_tp, added_flags) + dot(added_sums, before) + prompt_count
        spots = jnp.where(held, prompt_position, jnp.where(added, spots, 255.0))
        positions.append(jnp.minimum(spots, 255.0))
    position = jnp.where(ylo == 0, positions[0], positions[1])

    def pick(block):
        span = aligned(block, 128)
        hot_tp[:, span] = ones_where(iota((16, 128), 0) == sheet[pl.ds(block + 80, 1), :])
        line = sheet[pl.ds(block + 48, 1), :]
        line = ((line >> 4) * 2 + (line & 1)) + 4 * block
        hot_pool[:, span] = ones_where(iota((64, 128), 0) == line)

    whole_loop(16, pick, 8)
    gather_tp = ones_where(iota((16, 128), 0) == (iota((16, 128), 1) >> 4))
    base = dot(gather_tp, flags).astype(bf16)
    holder, column = iota((128, 64), 0), iota((128, 64), 1)
    pooled = ones_where((holder < 32) & (((holder >> 4) * 2 + (holder & 1)) == (column & 3)))
    needed = dot_nt(hot_tp[...], hot_pool[...]) + dot(base, pooled)
    needed = jnp.max(jnp.max(needed, axis=0, keepdims=True), axis=1, keepdims=True)
    enough = (sheet[96:97, 0:1] < 8 * SLOTS) & (needed <= float(KEPT))
    fits[0, 0] = jnp.max(jnp.where(enough, 1, 0))

    looked = dot(position.astype(bf16), holders[...]) * quads[...].astype(f32)
    line = jnp.sum(looked, axis=0, keepdims=True)
    found = [line[:, block * 128 : (block + 1) * 128] for block in range(19)]
    found = jnp.concatenate(found + [jnp.zeros((5, 128), f32)], axis=0)
    blank = jnp.zeros((5, 128), jnp.int32)
    quad_rows = jnp.concatenate([sheet[0:16, :], blank[:2], sheet[pl.ds(own, 1), :], blank], axis=0)
    holder_rows = jnp.concatenate([sheet[32:48, :], blank[:2], sheet[pl.ds(own + 32, 1), :], blank], axis=0)
    tp_rows = quad_rows >> 4
    source = ((holder_rows >> 4) * 2 + (holder_rows & 1)) * 4 + (tp_rows >> 1)
    side = jnp.where((tp_rows & 1) == core, 0, SIDE)
    final = found + (source * KEPT + side).astype(f32)
    tp_index = ex * 2 + core
    turned = pltpu.roll(final, (128 - tp_index * 16) % 128, 1)
    turned = jnp.where(iota((24, 128), 1) < 16, turned, -1.0)
    final = jnp.where(iota((24, 128), 0) == 18, turned, final)
    final = jnp.concatenate([final, jnp.zeros((104, 128), f32)], axis=0)
    columns[...] = jnp.transpose(final).astype(jnp.int32)
    few = (16, 128)
    for part in range(2):
        sheet_b[...] = positions[part]
        mine = sheet_b[pl.ds(pl.multiple_of(tp_index * 16, 16), 16), :].astype(bf16)
        spread = dot(mine, ones_where(up == (ylo * 8 + (down >> 4)) * 2 + section))
        spread = jnp.where((iota(few, 1) & 15) == iota(few, 0), spread, 0.0)
        kept[part : part + 1, :] = jnp.sum(spread, axis=0, keepdims=True)


def finish_kernel(parts, gain, sent):
    latent = parts[0]
    for tp in range(1, parts.shape[0]):
        latent = latent + parts[tp]
    plain = latent[:, :LAT]
    scaled = plain * lax.rsqrt(jnp.mean(plain * plain, axis=-1, keepdims=True) + norm_eps) * gain[...]
    rotary = latent[:, LAT:]
    coarse = rotary.astype(bf16)
    fine = (rotary - coarse.astype(f32)).astype(bf16)
    row = jnp.concatenate([scaled.astype(bf16), coarse, fine], axis=-1)
    for peer in range(sent.shape[0]):
        sent[peer] = row


def keep_kernel(kept, rows, sent):
    for ylo in range(2):
        chosen = iota((KEPT, 128), 0).astype(f32) == kept[ylo : ylo + 1, :]
        row = dot(ones_where(chosen), rows[...]).astype(bf16)
        for peer in range(8):
            sent[ylo * 8 + peer] = row


def cache_kernel(lengths, query, cache, out, level):
    length = lengths[pl.program_id(0)]
    scores = dot(query[0], cache[0]) * base_two
    scores = jnp.where(iota(scores.shape, 1) < length, scores, masked_fill)
    highest = jnp.max(scores, axis=-1, keepdims=True)
    weights = jnp.exp2(scores - highest)
    total = jnp.sum(weights, axis=-1, keepdims=True)
    out[...] = (dot_nt(weights.astype(bf16), cache[0, :LAT, :]) * (1.0 / total)).astype(bf16)
    level[...] = jnp.broadcast_to(highest + jnp.log2(total), level.shape)


def hot_rows(hot, columns, prompt, side):
    turned = pltpu.roll(columns[...], (128 - prompt * 8) % 128, 1) - side * SIDE
    for block in range(8):
        hot[block * 128 : (block + 1) * 128, :] = ones_where(iota((128, SIDE), 1) == turned[:, block : block + 1])


def empty_kernel(*refs):
    pass


def fresh_hot(columns, side):
    return ones_where(iota((128, SIDE), 1) == columns[:, 18:19] - side * SIDE)


def put_keys(keys, span, found, factor):
    turning = found[:, LAT:]
    turning = turning + pltpu.roll(turning, 64, 1)
    turned = turning * factor + pltpu.roll(turning, 32, 1) * pltpu.roll(factor, 64, 1)
    keys[span, :LAT] = found[:, :LAT].astype(bf16)
    keys[span, LAT:] = turned[:, : KVW - LAT].astype(bf16)


def copy_in(source, target, sem):
    copy = pltpu.make_async_copy(source, target, sem)
    copy.start()
    copy.wait()


def weigh(scores, old):
    new = jnp.maximum(old, jnp.max(scores, axis=-1, keepdims=True))
    weights = jnp.exp2(scores - new)
    return new, jnp.exp2(old - new), jnp.sum(weights, axis=-1, keepdims=True), weights.astype(bf16)


def near_kernel(place, owner, slots, columns, near, hot):
    group = place[0] * 8 + place[1]

    @pl.when(place[4] == 1)
    def _():
        near[KEYS : KEYS + 128, :] = dot(fresh_hot(columns, 0), slots[...]).astype(bf16)

        def open_prompt(prompt):
            @pl.when(owner[prompt] == group)
            def _():
                hot_rows(hot, columns, prompt, 0)

                def open_part(part):
                    near[aligned(prompt * 2 + part, 512), :] = dot(hot[aligned(part, 512), :], slots[...]).astype(bf16)

                whole_loop(2, open_part, 2)

        whole_loop(2, open_prompt)


def decode_kernel(
    place, owner, fits, near, others, columns, factors, new_factors, query, earlier, level, spare, spare_new,
    out, keys, hot, highest, total, mixed, sem
):
    group = place[0] * 8 + place[1]
    fitting = fits[0, 0] == 1

    @pl.when(place[4] == 1)
    def _():
        @pl.when(fitting)
        def _():
            span = slice(KEYS, KEYS + 128)
            found = near[span, :].astype(f32) + dot(fresh_hot(columns, 1), others[...])
            put_keys(keys, span, found, new_factors[...])

        @pl.when(jnp.logical_not(fitting))
        def _():
            copy_in(spare_new, keys.at[pl.ds(KEYS, 128)], sem)

        newest = keys[KEYS : KEYS + 128, :]

        def begin(piece):
            span = aligned(piece, 512)
            scores = dot_nt(query[span, :], newest) * base_two
            key = iota(scores.shape, 1)
            row = iota(scores.shape, 0) & 15
            allowed = ((key >> 1) == (row >> 1)) & ((key & 1) <= (row & 1))
            scores = jnp.where(allowed, scores, masked_fill)
            new, factor, summed, weights = weigh(scores, level[span, 0:1])
            mixed[span, :] = earlier[span, :].astype(f32) * factor + dot(weights, newest[:, :LAT])
            highest[span, :] = jnp.broadcast_to(new, (512, 128))
            total[span, :] = jnp.broadcast_to(factor + summed, (512, 128))

        whole_loop(2, begin, 2)

        def add_prompt(prompt):
            @pl.when(owner[prompt] == group)
            def _():
                @pl.when(fitting)
                def _():
                    hot_rows(hot, columns, prompt, 1)

                    def open_part(part):
                        span = aligned(prompt * 2 + part, 512)
                        found = near[span, :].astype(f32) + dot(hot[aligned(part, 512), :], others[...])
                        put_keys(keys, span, found, factors[aligned(part, 512), :])

                    whole_loop(2, open_part, 2)

                @pl.when(jnp.logical_not(fitting))
                def _():
                    copy_in(spare.at[pl.ds(prompt * 1024, 1024)], keys.at[pl.ds(prompt * 1024, 1024)], sem)

                def add_part(piece):
                    span = aligned(piece, 512)
                    some = keys[aligned(prompt, 1024), :]
                    new, factor, summed, weights = weigh(dot_nt(query[span, :], some) * base_two, highest[span, 0:1])
                    mixed[span, :] = mixed[span, :] * factor + dot(weights, some[:, :LAT])
                    highest[span, :] = jnp.broadcast_to(new, (512, 128))
                    total[span, :] = total[span, :] * factor + summed

                whole_loop(2, add_part, 2)

        whole_loop(2, add_prompt)

        def tp_rows(tp):
            for head in range(8):
                rows = pl.ds(pl.multiple_of(tp * 128 + head * 16, 16), 16)
                some = mixed[rows, :] * (1.0 / total[rows, 0:1])
                out[aligned(tp, 16), head * LAT : (head + 1) * LAT] = some.astype(bf16)

        whole_loop(8, tp_rows, 2)


def prefill_kernel(place, fits, slots, others, columns, factors, query, spare, out, keys, hot, mixed, lines, pairs, sem):
    group = place[0] * 8 + place[1]
    fitting = fits[0, 0] == 1

    @pl.when(place[4] == 0)
    def _():
        def add_prompt(prompt):
            @pl.when(fitting)
            def _():
                for side in range(2):
                    hot_rows(hot, columns, prompt, side)

                    def open_part(part, side=side):
                        span = aligned(part, 512)
                        if side == 0:
                            lines[span, :] = dot(hot[span, :], slots[...])
                        else:
                            found = lines[span, :] + dot(hot[span, :], others[...])
                            put_keys(keys, span, found, factors[span, :])

                    whole_loop(2, open_part, 2)

            @pl.when(jnp.logical_not(fitting))
            def _():
                copy_in(spare.at[pl.ds(prompt * 1024, 1024)], keys, sem)

            span = aligned(prompt, 512)
            some = keys[...]
            scores = dot_nt(query[span, :], some) * base_two
            last = (iota((512, 1), 0) & 63) + group * 64
            scores = jnp.where(iota(scores.shape, 1) <= last, scores, masked_fill)
            _, _, summed, weights = weigh(scores, jnp.full((512, 1), masked_fill, f32))
            added = dot(weights, some[:, :LAT]) * (1.0 / summed)
            for column in range(4):
                mixed[column, span, :] = added[:, column * 128 : (column + 1) * 128]

        whole_loop(2, add_prompt)

        def head_rows(head):
            for column in range(4):
                for prompt in range(2):
                    start = pl.multiple_of(prompt * 512 + head * 64, 64)
                    pairs[column, pl.ds(prompt, 64, stride=2), :] = mixed[column, pl.ds(start, 64), :]
                out[:, pl.ds(pl.multiple_of(head * LAT + column * 128, 128), 128)] = pairs[column].astype(bf16)

        whole_loop(8, head_rows, 2)


def join_kernel(place, turned, prefilled, out, sems):
    def bring(source):
        copies = []
        for part in range(4):
            span = pl.ds(part * 32, 32)
            copies.append(pltpu.make_async_copy(source.at[span], out.at[span], sems.at[part]))
        for copy in copies:
            copy.start()
        for copy in copies:
            copy.wait()

    @pl.when(place[4] == 0)
    def _():
        bring(prefilled)

    @pl.when(place[4] == 1)
    def _():
        bring(turned)


def rope_factors(position):
    frequency = np.float32(rope_base) ** (-np.arange(32, dtype=np.float32) / np.float32(32))
    angles = position[:, None] * frequency[None, :]
    if isinstance(position, np.ndarray):
        angles = angles.astype(np.float32).astype(np.float64)
        cosine, sine = np.cos(angles), np.sin(angles)
        return np.concatenate([cosine, cosine, -sine, sine], axis=-1).astype(np.float32)
    cosine, sine = jnp.cos(angles), jnp.sin(angles)
    return jnp.concatenate([cosine, cosine, -sine, sine], axis=-1)


def finish_keys(latent, latent_gain, position):
    plain = latent[:, :LAT]
    scaled = plain * lax.rsqrt(jnp.mean(plain * plain, axis=-1, keepdims=True) + norm_eps) * latent_gain
    factors = rope_factors(position.astype(f32))
    rotary = latent[:, LAT:]
    swapped = jnp.concatenate([rotary[:, 32:], rotary[:, :32]], axis=-1)
    turned = rotary * factors[:, :64] + swapped * factors[:, 64:]
    return jnp.concatenate([scaled, turned], axis=-1).astype(bf16)


def dense_keys(token_ids, place, embed_table, down, latent_gain, cache_length):
    group = place[0] * 8 + place[1]
    tp_index = place[2] * 2 + place[3]
    every = lax.all_to_all(jnp.broadcast_to(token_ids, (32, 128)).reshape(32, 1, 128), HOLDERS, 0, 0, tiled=True)
    local_row = every.reshape(-1) - (group * 2 + place[4]) * 2048
    inside = (local_row >= 0) & (local_row < 2048)
    picked = jnp.take(embed_table, jnp.clip(local_row, 0, 2047), axis=0)
    picked = jnp.where(inside[:, None], picked, jnp.zeros_like(picked)).reshape(32, 128, 896)
    embedded = jnp.sum(lax.all_to_all(picked, HOLDERS, 0, 0, tiled=True).astype(f32), axis=0).astype(bf16)
    partial = dot_nt(embedded, down)
    spread = jnp.broadcast_to(partial[None], (8, 128, KVW))
    latent = jnp.sum(lax.all_to_all(spread, TP, 0, 0, tiled=True), axis=0)
    index = jnp.arange(128, dtype=jnp.int32)
    mine = finish_keys(latent, latent_gain, group * 64 + index // 2)
    spread = jnp.broadcast_to(mine[None], (32, 128, KVW))
    prompts = lax.all_to_all(spread, HOLDERS, 0, 0, tiled=True).reshape(16, 2, 64, 2, KVW)[:, 0]
    prompts = jnp.transpose(prompts, (2, 0, 1, 3)).reshape(KEYS, KVW)
    own = lax.dynamic_slice_in_dim(latent, tp_index * 16, 16, 0)
    fresh = finish_keys(own, latent_gain, (cache_length[:, None] + jnp.arange(2, dtype=jnp.int32)[None]).reshape(-1))
    return prompts, jnp.concatenate([fresh, jnp.zeros((112, KVW), bf16)], axis=0)


def params(mebibytes):
    return pltpu.CompilerParams(vmem_limit_bytes=mebibytes * 1024 * 1024)


def shards(
    token_ids,
    embed_table,
    latent_down,
    latent_gain,
    prefill_query,
    decode_query,
    latent_cache,
    cache_length,
    prompt_owner,
):
    place = jnp.stack([lax.axis_index(name) for name in ("ylo", "z", "x", "core", "role")]).astype(jnp.int32)
    down = jnp.transpose(latent_down)
    whole = pl.BlockSpec(memory_space=VMEM)
    scalars = pl.BlockSpec(memory_space=SMEM)
    anywhere = pl.BlockSpec(memory_space=pl.ANY)
    shaped = jax.ShapeDtypeStruct

    every = lax.all_to_all(jnp.broadcast_to(token_ids, (32, 128)).reshape(32, 1, 128), HOLDERS, 0, 0, tiled=True)
    every = every.reshape(32, 128)

    earlier, level = pl.pallas_call(
        cache_kernel,
        grid_spec=pltpu.PrefetchScalarGridSpec(
            num_scalar_prefetch=1,
            grid=(8,),
            in_specs=[
                pl.BlockSpec((1, 128, KVW), lambda row, lengths: (row, 0, 0)),
                pl.BlockSpec((1, KVW, 512), lambda row, lengths: (row, 0, 0)),
            ],
            out_specs=[
                pl.BlockSpec((128, LAT), lambda row, lengths: (row, 0)),
                pl.BlockSpec((128, 128), lambda row, lengths: (row, 0)),
            ],
        ),
        out_shape=(shaped((1024, LAT), bf16), shaped((1024, 128), f32)),
        compiler_params=params(56),
        cost_estimate=pl.CostEstimate(flops=12 * 10**8, bytes_accessed=7 * 10**6, transcendentals=524288),
        name="cache_rows",
    )(cache_length, decode_query.reshape(8, 128, KVW), jnp.swapaxes(latent_cache, 1, 2))
    every, earlier, level = lax.optimization_barrier((every, earlier, level))

    partial = pl.pallas_call(
        select_kernel,
        out_shape=shaped((8, SLOTS, KVW), f32),
        in_specs=[scalars, whole, anywhere, anywhere],
        out_specs=whole,
        scratch_shapes=[
            VMEM((16, 4096), bf16),
            VMEM((128, 4096), bf16),
            VMEM((8 * SLOTS, 2048), bf16),
            VMEM((2048, 896), bf16),
            VMEM((KVW, 896), bf16),
            pltpu.SemaphoreType.DMA((2,)),
        ],
        compiler_params=params(16),
        cost_estimate=pl.CostEstimate(flops=3 * 10**9, bytes_accessed=5 * 10**6, transcendentals=0),
        name="select_rows",
    )(place, every, embed_table, down)
    parts = lax.all_to_all(partial, TP, 0, 0, tiled=True)

    sheet = pl.pallas_call(
        rank_kernel,
        out_shape=shaped((104, 128), jnp.int32),
        in_specs=[whole],
        out_specs=whole,
        scratch_shapes=[VMEM((512, 4096), bf16), VMEM((128, 4096), bf16)],
        compiler_params=params(18),
        cost_estimate=pl.CostEstimate(flops=2 * 10**9, bytes_accessed=10**6, transcendentals=0),
        name="rank_rows",
    )(every)
    columns, kept, fits = pl.pallas_call(
        place_kernel,
        out_shape=(shaped((128, 128), jnp.int32), shaped((8, 128), f32), shaped((1, 1), jnp.int32)),
        in_specs=[scalars, whole],
        out_specs=(whole, whole, scalars),
        scratch_shapes=[
            VMEM((128, 19 * 128), bf16),
            VMEM((128, 19 * 128), bf16),
            VMEM((16, 2048), bf16),
            VMEM((64, 2048), bf16),
            VMEM((128, 128), f32),
        ],
        compiler_params=params(12),
        cost_estimate=pl.CostEstimate(flops=10**9, bytes_accessed=10**6, transcendentals=0),
        name="place_rows",
    )(place, sheet)
    parts, columns, kept, fits = lax.optimization_barrier((parts, columns, kept, fits))
    spare, spare_new = lax.cond(
        fits[0, 0] == 1,
        lambda *unused: tuple(
            pl.pallas_call(
                empty_kernel,
                out_shape=[shaped((KEYS, KVW), bf16), shaped((128, KVW), bf16)],
                out_specs=[anywhere] * 2,
                name="no_keys",
            )()
        ),
        dense_keys,
        token_ids,
        place,
        embed_table,
        down,
        latent_gain,
        cache_length,
    )
    parts, spare, spare_new = lax.optimization_barrier((parts, spare, spare_new))
    sent = pl.pallas_call(
        finish_kernel,
        out_shape=shaped((8, SLOTS, WIDE), bf16),
        in_specs=[whole, whole],
        out_specs=whole,
        compiler_params=params(8),
        name="finish_rows",
    )(parts, latent_gain.reshape(1, LAT))
    arrived = lax.all_to_all(sent, "z", 0, 0, tiled=True)

    prompt_query = jnp.transpose(prefill_query.reshape(64, 2, 8, KVW), (1, 2, 0, 3)).reshape(1024, KVW)

    def by_head(rows):
        return jnp.transpose(rows.reshape(16, 64, -1), (1, 0, 2)).reshape(1024, -1)

    row_query, earlier, level = by_head(decode_query), by_head(earlier), by_head(level)
    new_position = (cache_length[:, None] + jnp.arange(2, dtype=jnp.int32)[None]).reshape(-1)
    new_factors = jnp.pad(rope_factors(new_position.astype(f32)), ((0, 112), (0, 0)))
    arrived, prompt_query, new_factors, row_query, earlier, level = lax.optimization_barrier(
        (arrived, prompt_query, new_factors, row_query, earlier, level)
    )
    handed = pl.pallas_call(
        keep_kernel,
        out_shape=shaped((16, KEPT, WIDE), bf16),
        in_specs=[whole, whole],
        out_specs=whole,
        compiler_params=params(8),
        name="keep_rows",
    )(kept, arrived.reshape(8 * SLOTS, WIDE))
    slots = lax.all_to_all(handed, PLANE, 0, 0, tiled=True).reshape(SIDE, WIDE)

    others = lax.ppermute(slots, "core", [(0, 1), (1, 0)])

    near = pl.pallas_call(
        near_kernel,
        out_shape=shaped((KEYS + 128, WIDE), bf16),
        in_specs=[scalars, scalars, whole, whole],
        out_specs=whole,
        scratch_shapes=[VMEM((1024, SIDE), bf16)],
        compiler_params=params(12),
        cost_estimate=pl.CostEstimate(flops=2 * 10**9, bytes_accessed=10**6, transcendentals=0),
        name="near_keys",
    )(place, prompt_owner, slots, columns)
    factors = jnp.asarray(rope_factors(np.arange(1024, dtype=np.float32)))
    decoded = pl.pallas_call(
        decode_kernel,
        out_shape=shaped((128, 4096), bf16),
        in_specs=[scalars] * 3 + [whole] * 8 + [anywhere] * 2,
        out_specs=whole,
        scratch_shapes=[
            VMEM((KEYS + 128, KVW), bf16),
            VMEM((1024, SIDE), bf16),
            VMEM((1024, 128), f32),
            VMEM((1024, 128), f32),
            VMEM((1024, LAT), f32),
            pltpu.SemaphoreType.DMA,
        ],
        compiler_params=params(20),
        cost_estimate=pl.CostEstimate(flops=5 * 10**9, bytes_accessed=7 * 10**6, transcendentals=10**6),
        name="decode_rows",
    )(
        place, prompt_owner, fits, near, others, columns, factors, new_factors, row_query, earlier, level, spare, spare_new
    )
    turned = lax.all_to_all(decoded.reshape(8, 16, 4096), TP, 0, 0, tiled=True).reshape(128, 4096)
    prefilled = pl.pallas_call(
        prefill_kernel,
        out_shape=shaped((128, 4096), bf16),
        in_specs=[scalars] * 2 + [whole] * 5 + [anywhere],
        out_specs=whole,
        scratch_shapes=[
            VMEM((1024, KVW), bf16),
            VMEM((1024, SIDE), bf16),
            VMEM((4, 1024, 128), f32),
            VMEM((1024, WIDE), f32),
            VMEM((4, 128, 128), f32),
            pltpu.SemaphoreType.DMA,
        ],
        compiler_params=params(20),
        cost_estimate=pl.CostEstimate(flops=7 * 10**9, bytes_accessed=7 * 10**6, transcendentals=10**6),
        name="prefill_rows",
    )(place, fits, slots, others, columns, factors, prompt_query, spare)
    out = pl.pallas_call(
        join_kernel,
        out_shape=shaped((128, 4096), bf16),
        in_specs=[scalars] + [anywhere] * 2,
        out_specs=anywhere,
        scratch_shapes=[pltpu.SemaphoreType.DMA((4,))],
        compiler_params=params(4),
        name="join_rows",
    )(place, turned, prefilled)
    return out[None]


def solution(mesh):
    fine_mesh = Mesh(mesh.devices.reshape(2, 8, 4, 2, 2), ("ylo", "z", "x", "core", "role"))
    ctx, tp = ("ylo", "z"), ("x", "core")
    in_specs = (
        P("role", ctx),
        P(ctx + ("role",), tp),
        P(tp, None),
        P(),
        P(ctx, tp, None),
        P(ctx + tp, None, None, None),
        P(ctx + tp, None, None),
        P(ctx + tp),
        P(),
    )
    out_specs = P("role", ctx, tp)
    return jax.shard_map(shards, mesh=fine_mesh, in_specs=in_specs, out_specs=out_specs, check_vma=False)
```

```python
import jax
import jax.numpy as jnp
import numpy as np
from jax import lax
from jax.experimental import pallas as pl
from jax.experimental.pallas import tpu as pltpu
from jax.sharding import Mesh
from jax.sharding import PartitionSpec as P

LAT = 512
KVW = 576
STEPS = 2
WIDE = 640
SLOTS = 16
KEPT = 48
SIDE = 16 * KEPT
KEYS = 2048

score_scale = 0.07216878364870322
base_two = score_scale * 1.4426950408889634
masked_fill = -1e30
norm_eps = 1e-06
rope_base = 10000.0
bf16 = jnp.bfloat16
f32 = jnp.float32
SMEM = pltpu.SMEM
VMEM = pltpu.VMEM

HOLDERS = ("ylo", "z", "role")
PLANE = ("ylo", "role", "x")
TP = ("x", "core")


def iota(shape, axis):
    return lax.broadcasted_iota(jnp.int32, shape, axis)


def ones_where(flags):
    return jnp.where(flags, 1.0, 0.0).astype(bf16)


def dot(left, right):
    return lax.dot_general(left, right, (((1,), (0,)), ((), ())), preferred_element_type=f32)


def dot_nt(left, right):
    return lax.dot_general(left, right, (((1,), (1,)), ((), ())), preferred_element_type=f32)


def whole_loop(count, body, unroll=1):
    def step(index, carry):
        body(index)
        return carry

    lax.fori_loop(0, count, step, 0, unroll=unroll)


def aligned(index, size):
    return pl.ds(pl.multiple_of(index * size, size), size)


def spread_kernel(ids, out):
    out[...] = jnp.broadcast_to(ids[...].reshape(1, 1, 128), out.shape)


def select_kernel(place, ids, table, down, partial, hots, lows, chosen, table_here, down_here, sems):
    holder = (place[0] * 8 + place[1]) * 2 + place[4]
    table_copy = pltpu.make_async_copy(table, table_here, sems.at[0])
    down_copy = pltpu.make_async_copy(down, down_here, sems.at[1])
    table_copy.start()
    down_copy.start()
    for line in range(32):
        tokens = ids[line : line + 1, :]
        start = ((line & 1) * 16 + (line >> 1)) * 128
        span = slice(start, start + 128)
        hots[:, span] = ones_where(iota((16, 128), 0) == (tokens >> 7) - holder * 16)
        lows[:, span] = ones_where(iota((128, 128), 0) == (tokens & 127))
    in_prompt = dot_nt(hots[:, :KEYS], lows[:, :KEYS]) > 0.5
    alone = (dot_nt(hots[:, KEYS:], lows[:, KEYS:]) > 0.5) & jnp.logical_not(in_prompt)
    upper = ones_where(iota((128, 128), 0) < iota((128, 128), 1))
    all_ones = jnp.ones((128, 128), bf16)
    row = iota((8 * SLOTS, 128), 0)
    wanted = ((row & 15) * 8 + (((row >> 4) - holder) & 7)).astype(f32)
    before = jnp.zeros((1, 128), f32)
    ranks = []
    for present in (in_prompt, alone):
        flags = ones_where(present)
        within = dot(flags, upper)
        totals = dot(flags, all_ones)
        lines = []
        for step in range(16):
            lines.append(within[step : step + 1, :] + before)
            before = before + totals[step : step + 1, :]
        ranks.append(lines)
    for step in range(16):
        rank = jnp.where(alone[step : step + 1, :], ranks[1][step], -1.0)
        rank = jnp.where(in_prompt[step : step + 1, :], ranks[0][step], rank)
        chosen[:, step * 128 : (step + 1) * 128] = ones_where(wanted == rank)
    table_copy.wait()
    rows = dot(chosen[...], table_here[...]).astype(bf16)
    down_copy.wait()
    partial[...] = dot_nt(rows, down_here[...]).reshape(partial.shape)


def rank_kernel(ids, sheet, highs, lows):
    square = (128, 128)
    lane = iota((8, 128), 1)
    sheet[0:16, :] = ids[pl.ds(0, 16, stride=2), :]
    sheet[16:32, :] = ids[pl.ds(1, 16, stride=2), :]
    target = iota(square, 1)
    mover = ones_where(iota(square, 0) == jnp.where(target < 64, 2 * target, 2 * target - 127))
    plain = sheet[0:16, :]
    decode_tokens = sheet[16:32, :]
    coarse = (plain >> 8).astype(f32).astype(bf16)
    fine = (plain & 255).astype(f32).astype(bf16)
    moved = dot(coarse, mover) * 256.0 + dot(fine, mover)
    sheet[0:16, :] = moved.astype(jnp.int32)
    even = sheet[pl.ds(0, 8, stride=2), :]
    odd = sheet[pl.ds(1, 8, stride=2), :]
    first = jnp.where(lane < 64, even, pltpu.roll(odd, 64, 1))
    second = jnp.where(lane < 64, pltpu.roll(even, 64, 1), odd)
    tokens = jnp.concatenate([first, second, decode_tokens], axis=0)
    sheet[0:32, :] = tokens

    def mark(block):
        line = sheet[pl.ds(block, 1), :]
        span = aligned(block, 128)
        highs[:, span] = ones_where(iota((512, 128), 0) == (line >> 7))
        lows[:, span] = ones_where(iota(square, 0) == (line & 127))

    whole_loop(32, mark, 8)
    in_prompt = dot_nt(lows[:, :KEYS], highs[:, :KEYS]) > 0.5
    alone = (dot_nt(lows[:, KEYS:], highs[:, KEYS:]) > 0.5) & jnp.logical_not(in_prompt)
    below = ones_where(iota(square, 1) < iota(square, 0))
    all_ones = jnp.ones(square, bf16)
    wide = (512, 512)
    same = (iota(wide, 0) >> 4) == (iota(wide, 1) >> 4)
    in_holder = ones_where(same & (iota(wide, 0) < iota(wide, 1)))
    prompt_flags = ones_where(in_prompt)
    alone_flags = ones_where(alone)
    prompt_columns = dot(all_ones, prompt_flags).astype(bf16)
    alone_columns = dot(all_ones, alone_flags).astype(bf16)
    prompt_rank = dot(below, prompt_flags) + dot(prompt_columns, in_holder)
    alone_rank = (
        dot(below, alone_flags) + dot(alone_columns, in_holder) + dot(prompt_columns, ones_where(same))
    )
    rank = jnp.where(in_prompt, prompt_rank, jnp.where(alone, alone_rank, 0.0))
    top_rank = jnp.max(jnp.max(rank, axis=0, keepdims=True), axis=1, keepdims=True).astype(jnp.int32)
    coded = (jnp.minimum(rank, 127.0) + jnp.where(in_prompt, 128.0, 0.0)).astype(bf16)
    pieces = []
    for chunk in range(4):
        span = slice(chunk * 1024, (chunk + 1) * 1024)
        looked = dot(coded, highs[:, span]) * lows[:, span].astype(f32)
        line = jnp.sum(looked, axis=0, keepdims=True)
        for part in range(8):
            pieces.append(line[:, part * 128 : (part + 1) * 128])
    value = jnp.concatenate(pieces, axis=0).astype(jnp.int32)
    ranks = value & 127
    holder = tokens >> 11
    tp_of = (ranks + holder) & 7
    quad = tp_of * 16 + (ranks >> 3)
    sheet[0:32, :] = quad
    sheet[32:64, :] = holder
    sheet[64:96, :] = jnp.where(value >= 128, -1, tp_of)
    sheet[96:104, :] = jnp.broadcast_to(top_rank, (8, 128))


def place_kernel(place, sheet, columns, kept, fits, quads, holders, hot_tp, hot_pool, sheet_b):
    ylo, zed, ex, core, section = place[0], place[1], place[2], place[3], place[4]
    square = (128, 128)

    def spot(block, source):
        span = aligned(block, 128)
        quads[:, span] = ones_where(iota(square, 0) == sheet[pl.ds(source, 1), :])
        holders[:, span] = ones_where(iota(square, 0) == sheet[pl.ds(source + 32, 1), :])

    whole_loop(16, lambda block: spot(block, block), 8)
    for part in range(2):
        spot(16 + part, 16 + part * 8 + zed)
    own = 16 + ylo * 8 + zed
    spot(18, own)
    up, down = iota(square, 0), iota(square, 1)
    same_tp = (up >> 4) == (down >> 4)
    same_pool = ((up >> 4) == (down >> 4)) & ((up & 1) == (down & 1))
    tp_ones = ones_where(same_tp)
    pool = ones_where(same_pool)
    before = ones_where(same_pool & (up < down))
    in_tp = ones_where(same_tp & (down < up))
    held = dot_nt(quads[:, :KEYS], holders[:, :KEYS]) > 0.5
    flags = ones_where(held)
    sums = dot(tp_ones, flags).astype(bf16)
    prompt_position = dot(in_tp, flags) + dot(sums, before)
    prompt_count = dot(sums, pool)
    positions = []
    for part in range(2):
        span = slice(KEYS + part * 128, KEYS + (part + 1) * 128)
        added = (dot_nt(quads[:, span], holders[:, span]) > 0.5) & jnp.logical_not(held)
        added_flags = ones_where(added)
        added_sums = dot(tp_ones, added_flags).astype(bf16)
        spots = dot(in_tp, added_flags) + dot(added_sums, before) + prompt_count
        spots = jnp.where(held, prompt_position, jnp.where(added, spots, 255.0))
        positions.append(jnp.minimum(spots, 255.0))
    position = jnp.where(ylo == 0, positions[0], positions[1])

    def pick(block):
        span = aligned(block, 128)
        hot_tp[:, span] = ones_where(iota((16, 128), 0) == sheet[pl.ds(block + 80, 1), :])
        line = sheet[pl.ds(block + 48, 1), :]
        line = ((line >> 4) * 2 + (line & 1)) + 4 * block
        hot_pool[:, span] = ones_where(iota((64, 128), 0) == line)

    whole_loop(16, pick, 8)
    gather_tp = ones_where(iota((16, 128), 0) == (iota((16, 128), 1) >> 4))
    base = dot(gather_tp, flags).astype(bf16)
    holder, column = iota((128, 64), 0), iota((128, 64), 1)
    pooled = ones_where((holder < 32) & (((holder >> 4) * 2 + (holder & 1)) == (column & 3)))
    needed = dot_nt(hot_tp[...], hot_pool[...]) + dot(base, pooled)
    needed = jnp.max(jnp.max(needed, axis=0, keepdims=True), axis=1, keepdims=True)
    enough = (sheet[96:97, 0:1] < 8 * SLOTS) & (needed <= float(KEPT))
    fits[0, 0] = jnp.max(jnp.where(enough, 1, 0))

    looked = dot(position.astype(bf16), holders[...]) * quads[...].astype(f32)
    line = jnp.sum(looked, axis=0, keepdims=True)
    found = [line[:, block * 128 : (block + 1) * 128] for block in range(19)]
    found = jnp.concatenate(found + [jnp.zeros((5, 128), f32)], axis=0)
    blank = jnp.zeros((5, 128), jnp.int32)
    quad_rows = jnp.concatenate([sheet[0:16, :], blank[:2], sheet[pl.ds(own, 1), :], blank], axis=0)
    holder_rows = jnp.concatenate([sheet[32:48, :], blank[:2], sheet[pl.ds(own + 32, 1), :], blank], axis=0)
    tp_rows = quad_rows >> 4
    source = ((holder_rows >> 4) * 2 + (holder_rows & 1)) * 4 + (tp_rows >> 1)
    side = jnp.where((tp_rows & 1) == core, 0, SIDE)
    final = found + (source * KEPT + side).astype(f32)
    tp_index = ex * 2 + core
    turned = pltpu.roll(final, (128 - tp_index * 16) % 128, 1)
    turned = jnp.where(iota((24, 128), 1) < 16, turned, -1.0)
    final = jnp.where(iota((24, 128), 0) == 18, turned, final)
    final = jnp.concatenate([final, jnp.zeros((104, 128), f32)], axis=0)
    columns[...] = jnp.transpose(final).astype(jnp.int32)
    few = (16, 128)
    for part in range(2):
        sheet_b[...] = positions[part]
        mine = sheet_b[pl.ds(pl.multiple_of(tp_index * 16, 16), 16), :].astype(bf16)
        spread = dot(mine, ones_where(up == (ylo * 8 + (down >> 4)) * 2 + section))
        spread = jnp.where((iota(few, 1) & 15) == iota(few, 0), spread, 0.0)
        kept[part : part + 1, :] = jnp.sum(spread, axis=0, keepdims=True)


def finish_kernel(parts, gain, sent):
    latent = parts[0]
    for tp in range(1, parts.shape[0]):
        latent = latent + parts[tp]
    plain = latent[:, :LAT]
    scaled = plain * lax.rsqrt(jnp.mean(plain * plain, axis=-1, keepdims=True) + norm_eps) * gain[...]
    rotary = latent[:, LAT:]
    coarse = rotary.astype(bf16)
    fine = (rotary - coarse.astype(f32)).astype(bf16)
    row = jnp.concatenate([scaled.astype(bf16), coarse, fine], axis=-1)
    for peer in range(sent.shape[0]):
        sent[peer] = row


def keep_kernel(kept, rows, sent):
    for ylo in range(2):
        chosen = iota((KEPT, 128), 0).astype(f32) == kept[ylo : ylo + 1, :]
        row = dot(ones_where(chosen), rows[...]).astype(bf16)
        for peer in range(8):
            sent[ylo * 8 + peer] = row


def cache_kernel(lengths, query, cache, out, level):
    length = lengths[pl.program_id(0)]
    scores = dot(query[0], cache[0]) * base_two
    scores = jnp.where(iota(scores.shape, 1) < length, scores, masked_fill)
    highest = jnp.max(scores, axis=-1, keepdims=True)
    weights = jnp.exp2(scores - highest)
    total = jnp.sum(weights, axis=-1, keepdims=True)
    out[...] = (dot_nt(weights.astype(bf16), cache[0, :LAT, :]) * (1.0 / total)).astype(bf16)
    level[...] = jnp.broadcast_to(highest + jnp.log2(total), level.shape)


def hot_rows(hot, columns, prompt, side):
    turned = pltpu.roll(columns[...], (128 - prompt * 8) % 128, 1) - side * SIDE
    for block in range(8):
        hot[block * 128 : (block + 1) * 128, :] = ones_where(iota((128, SIDE), 1) == turned[:, block : block + 1])


def empty_kernel(*refs):
    pass


def fresh_hot(columns, side):
    return ones_where(iota((128, SIDE), 1) == columns[:, 18:19] - side * SIDE)


def put_keys(keys, span, found, factor):
    turning = found[:, LAT:]
    turning = turning + pltpu.roll(turning, 64, 1)
    turned = turning * factor + pltpu.roll(turning, 32, 1) * pltpu.roll(factor, 64, 1)
    keys[span, :LAT] = found[:, :LAT].astype(bf16)
    keys[span, LAT:] = turned[:, : KVW - LAT].astype(bf16)


def copy_in(source, target, sem):
    copy = pltpu.make_async_copy(source, target, sem)
    copy.start()
    copy.wait()


def weigh(scores, old):
    new = jnp.maximum(old, jnp.max(scores, axis=-1, keepdims=True))
    weights = jnp.exp2(scores - new)
    return new, jnp.exp2(old - new), jnp.sum(weights, axis=-1, keepdims=True), weights.astype(bf16)


def near_kernel(place, owner, slots, columns, near, hot):
    group = place[0] * 8 + place[1]

    @pl.when(place[4] == 1)
    def _():
        near[KEYS : KEYS + 128, :] = dot(fresh_hot(columns, 0), slots[...]).astype(bf16)

    def open_prompt(prompt):
        @pl.when((place[4] == 0) | (owner[prompt] == group))
        def _():
            hot_rows(hot, columns, prompt, 0)

            def open_part(part):
                near[aligned(prompt * 2 + part, 512), :] = dot(hot[aligned(part, 512), :], slots[...]).astype(bf16)

            whole_loop(2, open_part, 2)

    whole_loop(2, open_prompt)


def decode_kernel(
    place, owner, fits, near, others, columns, factors, new_factors, query, earlier, level, spare, spare_new,
    out, keys, hot, highest, total, mixed, sem
):
    group = place[0] * 8 + place[1]
    fitting = fits[0, 0] == 1

    @pl.when(place[4] == 1)
    def _():
        @pl.when(fitting)
        def _():
            span = slice(KEYS, KEYS + 128)
            found = near[span, :].astype(f32) + dot(fresh_hot(columns, 1), others[...])
            put_keys(keys, span, found, new_factors[...])

        @pl.when(jnp.logical_not(fitting))
        def _():
            copy_in(spare_new, keys.at[pl.ds(KEYS, 128)], sem)

        newest = keys[KEYS : KEYS + 128, :]

        def begin(piece):
            span = aligned(piece, 512)
            scores = dot_nt(query[span, :], newest) * base_two
            key = iota(scores.shape, 1)
            row = iota(scores.shape, 0) & 15
            allowed = ((key >> 1) == (row >> 1)) & ((key & 1) <= (row & 1))
            scores = jnp.where(allowed, scores, masked_fill)
            new, factor, summed, weights = weigh(scores, level[span, 0:1])
            mixed[span, :] = earlier[span, :].astype(f32) * factor + dot(weights, newest[:, :LAT])
            highest[span, :] = jnp.broadcast_to(new, (512, 128))
            total[span, :] = jnp.broadcast_to(factor + summed, (512, 128))

        whole_loop(2, begin, 2)

        def add_prompt(prompt):
            @pl.when(owner[prompt] == group)
            def _():
                @pl.when(fitting)
                def _():
                    hot_rows(hot, columns, prompt, 1)

                    def open_part(part):
                        span = aligned(prompt * 2 + part, 512)
                        found = near[span, :].astype(f32) + dot(hot[aligned(part, 512), :], others[...])
                        put_keys(keys, span, found, factors[aligned(part, 512), :])

                    whole_loop(2, open_part, 2)

                @pl.when(jnp.logical_not(fitting))
                def _():
                    copy_in(spare.at[pl.ds(prompt * 1024, 1024)], keys.at[pl.ds(prompt * 1024, 1024)], sem)

                def add_part(piece):
                    span = aligned(piece, 512)
                    some = keys[aligned(prompt, 1024), :]
                    new, factor, summed, weights = weigh(dot_nt(query[span, :], some) * base_two, highest[span, 0:1])
                    mixed[span, :] = mixed[span, :] * factor + dot(weights, some[:, :LAT])
                    highest[span, :] = jnp.broadcast_to(new, (512, 128))
                    total[span, :] = total[span, :] * factor + summed

                whole_loop(2, add_part, 2)

        whole_loop(2, add_prompt)

        def tp_rows(tp):
            for head in range(8):
                rows = pl.ds(pl.multiple_of(tp * 128 + head * 16, 16), 16)
                some = mixed[rows, :] * (1.0 / total[rows, 0:1])
                out[aligned(tp, 16), head * LAT : (head + 1) * LAT] = some.astype(bf16)

        whole_loop(8, tp_rows, 2)


def prefill_kernel(place, fits, near, others, columns, factors, query, spare, out, keys, hot, mixed, pairs, sem):
    group = place[0] * 8 + place[1]
    fitting = fits[0, 0] == 1

    @pl.when(place[4] == 0)
    def _():
        def add_prompt(prompt):
            @pl.when(fitting)
            def _():
                hot_rows(hot, columns, prompt, 1)

                def open_part(part):
                    span = aligned(part, 512)
                    found = near[aligned(prompt * 2 + part, 512), :].astype(f32) + dot(hot[span, :], others[...])
                    put_keys(keys, span, found, factors[span, :])

                whole_loop(2, open_part, 2)

            @pl.when(jnp.logical_not(fitting))
            def _():
                copy_in(spare.at[pl.ds(prompt * 1024, 1024)], keys, sem)

            span = aligned(prompt, 512)
            some = keys[...]
            scores = dot_nt(query[span, :], some) * base_two
            last = (iota((512, 1), 0) & 63) + group * 64
            scores = jnp.where(iota(scores.shape, 1) <= last, scores, masked_fill)
            _, _, summed, weights = weigh(scores, jnp.full((512, 1), masked_fill, f32))
            added = dot(weights, some[:, :LAT]) * (1.0 / summed)
            for column in range(4):
                mixed[column, span, :] = added[:, column * 128 : (column + 1) * 128]

        whole_loop(2, add_prompt)

        def head_rows(head):
            for column in range(4):
                for prompt in range(2):
                    start = pl.multiple_of(prompt * 512 + head * 64, 64)
                    pairs[column, pl.ds(prompt, 64, stride=2), :] = mixed[column, pl.ds(start, 64), :]
                out[:, pl.ds(pl.multiple_of(head * LAT + column * 128, 128), 128)] = pairs[column].astype(bf16)

        whole_loop(8, head_rows, 2)


def join_kernel(place, turned, prefilled, out, sems):
    def bring(source):
        copies = []
        for part in range(4):
            span = pl.ds(part * 32, 32)
            copies.append(pltpu.make_async_copy(source.at[span], out.at[span], sems.at[part]))
        for copy in copies:
            copy.start()
        for copy in copies:
            copy.wait()

    @pl.when(place[4] == 0)
    def _():
        bring(prefilled)

    @pl.when(place[4] == 1)
    def _():
        bring(turned)


def rope_factors(position):
    frequency = np.float32(rope_base) ** (-np.arange(32, dtype=np.float32) / np.float32(32))
    angles = position[:, None] * frequency[None, :]
    if isinstance(position, np.ndarray):
        angles = angles.astype(np.float32).astype(np.float64)
        cosine, sine = np.cos(angles), np.sin(angles)
        return np.concatenate([cosine, cosine, -sine, sine], axis=-1).astype(np.float32)
    cosine, sine = jnp.cos(angles), jnp.sin(angles)
    return jnp.concatenate([cosine, cosine, -sine, sine], axis=-1)


def finish_keys(latent, latent_gain, position):
    plain = latent[:, :LAT]
    scaled = plain * lax.rsqrt(jnp.mean(plain * plain, axis=-1, keepdims=True) + norm_eps) * latent_gain
    factors = rope_factors(position.astype(f32))
    rotary = latent[:, LAT:]
    swapped = jnp.concatenate([rotary[:, 32:], rotary[:, :32]], axis=-1)
    turned = rotary * factors[:, :64] + swapped * factors[:, 64:]
    return jnp.concatenate([scaled, turned], axis=-1).astype(bf16)


def dense_keys(token_ids, place, embed_table, down, latent_gain, cache_length):
    group = place[0] * 8 + place[1]
    tp_index = place[2] * 2 + place[3]
    every = lax.all_to_all(jnp.broadcast_to(token_ids, (32, 128)).reshape(32, 1, 128), HOLDERS, 0, 0, tiled=True)
    local_row = every.reshape(-1) - (group * 2 + place[4]) * 2048
    inside = (local_row >= 0) & (local_row < 2048)
    picked = jnp.take(embed_table, jnp.clip(local_row, 0, 2047), axis=0)
    picked = jnp.where(inside[:, None], picked, jnp.zeros_like(picked)).reshape(32, 128, 896)
    embedded = jnp.sum(lax.all_to_all(picked, HOLDERS, 0, 0, tiled=True).astype(f32), axis=0).astype(bf16)
    partial = dot_nt(embedded, down)
    spread = jnp.broadcast_to(partial[None], (8, 128, KVW))
    latent = jnp.sum(lax.all_to_all(spread, TP, 0, 0, tiled=True), axis=0)
    index = jnp.arange(128, dtype=jnp.int32)
    mine = finish_keys(latent, latent_gain, group * 64 + index // 2)
    spread = jnp.broadcast_to(mine[None], (32, 128, KVW))
    prompts = lax.all_to_all(spread, HOLDERS, 0, 0, tiled=True).reshape(16, 2, 64, 2, KVW)[:, 0]
    prompts = jnp.transpose(prompts, (2, 0, 1, 3)).reshape(KEYS, KVW)
    own = lax.dynamic_slice_in_dim(latent, tp_index * 16, 16, 0)
    fresh = finish_keys(own, latent_gain, (cache_length[:, None] + jnp.arange(2, dtype=jnp.int32)[None]).reshape(-1))
    return prompts, jnp.concatenate([fresh, jnp.zeros((112, KVW), bf16)], axis=0)


def params(mebibytes):
    return pltpu.CompilerParams(vmem_limit_bytes=mebibytes * 1024 * 1024)


def shards(
    token_ids,
    embed_table,
    latent_down,
    latent_gain,
    prefill_query,
    decode_query,
    latent_cache,
    cache_length,
    prompt_owner,
):
    place = jnp.stack([lax.axis_index(name) for name in ("ylo", "z", "x", "core", "role")]).astype(jnp.int32)
    down = jnp.transpose(latent_down)
    whole = pl.BlockSpec(memory_space=VMEM)
    scalars = pl.BlockSpec(memory_space=SMEM)
    anywhere = pl.BlockSpec(memory_space=pl.ANY)
    shaped = jax.ShapeDtypeStruct

    spread = pl.pallas_call(
        spread_kernel,
        out_shape=shaped((32, 1, 128), jnp.int32),
        in_specs=[whole],
        out_specs=whole,
        compiler_params=params(4),
        name="spread_ids",
    )(token_ids)
    every = lax.all_to_all(spread, HOLDERS, 0, 0, tiled=True).reshape(32, 128)

    earlier, level = pl.pallas_call(
        cache_kernel,
        grid_spec=pltpu.PrefetchScalarGridSpec(
            num_scalar_prefetch=1,
            grid=(8,),
            in_specs=[
                pl.BlockSpec((1, 128, KVW), lambda row, lengths: (row, 0, 0)),
                pl.BlockSpec((1, KVW, 512), lambda row, lengths: (row, 0, 0)),
            ],
            out_specs=[
                pl.BlockSpec((128, LAT), lambda row, lengths: (row, 0)),
                pl.BlockSpec((128, 128), lambda row, lengths: (row, 0)),
            ],
        ),
        out_shape=(shaped((1024, LAT), bf16), shaped((1024, 128), f32)),
        compiler_params=params(56),
        cost_estimate=pl.CostEstimate(flops=12 * 10**8, bytes_accessed=7 * 10**6, transcendentals=524288),
        name="cache_rows",
    )(cache_length, decode_query.reshape(8, 128, KVW), jnp.swapaxes(latent_cache, 1, 2))
    every, earlier, level = lax.optimization_barrier((every, earlier, level))

    partial = pl.pallas_call(
        select_kernel,
        out_shape=shaped((8, SLOTS, KVW), f32),
        in_specs=[scalars, whole, anywhere, anywhere],
        out_specs=whole,
        scratch_shapes=[
            VMEM((16, 4096), bf16),
            VMEM((128, 4096), bf16),
            VMEM((8 * SLOTS, 2048), bf16),
            VMEM((2048, 896), bf16),
            VMEM((KVW, 896), bf16),
            pltpu.SemaphoreType.DMA((2,)),
        ],
        compiler_params=params(16),
        cost_estimate=pl.CostEstimate(flops=3 * 10**9, bytes_accessed=5 * 10**6, transcendentals=0),
        name="select_rows",
    )(place, every, embed_table, down)
    parts = lax.all_to_all(partial, TP, 0, 0, tiled=True)

    sheet = pl.pallas_call(
        rank_kernel,
        out_shape=shaped((104, 128), jnp.int32),
        in_specs=[whole],
        out_specs=whole,
        scratch_shapes=[VMEM((512, 4096), bf16), VMEM((128, 4096), bf16)],
        compiler_params=params(18),
        cost_estimate=pl.CostEstimate(flops=2 * 10**9, bytes_accessed=10**6, transcendentals=0),
        name="rank_rows",
    )(every)
    columns, kept, fits = pl.pallas_call(
        place_kernel,
        out_shape=(shaped((128, 128), jnp.int32), shaped((8, 128), f32), shaped((1, 1), jnp.int32)),
        in_specs=[scalars, whole],
        out_specs=(whole, whole, scalars),
        scratch_shapes=[
            VMEM((128, 19 * 128), bf16),
            VMEM((128, 19 * 128), bf16),
            VMEM((16, 2048), bf16),
            VMEM((64, 2048), bf16),
            VMEM((128, 128), f32),
        ],
        compiler_params=params(12),
        cost_estimate=pl.CostEstimate(flops=10**9, bytes_accessed=10**6, transcendentals=0),
        name="place_rows",
    )(place, sheet)
    parts, columns, kept, fits = lax.optimization_barrier((parts, columns, kept, fits))
    spare, spare_new = lax.cond(
        fits[0, 0] == 1,
        lambda *unused: tuple(
            pl.pallas_call(
                empty_kernel,
                out_shape=[shaped((KEYS, KVW), bf16), shaped((128, KVW), bf16)],
                out_specs=[anywhere] * 2,
                name="no_keys",
            )()
        ),
        dense_keys,
        token_ids,
        place,
        embed_table,
        down,
        latent_gain,
        cache_length,
    )
    parts, spare, spare_new, decode_rows, earlier, level = lax.optimization_barrier(
        (parts, spare, spare_new, decode_query, earlier, level)
    )
    sent = pl.pallas_call(
        finish_kernel,
        out_shape=shaped((8, SLOTS, WIDE), bf16),
        in_specs=[whole, whole],
        out_specs=whole,
        compiler_params=params(8),
        name="finish_rows",
    )(parts, latent_gain.reshape(1, LAT))
    arrived = lax.all_to_all(sent, "z", 0, 0, tiled=True)


    def by_head(rows):
        return jnp.transpose(rows.reshape(16, 64, -1), (1, 0, 2)).reshape(1024, -1)

    row_query, earlier, level = by_head(decode_rows), by_head(earlier), by_head(level)
    new_position = (cache_length[:, None] + jnp.arange(2, dtype=jnp.int32)[None]).reshape(-1)
    new_factors = jnp.pad(rope_factors(new_position.astype(f32)), ((0, 112), (0, 0)))
    arrived, prompt_rows, new_factors, row_query, earlier, level = lax.optimization_barrier(
        (arrived, prefill_query, new_factors, row_query, earlier, level)
    )
    handed = pl.pallas_call(
        keep_kernel,
        out_shape=shaped((16, KEPT, WIDE), bf16),
        in_specs=[whole, whole],
        out_specs=whole,
        compiler_params=params(8),
        name="keep_rows",
    )(kept, arrived.reshape(8 * SLOTS, WIDE))
    slots = lax.all_to_all(handed, PLANE, 0, 0, tiled=True).reshape(SIDE, WIDE)

    prompt_query = jnp.transpose(prompt_rows.reshape(64, 2, 8, KVW), (1, 2, 0, 3)).reshape(1024, KVW)
    slots, prompt_query = lax.optimization_barrier((slots, prompt_query))
    others = lax.ppermute(slots, "core", [(0, 1), (1, 0)])

    near = pl.pallas_call(
        near_kernel,
        out_shape=shaped((KEYS + 128, WIDE), bf16),
        in_specs=[scalars, scalars, whole, whole],
        out_specs=whole,
        scratch_shapes=[VMEM((1024, SIDE), bf16)],
        compiler_params=params(12),
        cost_estimate=pl.CostEstimate(flops=2 * 10**9, bytes_accessed=10**6, transcendentals=0),
        name="near_keys",
    )(place, prompt_owner, slots, columns)
    factors = jnp.asarray(rope_factors(np.arange(1024, dtype=np.float32)))
    decoded = pl.pallas_call(
        decode_kernel,
        out_shape=shaped((128, 4096), bf16),
        in_specs=[scalars] * 3 + [whole] * 8 + [anywhere] * 2,
        out_specs=whole,
        scratch_shapes=[
            VMEM((KEYS + 128, KVW), bf16),
            VMEM((1024, SIDE), bf16),
            VMEM((1024, 128), f32),
            VMEM((1024, 128), f32),
            VMEM((1024, LAT), f32),
            pltpu.SemaphoreType.DMA,
        ],
        compiler_params=params(20),
        cost_estimate=pl.CostEstimate(flops=5 * 10**9, bytes_accessed=7 * 10**6, transcendentals=10**6),
        name="decode_rows",
    )(
        place, prompt_owner, fits, near, others, columns, factors, new_factors, row_query, earlier, level, spare, spare_new
    )
    turned = lax.all_to_all(decoded.reshape(8, 16, 4096), TP, 0, 0, tiled=True).reshape(128, 4096)
    prefilled = pl.pallas_call(
        prefill_kernel,
        out_shape=shaped((128, 4096), bf16),
        in_specs=[scalars] * 2 + [whole] * 5 + [anywhere],
        out_specs=whole,
        scratch_shapes=[
            VMEM((1024, KVW), bf16),
            VMEM((1024, SIDE), bf16),
            VMEM((4, 1024, 128), f32),
            VMEM((4, 128, 128), f32),
            pltpu.SemaphoreType.DMA,
        ],
        compiler_params=params(20),
        cost_estimate=pl.CostEstimate(flops=7 * 10**9, bytes_accessed=7 * 10**6, transcendentals=10**6),
        name="prefill_rows",
    )(place, fits, near, others, columns, factors, prompt_query, spare)
    out = pl.pallas_call(
        join_kernel,
        out_shape=shaped((128, 4096), bf16),
        in_specs=[scalars] + [anywhere] * 2,
        out_specs=anywhere,
        scratch_shapes=[pltpu.SemaphoreType.DMA((4,))],
        compiler_params=params(4),
        name="join_rows",
    )(place, turned, prefilled)
    return out[None]


def solution(mesh):
    fine_mesh = Mesh(mesh.devices.reshape(2, 8, 4, 2, 2), ("ylo", "z", "x", "core", "role"))
    ctx, tp = ("ylo", "z"), ("x", "core")
    in_specs = (
        P("role", ctx),
        P(ctx + ("role",), tp),
        P(tp, None),
        P(),
        P(ctx, tp, None),
        P(ctx + tp, None, None, None),
        P(ctx + tp, None, None),
        P(ctx + tp),
        P(),
    )
    out_specs = P("role", ctx, tp)
    return jax.shard_map(shards, mesh=fine_mesh, in_specs=in_specs, out_specs=out_specs, check_vma=False)
```

```python
import jax
import jax.numpy as jnp
import numpy as np
from jax import lax
from jax.experimental import pallas as pl
from jax.experimental.pallas import tpu as pltpu
from jax.sharding import Mesh
from jax.sharding import PartitionSpec as P

LAT = 512
KVW = 576
STEPS = 2
WIDE = 640
SLOTS = 16
KEPT = 48
SIDE = 16 * KEPT
KEYS = 2048

score_scale = 0.07216878364870322
base_two = score_scale * 1.4426950408889634
masked_fill = -1e30
norm_eps = 1e-06
rope_base = 10000.0
bf16 = jnp.bfloat16
f32 = jnp.float32
SMEM = pltpu.SMEM
VMEM = pltpu.VMEM

HOLDERS = ("ylo", "z", "role")
PLANE = ("ylo", "role", "x")
TP = ("x", "core")


def iota(shape, axis):
    return lax.broadcasted_iota(jnp.int32, shape, axis)


def ones_where(flags):
    return jnp.where(flags, 1.0, 0.0).astype(bf16)


def dot(left, right):
    return lax.dot_general(left, right, (((1,), (0,)), ((), ())), preferred_element_type=f32)


def dot_nt(left, right):
    return lax.dot_general(left, right, (((1,), (1,)), ((), ())), preferred_element_type=f32)


def whole_loop(count, body, unroll=1):
    def step(index, carry):
        body(index)
        return carry

    lax.fori_loop(0, count, step, 0, unroll=unroll)


def aligned(index, size):
    return pl.ds(pl.multiple_of(index * size, size), size)


def spread_kernel(ids, out):
    out[...] = jnp.broadcast_to(ids[...].reshape(1, 1, 128), out.shape)


def select_kernel(place, ids, table, down, partial, hots, lows, chosen, table_here, down_here, sems):
    holder = (place[0] * 8 + place[1]) * 2 + place[4]
    table_copy = pltpu.make_async_copy(table, table_here, sems.at[0])
    down_copy = pltpu.make_async_copy(down, down_here, sems.at[1])
    table_copy.start()
    down_copy.start()

    def mark(line):
        tokens = ids[pl.ds(line, 1), :]
        span = aligned((line & 1) * 16 + (line >> 1), 128)
        hots[:, span] = ones_where(iota((16, 128), 0) == (tokens >> 7) - holder * 16)
        lows[:, span] = ones_where(iota((128, 128), 0) == (tokens & 127))

    whole_loop(32, mark, 8)
    in_prompt = dot_nt(hots[:, :KEYS], lows[:, :KEYS]) > 0.5
    alone = (dot_nt(hots[:, KEYS:], lows[:, KEYS:]) > 0.5) & jnp.logical_not(in_prompt)
    upper = ones_where(iota((128, 128), 0) < iota((128, 128), 1))
    all_ones = jnp.ones((128, 128), bf16)
    row = iota((8 * SLOTS, 128), 0)
    wanted = ((row & 15) * 8 + (((row >> 4) - holder) & 7)).astype(f32)
    before = jnp.zeros((1, 128), f32)
    ranks = []
    for present in (in_prompt, alone):
        flags = ones_where(present)
        within = dot(flags, upper)
        totals = dot(flags, all_ones)
        lines = []
        for step in range(16):
            lines.append(within[step : step + 1, :] + before)
            before = before + totals[step : step + 1, :]
        ranks.append(lines)
    for step in range(16):
        rank = jnp.where(alone[step : step + 1, :], ranks[1][step], -1.0)
        rank = jnp.where(in_prompt[step : step + 1, :], ranks[0][step], rank)
        chosen[:, step * 128 : (step + 1) * 128] = ones_where(wanted == rank)
    table_copy.wait()
    rows = dot(chosen[...], table_here[...]).astype(bf16)
    down_copy.wait()
    partial[...] = dot_nt(rows, down_here[...]).reshape(partial.shape)


def rank_kernel(ids, sheet, highs, lows):
    square = (128, 128)
    lane = iota((8, 128), 1)
    sheet[0:16, :] = ids[pl.ds(0, 16, stride=2), :]
    sheet[16:32, :] = ids[pl.ds(1, 16, stride=2), :]
    target = iota(square, 1)
    mover = ones_where(iota(square, 0) == jnp.where(target < 64, 2 * target, 2 * target - 127))
    plain = sheet[0:16, :]
    decode_tokens = sheet[16:32, :]
    coarse = (plain >> 8).astype(f32).astype(bf16)
    fine = (plain & 255).astype(f32).astype(bf16)
    moved = dot(coarse, mover) * 256.0 + dot(fine, mover)
    sheet[0:16, :] = moved.astype(jnp.int32)
    even = sheet[pl.ds(0, 8, stride=2), :]
    odd = sheet[pl.ds(1, 8, stride=2), :]
    first = jnp.where(lane < 64, even, pltpu.roll(odd, 64, 1))
    second = jnp.where(lane < 64, pltpu.roll(even, 64, 1), odd)
    tokens = jnp.concatenate([first, second, decode_tokens], axis=0)
    sheet[0:32, :] = tokens

    def mark(block):
        line = sheet[pl.ds(block, 1), :]
        span = aligned(block, 128)
        highs[:, span] = ones_where(iota((512, 128), 0) == (line >> 7))
        lows[:, span] = ones_where(iota(square, 0) == (line & 127))

    whole_loop(32, mark, 8)
    in_prompt = dot_nt(lows[:, :KEYS], highs[:, :KEYS]) > 0.5
    alone = (dot_nt(lows[:, KEYS:], highs[:, KEYS:]) > 0.5) & jnp.logical_not(in_prompt)
    below = ones_where(iota(square, 1) < iota(square, 0))
    all_ones = jnp.ones(square, bf16)
    wide = (512, 512)
    same = (iota(wide, 0) >> 4) == (iota(wide, 1) >> 4)
    in_holder = ones_where(same & (iota(wide, 0) < iota(wide, 1)))
    prompt_flags = ones_where(in_prompt)
    alone_flags = ones_where(alone)
    prompt_columns = dot(all_ones, prompt_flags).astype(bf16)
    alone_columns = dot(all_ones, alone_flags).astype(bf16)
    prompt_rank = dot(below, prompt_flags) + dot(prompt_columns, in_holder)
    alone_rank = (
        dot(below, alone_flags) + dot(alone_columns, in_holder) + dot(prompt_columns, ones_where(same))
    )
    rank = jnp.where(in_prompt, prompt_rank, jnp.where(alone, alone_rank, 0.0))
    top_rank = jnp.max(jnp.max(rank, axis=0, keepdims=True), axis=1, keepdims=True).astype(jnp.int32)
    coded = (jnp.minimum(rank, 127.0) + jnp.where(in_prompt, 128.0, 0.0)).astype(bf16)
    pieces = []
    for chunk in range(4):
        span = slice(chunk * 1024, (chunk + 1) * 1024)
        looked = dot(coded, highs[:, span]) * lows[:, span].astype(f32)
        line = jnp.sum(looked, axis=0, keepdims=True)
        for part in range(8):
            pieces.append(line[:, part * 128 : (part + 1) * 128])
    value = jnp.concatenate(pieces, axis=0).astype(jnp.int32)
    ranks = value & 127
    holder = tokens >> 11
    tp_of = (ranks + holder) & 7
    quad = tp_of * 16 + (ranks >> 3)
    sheet[0:32, :] = quad
    sheet[32:64, :] = holder
    sheet[64:96, :] = jnp.where(value >= 128, -1, tp_of)
    sheet[96:104, :] = jnp.broadcast_to(top_rank, (8, 128))


def place_kernel(place, sheet, columns, kept, fits, quads, holders, hot_tp, hot_pool, sheet_b):
    ylo, zed, ex, core, section = place[0], place[1], place[2], place[3], place[4]
    square = (128, 128)

    def spot(block, source):
        span = aligned(block, 128)
        quads[:, span] = ones_where(iota(square, 0) == sheet[pl.ds(source, 1), :])
        holders[:, span] = ones_where(iota(square, 0) == sheet[pl.ds(source + 32, 1), :])

    whole_loop(16, lambda block: spot(block, block), 8)
    for part in range(2):
        spot(16 + part, 16 + part * 8 + zed)
    own = 16 + ylo * 8 + zed
    spot(18, own)
    up, down = iota(square, 0), iota(square, 1)
    same_tp = (up >> 4) == (down >> 4)
    same_pool = ((up >> 4) == (down >> 4)) & ((up & 1) == (down & 1))
    tp_ones = ones_where(same_tp)
    pool = ones_where(same_pool)
    before = ones_where(same_pool & (up < down))
    in_tp = ones_where(same_tp & (down < up))
    held = dot_nt(quads[:, :KEYS], holders[:, :KEYS]) > 0.5
    flags = ones_where(held)
    sums = dot(tp_ones, flags).astype(bf16)
    prompt_position = dot(in_tp, flags) + dot(sums, before)
    prompt_count = dot(sums, pool)
    positions = []
    for part in range(2):
        span = slice(KEYS + part * 128, KEYS + (part + 1) * 128)
        added = (dot_nt(quads[:, span], holders[:, span]) > 0.5) & jnp.logical_not(held)
        added_flags = ones_where(added)
        added_sums = dot(tp_ones, added_flags).astype(bf16)
        spots = dot(in_tp, added_flags) + dot(added_sums, before) + prompt_count
        spots = jnp.where(held, prompt_position, jnp.where(added, spots, 255.0))
        positions.append(jnp.minimum(spots, 255.0))
    position = jnp.where(ylo == 0, positions[0], positions[1])

    def pick(block):
        span = aligned(block, 128)
        hot_tp[:, span] = ones_where(iota((16, 128), 0) == sheet[pl.ds(block + 80, 1), :])
        line = sheet[pl.ds(block + 48, 1), :]
        line = ((line >> 4) * 2 + (line & 1)) + 4 * block
        hot_pool[:, span] = ones_where(iota((64, 128), 0) == line)

    whole_loop(16, pick, 8)
    gather_tp = ones_where(iota((16, 128), 0) == (iota((16, 128), 1) >> 4))
    base = dot(gather_tp, flags).astype(bf16)
    holder, column = iota((128, 64), 0), iota((128, 64), 1)
    pooled = ones_where((holder < 32) & (((holder >> 4) * 2 + (holder & 1)) == (column & 3)))
    needed = dot_nt(hot_tp[...], hot_pool[...]) + dot(base, pooled)
    needed = jnp.max(jnp.max(needed, axis=0, keepdims=True), axis=1, keepdims=True)
    enough = (sheet[96:97, 0:1] < 8 * SLOTS) & (needed <= float(KEPT))
    fits[0, 0] = jnp.max(jnp.where(enough, 1, 0))

    looked = dot(position.astype(bf16), holders[...]) * quads[...].astype(f32)
    line = jnp.sum(looked, axis=0, keepdims=True)
    found = [line[:, block * 128 : (block + 1) * 128] for block in range(19)]
    found = jnp.concatenate(found + [jnp.zeros((5, 128), f32)], axis=0)
    blank = jnp.zeros((5, 128), jnp.int32)
    quad_rows = jnp.concatenate([sheet[0:16, :], blank[:2], sheet[pl.ds(own, 1), :], blank], axis=0)
    holder_rows = jnp.concatenate([sheet[32:48, :], blank[:2], sheet[pl.ds(own + 32, 1), :], blank], axis=0)
    tp_rows = quad_rows >> 4
    source = ((holder_rows >> 4) * 2 + (holder_rows & 1)) * 4 + (tp_rows >> 1)
    side = jnp.where((tp_rows & 1) == core, 0, SIDE)
    final = found + (source * KEPT + side).astype(f32)
    tp_index = ex * 2 + core
    turned = pltpu.roll(final, (128 - tp_index * 16) % 128, 1)
    turned = jnp.where(iota((24, 128), 1) < 16, turned, -1.0)
    final = jnp.where(iota((24, 128), 0) == 18, turned, final)
    final = jnp.concatenate([final, jnp.zeros((104, 128), f32)], axis=0)
    columns[...] = jnp.transpose(final).astype(jnp.int32)
    few = (16, 128)
    for part in range(2):
        sheet_b[...] = positions[part]
        mine = sheet_b[pl.ds(pl.multiple_of(tp_index * 16, 16), 16), :].astype(bf16)
        spread = dot(mine, ones_where(up == (ylo * 8 + ((down >> 4) ^ zed)) * 2 + section))
        spread = jnp.where((iota(few, 1) & 15) == iota(few, 0), spread, 0.0)
        kept[part : part + 1, :] = jnp.sum(spread, axis=0, keepdims=True)


def finish_kernel(parts, gain, sent):
    latent = parts[0]
    for tp in range(1, parts.shape[0]):
        latent = latent + parts[tp]
    plain = latent[:, :LAT]
    scaled = plain * lax.rsqrt(jnp.mean(plain * plain, axis=-1, keepdims=True) + norm_eps) * gain[...]
    rotary = latent[:, LAT:]
    coarse = rotary.astype(bf16)
    fine = (rotary - coarse.astype(f32)).astype(bf16)
    sent[...] = jnp.concatenate([scaled.astype(bf16), coarse, fine], axis=-1)


def stack_kernel(first, second, out):
    half = first.shape[0]
    out[:half, :] = first[...]
    out[half:, :] = second[...]


def keep_kernel(kept, first, second, sent):
    rows = jnp.concatenate([first[...], second[...]], axis=0)
    for ylo in range(2):
        chosen = iota((KEPT, 128), 0).astype(f32) == kept[ylo : ylo + 1, :]
        row = dot(ones_where(chosen), rows).astype(bf16)
        for peer in range(8):
            sent[ylo * 8 + peer] = row


def cache_kernel(lengths, query, cache, out, level):
    length = lengths[pl.program_id(0)]
    scores = dot(query[0], cache[0]) * base_two
    scores = jnp.where(iota(scores.shape, 1) < length, scores, masked_fill)
    highest = jnp.max(scores, axis=-1, keepdims=True)
    weights = jnp.exp2(scores - highest)
    total = jnp.sum(weights, axis=-1, keepdims=True)
    out[...] = (dot_nt(weights.astype(bf16), cache[0, :LAT, :]) * (1.0 / total)).astype(bf16)
    level[...] = jnp.broadcast_to(highest + jnp.log2(total), level.shape)


def hot_rows(hot, columns, prompt, side):
    turned = pltpu.roll(columns[...], (128 - prompt * 8) % 128, 1) - side * SIDE
    for block in range(8):
        hot[block * 128 : (block + 1) * 128, :] = ones_where(iota((128, SIDE), 1) == turned[:, block : block + 1])


def empty_kernel(*refs):
    pass


def fresh_hot(columns, side):
    return ones_where(iota((128, SIDE), 1) == columns[:, 18:19] - side * SIDE)


def put_keys(keys, span, found, factor):
    turning = found[:, LAT:]
    turning = turning + pltpu.roll(turning, 64, 1)
    turned = turning * factor + pltpu.roll(turning, 32, 1) * pltpu.roll(factor, 64, 1)
    keys[span, :LAT] = found[:, :LAT].astype(bf16)
    keys[span, LAT:] = turned[:, : KVW - LAT].astype(bf16)


def copy_in(source, target, sem):
    copy = pltpu.make_async_copy(source, target, sem)
    copy.start()
    copy.wait()


def weigh(scores, old):
    new = jnp.maximum(old, jnp.max(scores, axis=-1, keepdims=True))
    weights = jnp.exp2(scores - new)
    return new, jnp.exp2(old - new), jnp.sum(weights, axis=-1, keepdims=True), weights.astype(bf16)


def near_kernel(place, owner, slots, columns, near, hot):
    group = place[0] * 8 + place[1]

    @pl.when(place[4] == 1)
    def _():
        near[KEYS : KEYS + 128, :] = dot(fresh_hot(columns, 0), slots[...]).astype(bf16)

    def open_prompt(prompt):
        @pl.when((place[4] == 0) | (owner[prompt] == group))
        def _():
            hot_rows(hot, columns, prompt, 0)

            def open_part(part):
                near[aligned(prompt * 2 + part, 512), :] = dot(hot[aligned(part, 512), :], slots[...]).astype(bf16)

            whole_loop(2, open_part, 2)

    whole_loop(2, open_prompt)


def decode_kernel(
    place, owner, fits, near, others, columns, factors, new_factors, query, earlier, level, spare, spare_new,
    out, out_here, keys, hot, highest, total, mixed, sem, out_sems
):
    group = place[0] * 8 + place[1]
    fitting = fits[0, 0] == 1

    @pl.when(place[4] == 1)
    def _():
        @pl.when(fitting)
        def _():
            span = slice(KEYS, KEYS + 128)
            found = near[span, :].astype(f32) + dot(fresh_hot(columns, 1), others[...])
            put_keys(keys, span, found, new_factors[...])

        @pl.when(jnp.logical_not(fitting))
        def _():
            copy_in(spare_new, keys.at[pl.ds(KEYS, 128)], sem)

        newest = keys[KEYS : KEYS + 128, :]

        def begin(piece):
            span = aligned(piece, 512)
            scores = dot_nt(query[span, :], newest) * base_two
            key = iota(scores.shape, 1)
            row = iota(scores.shape, 0) & 15
            allowed = ((key >> 1) == (row >> 1)) & ((key & 1) <= (row & 1))
            scores = jnp.where(allowed, scores, masked_fill)
            new, factor, summed, weights = weigh(scores, level[span, 0:1])
            mixed[span, :] = earlier[span, :].astype(f32) * factor + dot(weights, newest[:, :LAT])
            highest[span, :] = jnp.broadcast_to(new, (512, 128))
            total[span, :] = jnp.broadcast_to(factor + summed, (512, 128))

        whole_loop(2, begin, 2)

        def add_prompt(prompt):
            @pl.when(owner[prompt] == group)
            def _():
                @pl.when(fitting)
                def _():
                    hot_rows(hot, columns, prompt, 1)

                    def open_part(part):
                        span = aligned(prompt * 2 + part, 512)
                        found = near[span, :].astype(f32) + dot(hot[aligned(part, 512), :], others[...])
                        put_keys(keys, span, found, factors[aligned(part, 512), :])

                    whole_loop(2, open_part, 2)

                @pl.when(jnp.logical_not(fitting))
                def _():
                    copy_in(spare.at[pl.ds(prompt * 1024, 1024)], keys.at[pl.ds(prompt * 1024, 1024)], sem)

                def add_part(piece):
                    span = aligned(piece, 512)
                    some = keys[aligned(prompt, 1024), :]
                    new, factor, summed, weights = weigh(dot_nt(query[span, :], some) * base_two, highest[span, 0:1])
                    mixed[span, :] = mixed[span, :] * factor + dot(weights, some[:, :LAT])
                    highest[span, :] = jnp.broadcast_to(new, (512, 128))
                    total[span, :] = total[span, :] * factor + summed

                whole_loop(2, add_part, 2)

        whole_loop(2, add_prompt)

        def out_copy(tp):
            rows = aligned(tp, 16)
            return pltpu.make_async_copy(out_here.at[rows], out.at[rows], out_sems.at[tp])

        def tp_rows(tp):
            for head in range(8):
                rows = pl.ds(pl.multiple_of(tp * 128 + head * 16, 16), 16)
                some = mixed[rows, :] * (1.0 / total[rows, 0:1])
                out_here[aligned(tp, 16), head * LAT : (head + 1) * LAT] = some.astype(bf16)
            out_copy(tp).start()

        whole_loop(8, tp_rows, 2)
        whole_loop(8, lambda tp: out_copy(tp).wait())


def prefill_kernel(place, fits, near, others, columns, factors, query, spare, out, keys, hot, mixed, pairs, sem):
    group = place[0] * 8 + place[1]
    fitting = fits[0, 0] == 1

    @pl.when(place[4] == 0)
    def _():
        def add_prompt(prompt):
            @pl.when(fitting)
            def _():
                hot_rows(hot, columns, prompt, 1)

                def open_part(part):
                    span = aligned(part, 512)
                    found = near[aligned(prompt * 2 + part, 512), :].astype(f32) + dot(hot[span, :], others[...])
                    put_keys(keys, span, found, factors[span, :])

                whole_loop(2, open_part, 2)

            @pl.when(jnp.logical_not(fitting))
            def _():
                copy_in(spare.at[pl.ds(prompt * 1024, 1024)], keys, sem)

            span = aligned(prompt, 512)
            some = keys[...]
            scores = dot_nt(query[span, :], some) * base_two
            last = (iota((512, 1), 0) & 63) + group * 64
            scores = jnp.where(iota(scores.shape, 1) <= last, scores, masked_fill)
            _, _, summed, weights = weigh(scores, jnp.full((512, 1), masked_fill, f32))
            added = dot(weights, some[:, :LAT]) * (1.0 / summed)
            for column in range(4):
                mixed[column, span, :] = added[:, column * 128 : (column + 1) * 128]

        whole_loop(2, add_prompt)

        def head_rows(head):
            for column in range(4):
                for prompt in range(2):
                    start = pl.multiple_of(prompt * 512 + head * 64, 64)
                    pairs[column, pl.ds(prompt, 64, stride=2), :] = mixed[column, pl.ds(start, 64), :]
                out[:, pl.ds(pl.multiple_of(head * LAT + column * 128, 128), 128)] = pairs[column].astype(bf16)

        whole_loop(8, head_rows, 2)


def join_kernel(place, prefilled, turned, out, sems):
    @pl.when(place[4] == 1)
    def _():
        copies = []
        for part in range(4):
            span = pl.ds(part * 32, 32)
            copies.append(pltpu.make_async_copy(turned.at[span], out.at[span], sems.at[part]))
        for copy in copies:
            copy.start()
        for copy in copies:
            copy.wait()


def rope_factors(position):
    frequency = np.float32(rope_base) ** (-np.arange(32, dtype=np.float32) / np.float32(32))
    angles = position[:, None] * frequency[None, :]
    if isinstance(position, np.ndarray):
        angles = angles.astype(np.float32).astype(np.float64)
        cosine, sine = np.cos(angles), np.sin(angles)
        return np.concatenate([cosine, cosine, -sine, sine], axis=-1).astype(np.float32)
    cosine, sine = jnp.cos(angles), jnp.sin(angles)
    return jnp.concatenate([cosine, cosine, -sine, sine], axis=-1)


def finish_keys(latent, latent_gain, position):
    plain = latent[:, :LAT]
    scaled = plain * lax.rsqrt(jnp.mean(plain * plain, axis=-1, keepdims=True) + norm_eps) * latent_gain
    factors = rope_factors(position.astype(f32))
    rotary = latent[:, LAT:]
    swapped = jnp.concatenate([rotary[:, 32:], rotary[:, :32]], axis=-1)
    turned = rotary * factors[:, :64] + swapped * factors[:, 64:]
    return jnp.concatenate([scaled, turned], axis=-1).astype(bf16)


def dense_keys(token_ids, place, embed_table, down, latent_gain, cache_length):
    group = place[0] * 8 + place[1]
    tp_index = place[2] * 2 + place[3]
    every = lax.all_to_all(jnp.broadcast_to(token_ids, (32, 128)).reshape(32, 1, 128), HOLDERS, 0, 0, tiled=True)
    local_row = every.reshape(-1) - (group * 2 + place[4]) * 2048
    inside = (local_row >= 0) & (local_row < 2048)
    picked = jnp.take(embed_table, jnp.clip(local_row, 0, 2047), axis=0)
    picked = jnp.where(inside[:, None], picked, jnp.zeros_like(picked)).reshape(32, 128, 896)
    embedded = jnp.sum(lax.all_to_all(picked, HOLDERS, 0, 0, tiled=True).astype(f32), axis=0).astype(bf16)
    partial = dot_nt(embedded, down)
    spread = jnp.broadcast_to(partial[None], (8, 128, KVW))
    latent = jnp.sum(lax.all_to_all(spread, TP, 0, 0, tiled=True), axis=0)
    index = jnp.arange(128, dtype=jnp.int32)
    mine = finish_keys(latent, latent_gain, group * 64 + index // 2)
    spread = jnp.broadcast_to(mine[None], (32, 128, KVW))
    prompts = lax.all_to_all(spread, HOLDERS, 0, 0, tiled=True).reshape(16, 2, 64, 2, KVW)[:, 0]
    prompts = jnp.transpose(prompts, (2, 0, 1, 3)).reshape(KEYS, KVW)
    own = lax.dynamic_slice_in_dim(latent, tp_index * 16, 16, 0)
    fresh = finish_keys(own, latent_gain, (cache_length[:, None] + jnp.arange(2, dtype=jnp.int32)[None]).reshape(-1))
    return prompts, jnp.concatenate([fresh, jnp.zeros((112, KVW), bf16)], axis=0)


def in_vmem(value):
    return pltpu.with_memory_space_constraint(value, VMEM)


def in_hbm(value):
    return pltpu.with_memory_space_constraint(value, pltpu.HBM)


def params(mebibytes):
    return pltpu.CompilerParams(vmem_limit_bytes=mebibytes * 1024 * 1024)


def shards(
    token_ids,
    embed_table,
    latent_down,
    latent_gain,
    prefill_query,
    decode_query,
    latent_cache,
    cache_length,
    prompt_owner,
):
    place = jnp.stack([lax.axis_index(name) for name in ("ylo", "z", "x", "core", "role")]).astype(jnp.int32)
    down = jnp.transpose(latent_down)
    whole = pl.BlockSpec(memory_space=VMEM)
    scalars = pl.BlockSpec(memory_space=SMEM)
    anywhere = pl.BlockSpec(memory_space=pl.ANY)
    shaped = jax.ShapeDtypeStruct

    spread = pl.pallas_call(
        spread_kernel,
        out_shape=shaped((32, 1, 128), jnp.int32),
        in_specs=[whole],
        out_specs=whole,
        compiler_params=params(4),
        name="spread_ids",
    )(token_ids)
    every = lax.all_to_all(spread, HOLDERS, 0, 0, tiled=True).reshape(32, 128)

    earlier, level = pl.pallas_call(
        cache_kernel,
        grid_spec=pltpu.PrefetchScalarGridSpec(
            num_scalar_prefetch=1,
            grid=(8,),
            in_specs=[
                pl.BlockSpec((1, 128, KVW), lambda row, lengths: (row, 0, 0)),
                pl.BlockSpec((1, KVW, 512), lambda row, lengths: (row, 0, 0)),
            ],
            out_specs=[
                pl.BlockSpec((128, LAT), lambda row, lengths: (row, 0)),
                pl.BlockSpec((128, 128), lambda row, lengths: (row, 0)),
            ],
        ),
        out_shape=(shaped((1024, LAT), bf16), shaped((1024, 128), f32)),
        compiler_params=params(12),
        cost_estimate=pl.CostEstimate(flops=12 * 10**8, bytes_accessed=7 * 10**6, transcendentals=524288),
        name="cache_rows",
    )(cache_length, in_hbm(decode_query.reshape(8, 128, KVW)), in_hbm(jnp.swapaxes(latent_cache, 1, 2)))
    every, earlier, level = lax.optimization_barrier((every, earlier, level))

    partial = pl.pallas_call(
        select_kernel,
        out_shape=shaped((8, SLOTS, KVW), f32),
        in_specs=[scalars, whole, anywhere, anywhere],
        out_specs=whole,
        scratch_shapes=[
            VMEM((16, 4096), bf16),
            VMEM((128, 4096), bf16),
            VMEM((8 * SLOTS, 2048), bf16),
            VMEM((2048, 896), bf16),
            VMEM((KVW, 896), bf16),
            pltpu.SemaphoreType.DMA((2,)),
        ],
        compiler_params=params(16),
        cost_estimate=pl.CostEstimate(flops=3 * 10**9, bytes_accessed=5 * 10**6, transcendentals=0),
        name="select_rows",
    )(place, every, in_hbm(embed_table), in_hbm(down))
    parts = lax.all_to_all(partial, TP, 0, 0, tiled=True)

    sheet = pl.pallas_call(
        rank_kernel,
        out_shape=shaped((104, 128), jnp.int32),
        in_specs=[whole],
        out_specs=whole,
        scratch_shapes=[VMEM((512, 4096), bf16), VMEM((128, 4096), bf16)],
        compiler_params=params(18),
        cost_estimate=pl.CostEstimate(flops=2 * 10**9, bytes_accessed=10**6, transcendentals=0),
        name="rank_rows",
    )(every)
    columns, kept, fits = pl.pallas_call(
        place_kernel,
        out_shape=(shaped((128, 128), jnp.int32), shaped((8, 128), f32), shaped((1, 1), jnp.int32)),
        in_specs=[scalars, whole],
        out_specs=(whole, whole, scalars),
        scratch_shapes=[
            VMEM((128, 19 * 128), bf16),
            VMEM((128, 19 * 128), bf16),
            VMEM((16, 2048), bf16),
            VMEM((64, 2048), bf16),
            VMEM((128, 128), f32),
        ],
        compiler_params=params(12),
        cost_estimate=pl.CostEstimate(flops=10**9, bytes_accessed=10**6, transcendentals=0),
        name="place_rows",
    )(place, sheet)
    parts, columns, kept, fits = lax.optimization_barrier((parts, columns, kept, fits))
    spare, spare_new = lax.cond(
        fits[0, 0] == 1,
        lambda *unused: tuple(
            pl.pallas_call(
                empty_kernel,
                out_shape=[shaped((KEYS, KVW), bf16), shaped((128, KVW), bf16)],
                out_specs=[anywhere] * 2,
                name="no_keys",
            )()
        ),
        dense_keys,
        token_ids,
        place,
        embed_table,
        down,
        latent_gain,
        cache_length,
    )
    parts, spare, spare_new = lax.optimization_barrier((parts, spare, spare_new))
    sent = pl.pallas_call(
        finish_kernel,
        out_shape=shaped((SLOTS, WIDE), bf16),
        in_specs=[whole, whole],
        out_specs=whole,
        compiler_params=params(8),
        name="finish_rows",
    )(parts, latent_gain.reshape(1, LAT))
    gathered = sent
    for step in range(3):
        arrived = lax.ppermute(gathered, "z", [(index, index ^ (1 << step)) for index in range(8)])
        if step < 2:
            gathered = pl.pallas_call(
                stack_kernel,
                out_shape=shaped((2 * gathered.shape[0], WIDE), bf16),
                in_specs=[whole] * 2,
                out_specs=whole,
                compiler_params=params(4),
                name="stack_rows",
            )(gathered, arrived)
    handed = pl.pallas_call(
        keep_kernel,
        out_shape=shaped((16, KEPT, WIDE), bf16),
        in_specs=[whole] * 3,
        out_specs=whole,
        compiler_params=params(8),
        name="keep_rows",
    )(kept, gathered, arrived)
    handed, prompt_rows, decode_rows, lengths, earlier, level = lax.optimization_barrier(
        (handed, prefill_query, decode_query, cache_length, earlier, level)
    )
    slots = lax.all_to_all(handed, PLANE, 0, 0, tiled=True).reshape(SIDE, WIDE)

    def by_head(rows):
        return jnp.transpose(rows.reshape(16, 64, -1), (1, 0, 2)).reshape(1024, -1)

    row_query, earlier, level = by_head(decode_rows), by_head(earlier), by_head(level)
    new_position = (lengths[:, None] + jnp.arange(2, dtype=jnp.int32)[None]).reshape(-1)
    new_factors = jnp.pad(rope_factors(new_position.astype(f32)), ((0, 112), (0, 0)))
    prompt_query = jnp.transpose(prompt_rows.reshape(64, 2, 8, KVW), (1, 2, 0, 3)).reshape(1024, KVW)
    slots, prompt_query, row_query, earlier, level, new_factors = lax.optimization_barrier(
        (slots, prompt_query, row_query, earlier, level, new_factors)
    )
    others = lax.ppermute(slots, "core", [(0, 1), (1, 0)])

    near = pl.pallas_call(
        near_kernel,
        out_shape=VMEM((KEYS + 128, WIDE), bf16),
        in_specs=[scalars, scalars, whole, whole],
        out_specs=whole,
        scratch_shapes=[VMEM((1024, SIDE), bf16)],
        compiler_params=params(12),
        cost_estimate=pl.CostEstimate(flops=2 * 10**9, bytes_accessed=10**6, transcendentals=0),
        name="near_keys",
    )(place, prompt_owner, slots, columns)
    factors = jnp.asarray(rope_factors(np.arange(1024, dtype=np.float32)))
    decoded = pl.pallas_call(
        decode_kernel,
        out_shape=pltpu.HBM((128, 4096), bf16),
        in_specs=[scalars] * 3 + [whole] * 8 + [anywhere] * 2,
        out_specs=anywhere,
        scratch_shapes=[
            VMEM((128, 4096), bf16),
            VMEM((KEYS + 128, KVW), bf16),
            VMEM((1024, SIDE), bf16),
            VMEM((1024, 128), f32),
            VMEM((1024, 128), f32),
            VMEM((1024, LAT), f32),
            pltpu.SemaphoreType.DMA,
            pltpu.SemaphoreType.DMA((8,)),
        ],
        compiler_params=params(20),
        cost_estimate=pl.CostEstimate(flops=5 * 10**9, bytes_accessed=7 * 10**6, transcendentals=10**6),
        name="decode_rows",
    )(
        place, prompt_owner, fits, in_vmem(near), in_vmem(others), columns, in_vmem(factors), new_factors,
        in_vmem(row_query), in_vmem(earlier), in_vmem(level), in_hbm(spare), in_hbm(spare_new),
    )
    turned = lax.all_to_all(decoded.reshape(8, 16, 4096), TP, 0, 0, tiled=True).reshape(128, 4096)
    prefilled = pl.pallas_call(
        prefill_kernel,
        out_shape=pltpu.HBM((128, 4096), bf16),
        in_specs=[scalars] * 2 + [whole] * 5 + [anywhere],
        out_specs=whole,
        scratch_shapes=[
            VMEM((1024, KVW), bf16),
            VMEM((1024, SIDE), bf16),
            VMEM((4, 1024, 128), f32),
            VMEM((4, 128, 128), f32),
            pltpu.SemaphoreType.DMA,
        ],
        compiler_params=params(20),
        cost_estimate=pl.CostEstimate(flops=7 * 10**9, bytes_accessed=7 * 10**6, transcendentals=10**6),
        name="prefill_rows",
    )(place, fits, in_vmem(near), in_vmem(others), columns, in_vmem(factors), in_vmem(prompt_query), in_hbm(spare))
    out = pl.pallas_call(
        join_kernel,
        out_shape=pltpu.HBM((128, 4096), bf16),
        in_specs=[scalars] + [anywhere] * 2,
        out_specs=anywhere,
        scratch_shapes=[pltpu.SemaphoreType.DMA((4,))],
        input_output_aliases={1: 0},
        compiler_params=params(4),
        name="join_rows",
    )(place, in_hbm(prefilled), turned)
    return out[None]


def solution(mesh):
    fine_mesh = Mesh(mesh.devices.reshape(2, 8, 4, 2, 2), ("ylo", "z", "x", "core", "role"))
    ctx, tp = ("ylo", "z"), ("x", "core")
    in_specs = (
        P("role", ctx),
        P(ctx + ("role",), tp),
        P(tp, None),
        P(),
        P(ctx, tp, None),
        P(ctx + tp, None, None, None),
        P(ctx + tp, None, None),
        P(ctx + tp),
        P(),
    )
    out_specs = P("role", ctx, tp)
    return jax.shard_map(shards, mesh=fine_mesh, in_specs=in_specs, out_specs=out_specs, check_vma=False)
```

```python
import jax
import jax.numpy as jnp
import numpy as np
from jax import lax
from jax.experimental import pallas as pl
from jax.experimental.pallas import tpu as pltpu
from jax.sharding import Mesh
from jax.sharding import PartitionSpec as P

LAT = 512
KVW = 576
STEPS = 2
WIDE = 640
SLOTS = 16
KEPT = 48
SIDE = 16 * KEPT
KEYS = 2048

score_scale = 0.07216878364870322
base_two = score_scale * 1.4426950408889634
masked_fill = -1e30
norm_eps = 1e-06
rope_base = 10000.0
bf16 = jnp.bfloat16
f32 = jnp.float32
SMEM = pltpu.SMEM
VMEM = pltpu.VMEM

HOLDERS = ("ylo", "z", "role")
PLANE = ("ylo", "role", "x")
TP = ("x", "core")


def iota(shape, axis):
    return lax.broadcasted_iota(jnp.int32, shape, axis)


def ones_where(flags):
    return jnp.where(flags, 1.0, 0.0).astype(bf16)


def dot(left, right):
    return lax.dot_general(left, right, (((1,), (0,)), ((), ())), preferred_element_type=f32)


def dot_nt(left, right):
    return lax.dot_general(left, right, (((1,), (1,)), ((), ())), preferred_element_type=f32)


def whole_loop(count, body, unroll=1):
    def step(index, carry):
        body(index)
        return carry

    lax.fori_loop(0, count, step, 0, unroll=unroll)


def aligned(index, size):
    return pl.ds(pl.multiple_of(index * size, size), size)


def spread_kernel(ids, out):
    out[...] = jnp.broadcast_to(ids[...].reshape(1, 1, 128), out.shape)


def select_kernel(place, ids, table, down, partial, hots, lows, chosen, table_here, down_here, sems):
    holder = (place[0] * 8 + place[1]) * 2 + place[4]
    table_copy = pltpu.make_async_copy(table, table_here, sems.at[0])
    down_copy = pltpu.make_async_copy(down, down_here, sems.at[1])
    table_copy.start()
    down_copy.start()

    def mark(line):
        tokens = ids[pl.ds(line, 1), :]
        span = aligned((line & 1) * 16 + (line >> 1), 128)
        hots[:, span] = ones_where(iota((16, 128), 0) == (tokens >> 7) - holder * 16)
        lows[:, span] = ones_where(iota((128, 128), 0) == (tokens & 127))

    whole_loop(32, mark, 8)
    in_prompt = dot_nt(hots[:, :KEYS], lows[:, :KEYS]) > 0.5
    alone = (dot_nt(hots[:, KEYS:], lows[:, KEYS:]) > 0.5) & jnp.logical_not(in_prompt)
    upper = ones_where(iota((128, 128), 0) < iota((128, 128), 1))
    all_ones = jnp.ones((128, 128), bf16)
    row = iota((8 * SLOTS, 128), 0)
    wanted = ((row & 15) * 8 + (((row >> 4) - holder) & 7)).astype(f32)
    before = jnp.zeros((1, 128), f32)
    ranks = []
    for present in (in_prompt, alone):
        flags = ones_where(present)
        within = dot(flags, upper)
        totals = dot(flags, all_ones)
        lines = []
        for step in range(16):
            lines.append(within[step : step + 1, :] + before)
            before = before + totals[step : step + 1, :]
        ranks.append(lines)
    for step in range(16):
        rank = jnp.where(alone[step : step + 1, :], ranks[1][step], -1.0)
        rank = jnp.where(in_prompt[step : step + 1, :], ranks[0][step], rank)
        chosen[:, step * 128 : (step + 1) * 128] = ones_where(wanted == rank)
    table_copy.wait()
    rows = dot(chosen[...], table_here[...]).astype(bf16)
    down_copy.wait()
    partial[...] = dot_nt(rows, down_here[...]).reshape(partial.shape)


def rank_kernel(ids, sheet, highs, lows):
    square = (128, 128)
    lane = iota((8, 128), 1)
    sheet[0:16, :] = ids[pl.ds(0, 16, stride=2), :]
    sheet[16:32, :] = ids[pl.ds(1, 16, stride=2), :]
    target = iota(square, 1)
    mover = ones_where(iota(square, 0) == jnp.where(target < 64, 2 * target, 2 * target - 127))
    plain = sheet[0:16, :]
    decode_tokens = sheet[16:32, :]
    coarse = (plain >> 8).astype(f32).astype(bf16)
    fine = (plain & 255).astype(f32).astype(bf16)
    moved = dot(coarse, mover) * 256.0 + dot(fine, mover)
    sheet[0:16, :] = moved.astype(jnp.int32)
    even = sheet[pl.ds(0, 8, stride=2), :]
    odd = sheet[pl.ds(1, 8, stride=2), :]
    first = jnp.where(lane < 64, even, pltpu.roll(odd, 64, 1))
    second = jnp.where(lane < 64, pltpu.roll(even, 64, 1), odd)
    tokens = jnp.concatenate([first, second, decode_tokens], axis=0)
    sheet[0:32, :] = tokens

    def mark(block):
        line = sheet[pl.ds(block, 1), :]
        span = aligned(block, 128)
        highs[:, span] = ones_where(iota((512, 128), 0) == (line >> 7))
        lows[:, span] = ones_where(iota(square, 0) == (line & 127))

    whole_loop(32, mark, 8)
    in_prompt = dot_nt(lows[:, :KEYS], highs[:, :KEYS]) > 0.5
    alone = (dot_nt(lows[:, KEYS:], highs[:, KEYS:]) > 0.5) & jnp.logical_not(in_prompt)
    below = ones_where(iota(square, 1) < iota(square, 0))
    all_ones = jnp.ones(square, bf16)
    wide = (512, 512)
    same = (iota(wide, 0) >> 4) == (iota(wide, 1) >> 4)
    in_holder = ones_where(same & (iota(wide, 0) < iota(wide, 1)))
    prompt_flags = ones_where(in_prompt)
    alone_flags = ones_where(alone)
    prompt_columns = dot(all_ones, prompt_flags).astype(bf16)
    alone_columns = dot(all_ones, alone_flags).astype(bf16)
    prompt_rank = dot(below, prompt_flags) + dot(prompt_columns, in_holder)
    alone_rank = (
        dot(below, alone_flags) + dot(alone_columns, in_holder) + dot(prompt_columns, ones_where(same))
    )
    rank = jnp.where(in_prompt, prompt_rank, jnp.where(alone, alone_rank, 0.0))
    top_rank = jnp.max(jnp.max(rank, axis=0, keepdims=True), axis=1, keepdims=True).astype(jnp.int32)
    coded = (jnp.minimum(rank, 127.0) + jnp.where(in_prompt, 128.0, 0.0)).astype(bf16)
    pieces = []
    for chunk in range(4):
        span = slice(chunk * 1024, (chunk + 1) * 1024)
        looked = dot(coded, highs[:, span]) * lows[:, span].astype(f32)
        line = jnp.sum(looked, axis=0, keepdims=True)
        for part in range(8):
            pieces.append(line[:, part * 128 : (part + 1) * 128])
    value = jnp.concatenate(pieces, axis=0).astype(jnp.int32)
    ranks = value & 127
    holder = tokens >> 11
    tp_of = (ranks + holder) & 7
    quad = tp_of * 16 + (ranks >> 3)
    sheet[0:32, :] = quad
    sheet[32:64, :] = holder
    sheet[64:96, :] = jnp.where(value >= 128, -1, tp_of)
    sheet[96:104, :] = jnp.broadcast_to(top_rank, (8, 128))


def place_kernel(place, sheet, columns, kept, fits, quads, holders, hot_tp, hot_pool, sheet_b):
    ylo, zed, ex, core, section = place[0], place[1], place[2], place[3], place[4]
    square = (128, 128)

    def spot(block, source):
        span = aligned(block, 128)
        quads[:, span] = ones_where(iota(square, 0) == sheet[pl.ds(source, 1), :])
        holders[:, span] = ones_where(iota(square, 0) == sheet[pl.ds(source + 32, 1), :])

    whole_loop(16, lambda block: spot(block, block), 8)
    for part in range(2):
        spot(16 + part, 16 + part * 8 + zed)
    own = 16 + ylo * 8 + zed
    spot(18, own)
    up, down = iota(square, 0), iota(square, 1)
    same_tp = (up >> 4) == (down >> 4)
    same_pool = ((up >> 4) == (down >> 4)) & ((up & 1) == (down & 1))
    tp_ones = ones_where(same_tp)
    pool = ones_where(same_pool)
    before = ones_where(same_pool & (up < down))
    in_tp = ones_where(same_tp & (down < up))
    held = dot_nt(quads[:, :KEYS], holders[:, :KEYS]) > 0.5
    flags = ones_where(held)
    sums = dot(tp_ones, flags).astype(bf16)
    prompt_position = dot(in_tp, flags) + dot(sums, before)
    prompt_count = dot(sums, pool)
    positions = []
    for part in range(2):
        span = slice(KEYS + part * 128, KEYS + (part + 1) * 128)
        added = (dot_nt(quads[:, span], holders[:, span]) > 0.5) & jnp.logical_not(held)
        added_flags = ones_where(added)
        added_sums = dot(tp_ones, added_flags).astype(bf16)
        spots = dot(in_tp, added_flags) + dot(added_sums, before) + prompt_count
        spots = jnp.where(held, prompt_position, jnp.where(added, spots, 255.0))
        positions.append(jnp.minimum(spots, 255.0))
    position = jnp.where(ylo == 0, positions[0], positions[1])

    def pick(block):
        span = aligned(block, 128)
        hot_tp[:, span] = ones_where(iota((16, 128), 0) == sheet[pl.ds(block + 80, 1), :])
        line = sheet[pl.ds(block + 48, 1), :]
        line = ((line >> 4) * 2 + (line & 1)) + 4 * block
        hot_pool[:, span] = ones_where(iota((64, 128), 0) == line)

    whole_loop(16, pick, 8)
    gather_tp = ones_where(iota((16, 128), 0) == (iota((16, 128), 1) >> 4))
    base = dot(gather_tp, flags).astype(bf16)
    holder, column = iota((128, 64), 0), iota((128, 64), 1)
    pooled = ones_where((holder < 32) & (((holder >> 4) * 2 + (holder & 1)) == (column & 3)))
    needed = dot_nt(hot_tp[...], hot_pool[...]) + dot(base, pooled)
    needed = jnp.max(jnp.max(needed, axis=0, keepdims=True), axis=1, keepdims=True)
    enough = (sheet[96:97, 0:1] < 8 * SLOTS) & (needed <= float(KEPT))
    fits[0, 0] = jnp.max(jnp.where(enough, 1, 0))

    looked = dot(position.astype(bf16), holders[...]) * quads[...].astype(f32)
    line = jnp.sum(looked, axis=0, keepdims=True)
    found = [line[:, block * 128 : (block + 1) * 128] for block in range(19)]
    found = jnp.concatenate(found + [jnp.zeros((5, 128), f32)], axis=0)
    blank = jnp.zeros((5, 128), jnp.int32)
    quad_rows = jnp.concatenate([sheet[0:16, :], blank[:2], sheet[pl.ds(own, 1), :], blank], axis=0)
    holder_rows = jnp.concatenate([sheet[32:48, :], blank[:2], sheet[pl.ds(own + 32, 1), :], blank], axis=0)
    tp_rows = quad_rows >> 4
    source = ((holder_rows >> 4) * 2 + (holder_rows & 1)) * 4 + (tp_rows >> 1)
    side = jnp.where((tp_rows & 1) == core, 0, SIDE)
    final = found + (source * KEPT + side).astype(f32)
    tp_index = ex * 2 + core
    turned = pltpu.roll(final, (128 - tp_index * 16) % 128, 1)
    turned = jnp.where(iota((24, 128), 1) < 16, turned, -1.0)
    final = jnp.where(iota((24, 128), 0) == 18, turned, final)
    final = jnp.concatenate([final, jnp.zeros((104, 128), f32)], axis=0)
    columns[...] = jnp.transpose(final).astype(jnp.int32)
    few = (16, 128)
    for part in range(2):
        sheet_b[...] = positions[part]
        mine = sheet_b[pl.ds(pl.multiple_of(tp_index * 16, 16), 16), :].astype(bf16)
        spread = dot(mine, ones_where(up == (ylo * 8 + (down >> 4)) * 2 + section))
        spread = jnp.where((iota(few, 1) & 15) == iota(few, 0), spread, 0.0)
        kept[part : part + 1, :] = jnp.sum(spread, axis=0, keepdims=True)


def finish_kernel(parts, gain, sent):
    latent = parts[0]
    for tp in range(1, parts.shape[0]):
        latent = latent + parts[tp]
    plain = latent[:, :LAT]
    scaled = plain * lax.rsqrt(jnp.mean(plain * plain, axis=-1, keepdims=True) + norm_eps) * gain[...]
    rotary = latent[:, LAT:]
    coarse = rotary.astype(bf16)
    fine = (rotary - coarse.astype(f32)).astype(bf16)
    row = jnp.concatenate([scaled.astype(bf16), coarse, fine], axis=-1)
    for peer in range(sent.shape[0]):
        sent[peer] = row


def keep_kernel(kept, rows, sent):
    for ylo in range(2):
        chosen = iota((KEPT, 128), 0).astype(f32) == kept[ylo : ylo + 1, :]
        row = dot(ones_where(chosen), rows[...]).astype(bf16)
        for peer in range(8):
            sent[ylo * 8 + peer] = row


def cache_kernel(lengths, query, cache, out, level):
    length = lengths[pl.program_id(0)]
    scores = dot(query[0], cache[0]) * base_two
    scores = jnp.where(iota(scores.shape, 1) < length, scores, masked_fill)
    highest = jnp.max(scores, axis=-1, keepdims=True)
    weights = jnp.exp2(scores - highest)
    total = jnp.sum(weights, axis=-1, keepdims=True)
    out[...] = (dot_nt(weights.astype(bf16), cache[0, :LAT, :]) * (1.0 / total)).astype(bf16)
    level[...] = jnp.broadcast_to(highest + jnp.log2(total), level.shape)


def hot_rows(hot, columns, prompt, side):
    turned = pltpu.roll(columns[...], (128 - prompt * 8) % 128, 1) - side * SIDE
    for block in range(8):
        hot[block * 128 : (block + 1) * 128, :] = ones_where(iota((128, SIDE), 1) == turned[:, block : block + 1])


def empty_kernel(*refs):
    pass


def fresh_hot(columns, side):
    return ones_where(iota((128, SIDE), 1) == columns[:, 18:19] - side * SIDE)


def put_keys(keys, span, found, factor):
    turning = found[:, LAT:]
    turning = turning + pltpu.roll(turning, 64, 1)
    turned = turning * factor + pltpu.roll(turning, 32, 1) * pltpu.roll(factor, 64, 1)
    keys[span, :LAT] = found[:, :LAT].astype(bf16)
    keys[span, LAT:] = turned[:, : KVW - LAT].astype(bf16)


def copy_in(source, target, sem):
    copy = pltpu.make_async_copy(source, target, sem)
    copy.start()
    copy.wait()


def weigh(scores, old):
    new = jnp.maximum(old, jnp.max(scores, axis=-1, keepdims=True))
    weights = jnp.exp2(scores - new)
    return new, jnp.exp2(old - new), jnp.sum(weights, axis=-1, keepdims=True), weights.astype(bf16)


def near_kernel(place, owner, slots, columns, near, hot):
    group = place[0] * 8 + place[1]

    @pl.when(place[4] == 1)
    def _():
        near[KEYS : KEYS + 128, :] = dot(fresh_hot(columns, 0), slots[...]).astype(bf16)

    def open_prompt(prompt):
        @pl.when((place[4] == 0) | (owner[prompt] == group))
        def _():
            hot_rows(hot, columns, prompt, 0)

            def open_part(part):
                near[aligned(prompt * 2 + part, 512), :] = dot(hot[aligned(part, 512), :], slots[...]).astype(bf16)

            whole_loop(2, open_part, 2)

    whole_loop(2, open_prompt)


def decode_kernel(
    place, owner, fits, near, others, columns, factors, new_factors, query, earlier, level, spare, spare_new,
    out, out_here, keys, hot, highest, total, mixed, sem, out_sems
):
    group = place[0] * 8 + place[1]
    fitting = fits[0, 0] == 1

    @pl.when(place[4] == 1)
    def _():
        @pl.when(fitting)
        def _():
            span = slice(KEYS, KEYS + 128)
            found = near[span, :].astype(f32) + dot(fresh_hot(columns, 1), others[...])
            put_keys(keys, span, found, new_factors[...])

        @pl.when(jnp.logical_not(fitting))
        def _():
            copy_in(spare_new, keys.at[pl.ds(KEYS, 128)], sem)

        newest = keys[KEYS : KEYS + 128, :]

        def begin(piece):
            span = aligned(piece, 256)
            scores = dot_nt(query[span, :], newest) * base_two
            key = iota(scores.shape, 1)
            row = iota(scores.shape, 0) & 15
            allowed = ((key >> 1) == (row >> 1)) & ((key & 1) <= (row & 1))
            scores = jnp.where(allowed, scores, masked_fill)
            new, factor, summed, weights = weigh(scores, level[span, 0:1])
            mixed[span, :] = earlier[span, :].astype(f32) * factor + dot(weights, newest[:, :LAT])
            highest[span, :] = jnp.broadcast_to(new, (256, 128))
            total[span, :] = jnp.broadcast_to(factor + summed, (256, 128))

        whole_loop(4, begin, 4)

        def add_prompt(prompt):
            @pl.when(owner[prompt] == group)
            def _():
                @pl.when(fitting)
                def _():
                    hot_rows(hot, columns, prompt, 1)

                    def open_part(part):
                        span = aligned(prompt * 2 + part, 512)
                        found = near[span, :].astype(f32) + dot(hot[aligned(part, 512), :], others[...])
                        put_keys(keys, span, found, factors[aligned(part, 512), :])

                    whole_loop(2, open_part, 2)

                @pl.when(jnp.logical_not(fitting))
                def _():
                    copy_in(spare.at[pl.ds(prompt * 1024, 1024)], keys.at[pl.ds(prompt * 1024, 1024)], sem)

                def add_part(piece):
                    span = aligned(piece, 256)
                    some = keys[aligned(prompt, 1024), :]
                    new, factor, summed, weights = weigh(dot_nt(query[span, :], some) * base_two, highest[span, 0:1])
                    mixed[span, :] = mixed[span, :] * factor + dot(weights, some[:, :LAT])
                    highest[span, :] = jnp.broadcast_to(new, (256, 128))
                    total[span, :] = total[span, :] * factor + summed

                whole_loop(4, add_part, 4)

        whole_loop(2, add_prompt)

        def out_copy(tp):
            rows = aligned(tp, 16)
            return pltpu.make_async_copy(out_here.at[rows], out.at[rows], out_sems.at[tp])

        def tp_rows(tp):
            for head in range(8):
                rows = pl.ds(pl.multiple_of(tp * 128 + head * 16, 16), 16)
                some = mixed[rows, :] * (1.0 / total[rows, 0:1])
                out_here[aligned(tp, 16), head * LAT : (head + 1) * LAT] = some.astype(bf16)
            out_copy(tp).start()

        whole_loop(8, tp_rows, 2)
        whole_loop(8, lambda tp: out_copy(tp).wait())


def prefill_kernel(place, fits, near, others, columns, factors, query, spare, out, keys, hot, mixed, pairs, sem):
    group = place[0] * 8 + place[1]
    fitting = fits[0, 0] == 1

    @pl.when(place[4] == 0)
    def _():
        def add_prompt(prompt):
            @pl.when(fitting)
            def _():
                hot_rows(hot, columns, prompt, 1)

                def open_part(part):
                    span = aligned(part, 512)
                    found = near[aligned(prompt * 2 + part, 512), :].astype(f32) + dot(hot[span, :], others[...])
                    put_keys(keys, span, found, factors[span, :])

                whole_loop(2, open_part, 2)

            @pl.when(jnp.logical_not(fitting))
            def _():
                copy_in(spare.at[pl.ds(prompt * 1024, 1024)], keys, sem)

            span = aligned(prompt, 512)
            some = keys[...]
            scores = dot_nt(query[span, :], some) * base_two
            last = (iota((512, 1), 0) & 63) + group * 64
            scores = jnp.where(iota(scores.shape, 1) <= last, scores, masked_fill)
            _, _, summed, weights = weigh(scores, jnp.full((512, 1), masked_fill, f32))
            added = dot(weights, some[:, :LAT]) * (1.0 / summed)
            for column in range(4):
                mixed[column, span, :] = added[:, column * 128 : (column + 1) * 128]

        whole_loop(2, add_prompt)

        def head_rows(head):
            for column in range(4):
                for prompt in range(2):
                    start = pl.multiple_of(prompt * 512 + head * 64, 64)
                    pairs[column, pl.ds(prompt, 64, stride=2), :] = mixed[column, pl.ds(start, 64), :]
                out[:, pl.ds(pl.multiple_of(head * LAT + column * 128, 128), 128)] = pairs[column].astype(bf16)

        whole_loop(8, head_rows, 2)


def join_kernel(place, prefilled, turned, out, sems):
    @pl.when(place[4] == 1)
    def _():
        copies = []
        for part in range(4):
            span = pl.ds(part * 32, 32)
            copies.append(pltpu.make_async_copy(turned.at[span], out.at[span], sems.at[part]))
        for copy in copies:
            copy.start()
        for copy in copies:
            copy.wait()


def rope_factors(position):
    frequency = np.float32(rope_base) ** (-np.arange(32, dtype=np.float32) / np.float32(32))
    angles = position[:, None] * frequency[None, :]
    if isinstance(position, np.ndarray):
        angles = angles.astype(np.float32).astype(np.float64)
        cosine, sine = np.cos(angles), np.sin(angles)
        return np.concatenate([cosine, cosine, -sine, sine], axis=-1).astype(np.float32)
    cosine, sine = jnp.cos(angles), jnp.sin(angles)
    return jnp.concatenate([cosine, cosine, -sine, sine], axis=-1)


def finish_keys(latent, latent_gain, position):
    plain = latent[:, :LAT]
    scaled = plain * lax.rsqrt(jnp.mean(plain * plain, axis=-1, keepdims=True) + norm_eps) * latent_gain
    factors = rope_factors(position.astype(f32))
    rotary = latent[:, LAT:]
    swapped = jnp.concatenate([rotary[:, 32:], rotary[:, :32]], axis=-1)
    turned = rotary * factors[:, :64] + swapped * factors[:, 64:]
    return jnp.concatenate([scaled, turned], axis=-1).astype(bf16)


def dense_keys(token_ids, place, embed_table, down, latent_gain, cache_length):
    group = place[0] * 8 + place[1]
    tp_index = place[2] * 2 + place[3]
    every = lax.all_to_all(jnp.broadcast_to(token_ids, (32, 128)).reshape(32, 1, 128), HOLDERS, 0, 0, tiled=True)
    local_row = every.reshape(-1) - (group * 2 + place[4]) * 2048
    inside = (local_row >= 0) & (local_row < 2048)
    picked = jnp.take(embed_table, jnp.clip(local_row, 0, 2047), axis=0)
    picked = jnp.where(inside[:, None], picked, jnp.zeros_like(picked)).reshape(32, 128, 896)
    embedded = jnp.sum(lax.all_to_all(picked, HOLDERS, 0, 0, tiled=True).astype(f32), axis=0).astype(bf16)
    partial = dot_nt(embedded, down)
    spread = jnp.broadcast_to(partial[None], (8, 128, KVW))
    latent = jnp.sum(lax.all_to_all(spread, TP, 0, 0, tiled=True), axis=0)
    index = jnp.arange(128, dtype=jnp.int32)
    mine = finish_keys(latent, latent_gain, group * 64 + index // 2)
    spread = jnp.broadcast_to(mine[None], (32, 128, KVW))
    prompts = lax.all_to_all(spread, HOLDERS, 0, 0, tiled=True).reshape(16, 2, 64, 2, KVW)[:, 0]
    prompts = jnp.transpose(prompts, (2, 0, 1, 3)).reshape(KEYS, KVW)
    own = lax.dynamic_slice_in_dim(latent, tp_index * 16, 16, 0)
    fresh = finish_keys(own, latent_gain, (cache_length[:, None] + jnp.arange(2, dtype=jnp.int32)[None]).reshape(-1))
    return prompts, jnp.concatenate([fresh, jnp.zeros((112, KVW), bf16)], axis=0)


def in_vmem(value):
    return pltpu.with_memory_space_constraint(value, VMEM)


def in_hbm(value):
    return pltpu.with_memory_space_constraint(value, pltpu.HBM)


def params(mebibytes):
    return pltpu.CompilerParams(vmem_limit_bytes=mebibytes * 1024 * 1024)


def shards(
    token_ids,
    embed_table,
    latent_down,
    latent_gain,
    prefill_query,
    decode_query,
    latent_cache,
    cache_length,
    prompt_owner,
):
    place = jnp.stack([lax.axis_index(name) for name in ("ylo", "z", "x", "core", "role")]).astype(jnp.int32)
    down = jnp.transpose(latent_down)
    whole = pl.BlockSpec(memory_space=VMEM)
    scalars = pl.BlockSpec(memory_space=SMEM)
    anywhere = pl.BlockSpec(memory_space=pl.ANY)
    shaped = jax.ShapeDtypeStruct

    spread = pl.pallas_call(
        spread_kernel,
        out_shape=shaped((32, 1, 128), jnp.int32),
        in_specs=[whole],
        out_specs=whole,
        compiler_params=params(4),
        name="spread_ids",
    )(token_ids)
    every = lax.all_to_all(spread, HOLDERS, 0, 0, tiled=True).reshape(32, 128)

    earlier, level = pl.pallas_call(
        cache_kernel,
        grid_spec=pltpu.PrefetchScalarGridSpec(
            num_scalar_prefetch=1,
            grid=(8,),
            in_specs=[
                pl.BlockSpec((1, 128, KVW), lambda row, lengths: (row, 0, 0)),
                pl.BlockSpec((1, KVW, 512), lambda row, lengths: (row, 0, 0)),
            ],
            out_specs=[
                pl.BlockSpec((128, LAT), lambda row, lengths: (row, 0)),
                pl.BlockSpec((128, 128), lambda row, lengths: (row, 0)),
            ],
        ),
        out_shape=(pltpu.HBM((1024, LAT), bf16), pltpu.HBM((1024, 128), f32)),
        compiler_params=params(12),
        cost_estimate=pl.CostEstimate(flops=12 * 10**8, bytes_accessed=7 * 10**6, transcendentals=524288),
        name="cache_rows",
    )(cache_length, in_hbm(decode_query.reshape(8, 128, KVW)), in_hbm(jnp.swapaxes(latent_cache, 1, 2)))
    every, earlier, level = lax.optimization_barrier((every, earlier, level))

    partial = pl.pallas_call(
        select_kernel,
        out_shape=shaped((8, SLOTS, KVW), f32),
        in_specs=[scalars, whole, anywhere, anywhere],
        out_specs=whole,
        scratch_shapes=[
            VMEM((16, 4096), bf16),
            VMEM((128, 4096), bf16),
            VMEM((8 * SLOTS, 2048), bf16),
            VMEM((2048, 896), bf16),
            VMEM((KVW, 896), bf16),
            pltpu.SemaphoreType.DMA((2,)),
        ],
        compiler_params=params(16),
        cost_estimate=pl.CostEstimate(flops=3 * 10**9, bytes_accessed=5 * 10**6, transcendentals=0),
        name="select_rows",
    )(place, every, in_hbm(embed_table), in_hbm(down))
    parts = lax.all_to_all(partial, TP, 0, 0, tiled=True)

    sheet = pl.pallas_call(
        rank_kernel,
        out_shape=shaped((104, 128), jnp.int32),
        in_specs=[whole],
        out_specs=whole,
        scratch_shapes=[VMEM((512, 4096), bf16), VMEM((128, 4096), bf16)],
        compiler_params=params(18),
        cost_estimate=pl.CostEstimate(flops=2 * 10**9, bytes_accessed=10**6, transcendentals=0),
        name="rank_rows",
    )(every)
    columns, kept, fits = pl.pallas_call(
        place_kernel,
        out_shape=(shaped((128, 128), jnp.int32), shaped((8, 128), f32), shaped((1, 1), jnp.int32)),
        in_specs=[scalars, whole],
        out_specs=(whole, whole, scalars),
        scratch_shapes=[
            VMEM((128, 19 * 128), bf16),
            VMEM((128, 19 * 128), bf16),
            VMEM((16, 2048), bf16),
            VMEM((64, 2048), bf16),
            VMEM((128, 128), f32),
        ],
        compiler_params=params(12),
        cost_estimate=pl.CostEstimate(flops=10**9, bytes_accessed=10**6, transcendentals=0),
        name="place_rows",
    )(place, sheet)
    parts, columns, kept, fits = lax.optimization_barrier((parts, columns, kept, fits))
    spare, spare_new = lax.cond(
        fits[0, 0] == 1,
        lambda *unused: tuple(
            pl.pallas_call(
                empty_kernel,
                out_shape=[shaped((KEYS, KVW), bf16), shaped((128, KVW), bf16)],
                out_specs=[anywhere] * 2,
                name="no_keys",
            )()
        ),
        dense_keys,
        token_ids,
        place,
        embed_table,
        down,
        latent_gain,
        cache_length,
    )
    parts, spare, spare_new = lax.optimization_barrier((parts, spare, spare_new))
    sent = pl.pallas_call(
        finish_kernel,
        out_shape=shaped((8, SLOTS, WIDE), bf16),
        in_specs=[whole, whole],
        out_specs=whole,
        compiler_params=params(8),
        name="finish_rows",
    )(parts, latent_gain.reshape(1, LAT))
    arrived = lax.all_to_all(sent, "z", 0, 0, tiled=True)
    handed = pl.pallas_call(
        keep_kernel,
        out_shape=shaped((16, KEPT, WIDE), bf16),
        in_specs=[whole] * 2,
        out_specs=whole,
        compiler_params=params(8),
        name="keep_rows",
    )(kept, arrived.reshape(8 * SLOTS, WIDE))
    handed, prompt_rows, decode_rows, lengths, earlier, level = lax.optimization_barrier(
        (handed, prefill_query, decode_query, cache_length, earlier, level)
    )
    slots = lax.all_to_all(handed, PLANE, 0, 0, tiled=True).reshape(SIDE, WIDE)

    def by_head(rows):
        return jnp.transpose(rows.reshape(16, 64, -1), (1, 0, 2)).reshape(1024, -1)

    row_query, earlier, level = by_head(decode_rows), by_head(earlier), by_head(level)
    new_position = (lengths[:, None] + jnp.arange(2, dtype=jnp.int32)[None]).reshape(-1)
    new_factors = jnp.pad(rope_factors(new_position.astype(f32)), ((0, 112), (0, 0)))
    prompt_query = jnp.transpose(prompt_rows.reshape(64, 2, 8, KVW), (1, 2, 0, 3)).reshape(1024, KVW)
    slots, prompt_query, row_query, earlier, level, new_factors = lax.optimization_barrier(
        (slots, prompt_query, row_query, earlier, level, new_factors)
    )
    others = lax.ppermute(slots, "core", [(0, 1), (1, 0)])

    near = pl.pallas_call(
        near_kernel,
        out_shape=VMEM((KEYS + 128, WIDE), bf16),
        in_specs=[scalars, scalars, whole, whole],
        out_specs=whole,
        scratch_shapes=[VMEM((1024, SIDE), bf16)],
        compiler_params=params(12),
        cost_estimate=pl.CostEstimate(flops=2 * 10**9, bytes_accessed=10**6, transcendentals=0),
        name="near_keys",
    )(place, prompt_owner, slots, columns)
    factors = jnp.asarray(rope_factors(np.arange(1024, dtype=np.float32)))
    decoded = pl.pallas_call(
        decode_kernel,
        out_shape=pltpu.HBM((128, 4096), bf16),
        in_specs=[scalars] * 3 + [whole] * 8 + [anywhere] * 2,
        out_specs=anywhere,
        scratch_shapes=[
            VMEM((128, 4096), bf16),
            VMEM((KEYS + 128, KVW), bf16),
            VMEM((1024, SIDE), bf16),
            VMEM((1024, 128), f32),
            VMEM((1024, 128), f32),
            VMEM((1024, LAT), f32),
            pltpu.SemaphoreType.DMA,
            pltpu.SemaphoreType.DMA((8,)),
        ],
        compiler_params=params(20),
        cost_estimate=pl.CostEstimate(flops=5 * 10**9, bytes_accessed=7 * 10**6, transcendentals=10**6),
        name="decode_rows",
    )(
        place, prompt_owner, fits, in_vmem(near), in_vmem(others), columns, in_vmem(factors), new_factors,
        in_vmem(row_query), in_vmem(earlier), in_vmem(level), in_hbm(spare), in_hbm(spare_new),
    )
    turned = lax.all_to_all(decoded.reshape(8, 16, 4096), TP, 0, 0, tiled=True).reshape(128, 4096)
    prefilled = pl.pallas_call(
        prefill_kernel,
        out_shape=pltpu.HBM((128, 4096), bf16),
        in_specs=[scalars] * 2 + [whole] * 5 + [anywhere],
        out_specs=whole,
        scratch_shapes=[
            VMEM((1024, KVW), bf16),
            VMEM((1024, SIDE), bf16),
            VMEM((4, 1024, 128), f32),
            VMEM((4, 128, 128), f32),
            pltpu.SemaphoreType.DMA,
        ],
        compiler_params=params(20),
        cost_estimate=pl.CostEstimate(flops=7 * 10**9, bytes_accessed=7 * 10**6, transcendentals=10**6),
        name="prefill_rows",
    )(place, fits, in_vmem(near), in_vmem(others), columns, in_vmem(factors), in_vmem(prompt_query), in_hbm(spare))
    out = pl.pallas_call(
        join_kernel,
        out_shape=pltpu.HBM((128, 4096), bf16),
        in_specs=[scalars] + [anywhere] * 2,
        out_specs=anywhere,
        scratch_shapes=[pltpu.SemaphoreType.DMA((4,))],
        input_output_aliases={1: 0},
        compiler_params=params(4),
        name="join_rows",
    )(place, in_hbm(prefilled), turned)
    return out[None]


def solution(mesh):
    fine_mesh = Mesh(mesh.devices.reshape(2, 8, 4, 2, 2), ("ylo", "z", "x", "core", "role"))
    ctx, tp = ("ylo", "z"), ("x", "core")
    in_specs = (
        P("role", ctx),
        P(ctx + ("role",), tp),
        P(tp, None),
        P(),
        P(ctx, tp, None),
        P(ctx + tp, None, None, None),
        P(ctx + tp, None, None),
        P(ctx + tp),
        P(),
    )
    out_specs = P("role", ctx, tp)
    return jax.shard_map(shards, mesh=fine_mesh, in_specs=in_specs, out_specs=out_specs, check_vma=False)
```

```python
import jax
import jax.numpy as jnp
import numpy as np
from jax import lax
from jax.experimental import pallas as pl
from jax.experimental.pallas import tpu as pltpu
from jax.sharding import Mesh
from jax.sharding import PartitionSpec as P

LAT = 512
KVW = 576
STEPS = 2
WIDE = 640
SLOTS = 16
KEPT = 48
SIDE = 16 * KEPT
KEYS = 2048

score_scale = 0.07216878364870322
base_two = score_scale * 1.4426950408889634
masked_fill = -1e30
norm_eps = 1e-06
rope_base = 10000.0
bf16 = jnp.bfloat16
f32 = jnp.float32
SMEM = pltpu.SMEM
VMEM = pltpu.VMEM

HOLDERS = ("ylo", "z", "role")
PLANE = ("ylo", "role", "x")
TP = ("x", "core")


def iota(shape, axis):
    return lax.broadcasted_iota(jnp.int32, shape, axis)


def ones_where(flags):
    return jnp.where(flags, 1.0, 0.0).astype(bf16)


def dot(left, right):
    return lax.dot_general(left, right, (((1,), (0,)), ((), ())), preferred_element_type=f32)


def dot_nt(left, right):
    return lax.dot_general(left, right, (((1,), (1,)), ((), ())), preferred_element_type=f32)


def whole_loop(count, body, unroll=1):
    def step(index, carry):
        body(index)
        return carry

    lax.fori_loop(0, count, step, 0, unroll=unroll)


def aligned(index, size):
    return pl.ds(pl.multiple_of(index * size, size), size)


def spread_kernel(ids, out):
    out[...] = jnp.broadcast_to(ids[...].reshape(1, 1, 128), out.shape)


def select_kernel(place, ids, table, down, partial, hots, lows, chosen, table_here, down_here, sems):
    holder = (place[0] * 8 + place[1]) * 2 + place[4]
    table_copy = pltpu.make_async_copy(table, table_here, sems.at[0])
    down_copy = pltpu.make_async_copy(down, down_here, sems.at[1])
    table_copy.start()
    down_copy.start()

    def mark(line):
        tokens = ids[pl.ds(line, 1), :]
        span = aligned((line & 1) * 16 + (line >> 1), 128)
        hots[:, span] = ones_where(iota((16, 128), 0) == (tokens >> 7) - holder * 16)
        lows[:, span] = ones_where(iota((128, 128), 0) == (tokens & 127))

    whole_loop(32, mark, 8)
    in_prompt = dot_nt(hots[:, :KEYS], lows[:, :KEYS]) > 0.5
    alone = (dot_nt(hots[:, KEYS:], lows[:, KEYS:]) > 0.5) & jnp.logical_not(in_prompt)
    upper = ones_where(iota((128, 128), 0) < iota((128, 128), 1))
    all_ones = jnp.ones((128, 128), bf16)
    row = iota((8 * SLOTS, 128), 0)
    wanted = ((row & 15) * 8 + (((row >> 4) - holder) & 7)).astype(f32)
    before = jnp.zeros((1, 128), f32)
    ranks = []
    for present in (in_prompt, alone):
        flags = ones_where(present)
        within = dot(flags, upper)
        totals = dot(flags, all_ones)
        lines = []
        for step in range(16):
            lines.append(within[step : step + 1, :] + before)
            before = before + totals[step : step + 1, :]
        ranks.append(lines)
    for step in range(16):
        rank = jnp.where(alone[step : step + 1, :], ranks[1][step], -1.0)
        rank = jnp.where(in_prompt[step : step + 1, :], ranks[0][step], rank)
        chosen[:, step * 128 : (step + 1) * 128] = ones_where(wanted == rank)
    table_copy.wait()
    rows = dot(chosen[...], table_here[...]).astype(bf16)
    down_copy.wait()
    partial[...] = dot_nt(rows, down_here[...]).reshape(partial.shape)


def rank_kernel(ids, sheet, highs, lows):
    square = (128, 128)
    lane = iota((8, 128), 1)
    sheet[0:16, :] = ids[pl.ds(0, 16, stride=2), :]
    sheet[16:32, :] = ids[pl.ds(1, 16, stride=2), :]
    target = iota(square, 1)
    mover = ones_where(iota(square, 0) == jnp.where(target < 64, 2 * target, 2 * target - 127))
    plain = sheet[0:16, :]
    decode_tokens = sheet[16:32, :]
    coarse = (plain >> 8).astype(f32).astype(bf16)
    fine = (plain & 255).astype(f32).astype(bf16)
    moved = dot(coarse, mover) * 256.0 + dot(fine, mover)
    sheet[0:16, :] = moved.astype(jnp.int32)
    even = sheet[pl.ds(0, 8, stride=2), :]
    odd = sheet[pl.ds(1, 8, stride=2), :]
    first = jnp.where(lane < 64, even, pltpu.roll(odd, 64, 1))
    second = jnp.where(lane < 64, pltpu.roll(even, 64, 1), odd)
    tokens = jnp.concatenate([first, second, decode_tokens], axis=0)
    sheet[0:32, :] = tokens

    def mark(block):
        line = sheet[pl.ds(block, 1), :]
        span = aligned(block, 128)
        highs[:, span] = ones_where(iota((512, 128), 0) == (line >> 7))
        lows[:, span] = ones_where(iota(square, 0) == (line & 127))

    whole_loop(32, mark, 8)
    in_prompt = dot_nt(lows[:, :KEYS], highs[:, :KEYS]) > 0.5
    alone = (dot_nt(lows[:, KEYS:], highs[:, KEYS:]) > 0.5) & jnp.logical_not(in_prompt)
    below = ones_where(iota(square, 1) < iota(square, 0))
    all_ones = jnp.ones(square, bf16)
    wide = (512, 512)
    same = (iota(wide, 0) >> 4) == (iota(wide, 1) >> 4)
    in_holder = ones_where(same & (iota(wide, 0) < iota(wide, 1)))
    prompt_flags = ones_where(in_prompt)
    alone_flags = ones_where(alone)
    prompt_columns = dot(all_ones, prompt_flags).astype(bf16)
    alone_columns = dot(all_ones, alone_flags).astype(bf16)
    prompt_rank = dot(below, prompt_flags) + dot(prompt_columns, in_holder)
    alone_rank = (
        dot(below, alone_flags) + dot(alone_columns, in_holder) + dot(prompt_columns, ones_where(same))
    )
    rank = jnp.where(in_prompt, prompt_rank, jnp.where(alone, alone_rank, 0.0))
    top_rank = jnp.max(jnp.max(rank, axis=0, keepdims=True), axis=1, keepdims=True).astype(jnp.int32)
    coded = (jnp.minimum(rank, 127.0) + jnp.where(in_prompt, 128.0, 0.0)).astype(bf16)
    pieces = []
    for chunk in range(4):
        span = slice(chunk * 1024, (chunk + 1) * 1024)
        looked = dot(coded, highs[:, span]) * lows[:, span].astype(f32)
        line = jnp.sum(looked, axis=0, keepdims=True)
        for part in range(8):
            pieces.append(line[:, part * 128 : (part + 1) * 128])
    value = jnp.concatenate(pieces, axis=0).astype(jnp.int32)
    ranks = value & 127
    holder = tokens >> 11
    tp_of = (ranks + holder) & 7
    quad = tp_of * 16 + (ranks >> 3)
    sheet[0:32, :] = quad
    sheet[32:64, :] = holder
    sheet[64:96, :] = jnp.where(value >= 128, -1, tp_of)
    sheet[96:104, :] = jnp.broadcast_to(top_rank, (8, 128))


def place_kernel(place, sheet, columns, kept, fits, quads, holders, hot_tp, hot_pool, sheet_b):
    ylo, zed, ex, core, section = place[0], place[1], place[2], place[3], place[4]
    square = (128, 128)

    def spot(block, source):
        span = aligned(block, 128)
        quads[:, span] = ones_where(iota(square, 0) == sheet[pl.ds(source, 1), :])
        holders[:, span] = ones_where(iota(square, 0) == sheet[pl.ds(source + 32, 1), :])

    whole_loop(16, lambda block: spot(block, block), 8)
    for part in range(2):
        spot(16 + part, 16 + part * 8 + zed)
    own = 16 + ylo * 8 + zed
    spot(18, own)
    up, down = iota(square, 0), iota(square, 1)
    same_tp = (up >> 4) == (down >> 4)
    same_pool = ((up >> 4) == (down >> 4)) & ((up & 1) == (down & 1))
    tp_ones = ones_where(same_tp)
    pool = ones_where(same_pool)
    before = ones_where(same_pool & (up < down))
    in_tp = ones_where(same_tp & (down < up))
    held = dot_nt(quads[:, :KEYS], holders[:, :KEYS]) > 0.5
    flags = ones_where(held)
    sums = dot(tp_ones, flags).astype(bf16)
    prompt_position = dot(in_tp, flags) + dot(sums, before)
    prompt_count = dot(sums, pool)
    positions = []
    for part in range(2):
        span = slice(KEYS + part * 128, KEYS + (part + 1) * 128)
        added = (dot_nt(quads[:, span], holders[:, span]) > 0.5) & jnp.logical_not(held)
        added_flags = ones_where(added)
        added_sums = dot(tp_ones, added_flags).astype(bf16)
        spots = dot(in_tp, added_flags) + dot(added_sums, before) + prompt_count
        spots = jnp.where(held, prompt_position, jnp.where(added, spots, 255.0))
        positions.append(jnp.minimum(spots, 255.0))
    position = jnp.where(ylo == 0, positions[0], positions[1])

    def pick(block):
        span = aligned(block, 128)
        hot_tp[:, span] = ones_where(iota((16, 128), 0) == sheet[pl.ds(block + 80, 1), :])
        line = sheet[pl.ds(block + 48, 1), :]
        line = ((line >> 4) * 2 + (line & 1)) + 4 * block
        hot_pool[:, span] = ones_where(iota((64, 128), 0) == line)

    whole_loop(16, pick, 8)
    gather_tp = ones_where(iota((16, 128), 0) == (iota((16, 128), 1) >> 4))
    base = dot(gather_tp, flags).astype(bf16)
    holder, column = iota((128, 64), 0), iota((128, 64), 1)
    pooled = ones_where((holder < 32) & (((holder >> 4) * 2 + (holder & 1)) == (column & 3)))
    needed = dot_nt(hot_tp[...], hot_pool[...]) + dot(base, pooled)
    needed = jnp.max(jnp.max(needed, axis=0, keepdims=True), axis=1, keepdims=True)
    enough = (sheet[96:97, 0:1] < 8 * SLOTS) & (needed <= float(KEPT))
    fits[0, 0] = jnp.max(jnp.where(enough, 1, 0))

    looked = dot(position.astype(bf16), holders[...]) * quads[...].astype(f32)
    line = jnp.sum(looked, axis=0, keepdims=True)
    found = [line[:, block * 128 : (block + 1) * 128] for block in range(19)]
    found = jnp.concatenate(found + [jnp.zeros((5, 128), f32)], axis=0)
    blank = jnp.zeros((5, 128), jnp.int32)
    quad_rows = jnp.concatenate([sheet[0:16, :], blank[:2], sheet[pl.ds(own, 1), :], blank], axis=0)
    holder_rows = jnp.concatenate([sheet[32:48, :], blank[:2], sheet[pl.ds(own + 32, 1), :], blank], axis=0)
    tp_rows = quad_rows >> 4
    source = ((holder_rows >> 4) * 2 + (holder_rows & 1)) * 4 + (tp_rows >> 1)
    side = jnp.where((tp_rows & 1) == core, 0, SIDE)
    final = found + (source * KEPT + side).astype(f32)
    tp_index = ex * 2 + core
    turned = pltpu.roll(final, (128 - tp_index * 16) % 128, 1)
    turned = jnp.where(iota((24, 128), 1) < 16, turned, -1.0)
    final = jnp.where(iota((24, 128), 0) == 18, turned, final)
    final = jnp.concatenate([final, jnp.zeros((104, 128), f32)], axis=0)
    columns[...] = jnp.transpose(final).astype(jnp.int32)
    few = (16, 128)
    for part in range(2):
        sheet_b[...] = positions[part]
        mine = sheet_b[pl.ds(pl.multiple_of(tp_index * 16, 16), 16), :].astype(bf16)
        spread = dot(mine, ones_where(up == (ylo * 8 + (down >> 4)) * 2 + section))
        spread = jnp.where((iota(few, 1) & 15) == iota(few, 0), spread, 0.0)
        kept[part : part + 1, :] = jnp.sum(spread, axis=0, keepdims=True)


def finish_kernel(parts, gain, sent):
    latent = parts[0]
    for tp in range(1, parts.shape[0]):
        latent = latent + parts[tp]
    plain = latent[:, :LAT]
    scaled = plain * lax.rsqrt(jnp.mean(plain * plain, axis=-1, keepdims=True) + norm_eps) * gain[...]
    rotary = latent[:, LAT:]
    coarse = rotary.astype(bf16)
    fine = (rotary - coarse.astype(f32)).astype(bf16)
    row = jnp.concatenate([scaled.astype(bf16), coarse, fine], axis=-1)
    for peer in range(sent.shape[0]):
        sent[peer] = row


def keep_kernel(kept, rows, sent):
    for ylo in range(2):
        chosen = iota((KEPT, 128), 0).astype(f32) == kept[ylo : ylo + 1, :]
        row = dot(ones_where(chosen), rows[...]).astype(bf16)
        for peer in range(8):
            sent[ylo * 8 + peer] = row


def cache_kernel(lengths, query, cache, out, level):
    length = lengths[pl.program_id(0)]
    scores = dot(query[0], cache[0]) * base_two
    scores = jnp.where(iota(scores.shape, 1) < length, scores, masked_fill)
    highest = jnp.max(scores, axis=-1, keepdims=True)
    weights = jnp.exp2(scores - highest)
    total = jnp.sum(weights, axis=-1, keepdims=True)
    out[...] = (dot_nt(weights.astype(bf16), cache[0, :LAT, :]) * (1.0 / total)).astype(bf16)
    level[...] = jnp.broadcast_to(highest + jnp.log2(total), level.shape)


def hot_rows(hot, columns, prompt, side):
    turned = pltpu.roll(columns[...], (128 - prompt * 8) % 128, 1) - side * SIDE
    for block in range(8):
        hot[block * 128 : (block + 1) * 128, :] = ones_where(iota((128, SIDE), 1) == turned[:, block : block + 1])


def empty_kernel(*refs):
    pass


def fresh_hot(columns, side):
    return ones_where(iota((128, SIDE), 1) == columns[:, 18:19] - side * SIDE)


def put_keys(keys, span, found, factor):
    turning = found[:, LAT:]
    turning = turning + pltpu.roll(turning, 64, 1)
    turned = turning * factor + pltpu.roll(turning, 32, 1) * pltpu.roll(factor, 64, 1)
    keys[span, :LAT] = found[:, :LAT].astype(bf16)
    keys[span, LAT:] = turned[:, : KVW - LAT].astype(bf16)


def copy_in(source, target, sem):
    copy = pltpu.make_async_copy(source, target, sem)
    copy.start()
    copy.wait()


def weigh(scores, old):
    new = jnp.maximum(old, jnp.max(scores, axis=-1, keepdims=True))
    weights = jnp.exp2(scores - new)
    return new, jnp.exp2(old - new), jnp.sum(weights, axis=-1, keepdims=True), weights.astype(bf16)


def near_kernel(place, owner, slots, columns, near, hot):
    group = place[0] * 8 + place[1]

    @pl.when(place[4] == 1)
    def _():
        near[KEYS : KEYS + 128, :] = dot(fresh_hot(columns, 0), slots[...]).astype(bf16)

    def open_prompt(prompt):
        @pl.when((place[4] == 0) | (owner[prompt] == group))
        def _():
            hot_rows(hot, columns, prompt, 0)

            def open_part(part):
                near[aligned(prompt * 2 + part, 512), :] = dot(hot[aligned(part, 512), :], slots[...]).astype(bf16)

            whole_loop(2, open_part, 2)

    whole_loop(2, open_prompt)


def decode_kernel(
    place, owner, fits, near, others, columns, new_factors, factors_far, query_far, earlier_far, level_far, spare, spare_new,
    out, out_here, factors, query, earlier, level, keys, hot, highest, total, mixed, sem, in_sems, out_sems
):
    group = place[0] * 8 + place[1]
    fitting = fits[0, 0] == 1

    @pl.when(place[4] == 1)
    def _():
        loads = [
            pltpu.make_async_copy(source, target, in_sems.at[index])
            for index, (source, target) in enumerate(
                ((factors_far, factors), (query_far, query), (level_far, level), (earlier_far, earlier))
            )
        ]
        for load in loads:
            load.start()

        @pl.when(fitting)
        def _():
            span = slice(KEYS, KEYS + 128)
            found = near[span, :].astype(f32) + dot(fresh_hot(columns, 1), others[...])
            put_keys(keys, span, found, new_factors[...])

        @pl.when(jnp.logical_not(fitting))
        def _():
            copy_in(spare_new, keys.at[pl.ds(KEYS, 128)], sem)

        loads[0].wait()

        def open_prompt(prompt):
            owned = owner[prompt] == group

            @pl.when(owned & fitting)
            def _():
                hot_rows(hot, columns, prompt, 1)

                def open_part(part):
                    span = aligned(prompt * 2 + part, 512)
                    found = near[span, :].astype(f32) + dot(hot[aligned(part, 512), :], others[...])
                    put_keys(keys, span, found, factors[aligned(part, 512), :])

                whole_loop(2, open_part, 2)

            @pl.when(owned & jnp.logical_not(fitting))
            def _():
                copy_in(spare.at[pl.ds(prompt * 1024, 1024)], keys.at[pl.ds(prompt * 1024, 1024)], sem)

        whole_loop(2, open_prompt)
        for load in loads[1:]:
            load.wait()
        newest = keys[KEYS : KEYS + 128, :]

        def begin(piece):
            span = aligned(piece, 256)
            scores = dot_nt(query[span, :], newest) * base_two
            key = iota(scores.shape, 1)
            row = iota(scores.shape, 0) & 15
            allowed = ((key >> 1) == (row >> 1)) & ((key & 1) <= (row & 1))
            scores = jnp.where(allowed, scores, masked_fill)
            new, factor, summed, weights = weigh(scores, level[span, 0:1])
            mixed[span, :] = earlier[span, :].astype(f32) * factor + dot(weights, newest[:, :LAT])
            highest[span, :] = jnp.broadcast_to(new, (256, 128))
            total[span, :] = jnp.broadcast_to(factor + summed, (256, 128))

        whole_loop(4, begin, 4)

        def add_prompt(prompt):
            @pl.when(owner[prompt] == group)
            def _():
                def add_part(piece):
                    span = aligned(piece, 256)
                    some = keys[aligned(prompt, 1024), :]
                    new, factor, summed, weights = weigh(dot_nt(query[span, :], some) * base_two, highest[span, 0:1])
                    mixed[span, :] = mixed[span, :] * factor + dot(weights, some[:, :LAT])
                    highest[span, :] = jnp.broadcast_to(new, (256, 128))
                    total[span, :] = total[span, :] * factor + summed

                whole_loop(4, add_part, 4)

        whole_loop(2, add_prompt)

        def out_copy(tp):
            rows = aligned(tp, 16)
            return pltpu.make_async_copy(out_here.at[rows], out.at[rows], out_sems.at[tp])

        def tp_rows(tp):
            for head in range(8):
                rows = pl.ds(pl.multiple_of(tp * 128 + head * 16, 16), 16)
                some = mixed[rows, :] * (1.0 / total[rows, 0:1])
                out_here[aligned(tp, 16), head * LAT : (head + 1) * LAT] = some.astype(bf16)
            out_copy(tp).start()

        whole_loop(8, tp_rows, 2)
        whole_loop(8, lambda tp: out_copy(tp).wait())


def prefill_kernel(place, fits, near, others, columns, factors, query, spare, out, keys, hot, mixed, pairs, sem):
    group = place[0] * 8 + place[1]
    fitting = fits[0, 0] == 1

    @pl.when(place[4] == 0)
    def _():
        def add_prompt(prompt):
            @pl.when(fitting)
            def _():
                hot_rows(hot, columns, prompt, 1)

                def open_part(part):
                    span = aligned(part, 512)
                    found = near[aligned(prompt * 2 + part, 512), :].astype(f32) + dot(hot[span, :], others[...])
                    put_keys(keys, span, found, factors[span, :])

                whole_loop(2, open_part, 2)

            @pl.when(jnp.logical_not(fitting))
            def _():
                copy_in(spare.at[pl.ds(prompt * 1024, 1024)], keys, sem)

            span = aligned(prompt, 512)
            some = keys[...]
            scores = dot_nt(query[span, :], some) * base_two
            last = (iota((512, 1), 0) & 63) + group * 64
            scores = jnp.where(iota(scores.shape, 1) <= last, scores, masked_fill)
            _, _, summed, weights = weigh(scores, jnp.full((512, 1), masked_fill, f32))
            added = dot(weights, some[:, :LAT]) * (1.0 / summed)
            for column in range(4):
                mixed[column, span, :] = added[:, column * 128 : (column + 1) * 128]

        whole_loop(2, add_prompt)

        def head_rows(head):
            for column in range(4):
                for prompt in range(2):
                    start = pl.multiple_of(prompt * 512 + head * 64, 64)
                    pairs[column, pl.ds(prompt, 64, stride=2), :] = mixed[column, pl.ds(start, 64), :]
                out[:, pl.ds(pl.multiple_of(head * LAT + column * 128, 128), 128)] = pairs[column].astype(bf16)

        whole_loop(8, head_rows, 2)


def join_kernel(place, prefilled, turned, out, sems):
    @pl.when(place[4] == 1)
    def _():
        copies = []
        for part in range(4):
            span = pl.ds(part * 32, 32)
            copies.append(pltpu.make_async_copy(turned.at[span], out.at[span], sems.at[part]))
        for copy in copies:
            copy.start()
        for copy in copies:
            copy.wait()


def rope_factors(position):
    frequency = np.float32(rope_base) ** (-np.arange(32, dtype=np.float32) / np.float32(32))
    angles = position[:, None] * frequency[None, :]
    if isinstance(position, np.ndarray):
        angles = angles.astype(np.float32).astype(np.float64)
        cosine, sine = np.cos(angles), np.sin(angles)
        return np.concatenate([cosine, cosine, -sine, sine], axis=-1).astype(np.float32)
    cosine, sine = jnp.cos(angles), jnp.sin(angles)
    return jnp.concatenate([cosine, cosine, -sine, sine], axis=-1)


def finish_keys(latent, latent_gain, position):
    plain = latent[:, :LAT]
    scaled = plain * lax.rsqrt(jnp.mean(plain * plain, axis=-1, keepdims=True) + norm_eps) * latent_gain
    factors = rope_factors(position.astype(f32))
    rotary = latent[:, LAT:]
    swapped = jnp.concatenate([rotary[:, 32:], rotary[:, :32]], axis=-1)
    turned = rotary * factors[:, :64] + swapped * factors[:, 64:]
    return jnp.concatenate([scaled, turned], axis=-1).astype(bf16)


def dense_keys(token_ids, place, embed_table, down, latent_gain, cache_length):
    group = place[0] * 8 + place[1]
    tp_index = place[2] * 2 + place[3]
    every = lax.all_to_all(jnp.broadcast_to(token_ids, (32, 128)).reshape(32, 1, 128), HOLDERS, 0, 0, tiled=True)
    local_row = every.reshape(-1) - (group * 2 + place[4]) * 2048
    inside = (local_row >= 0) & (local_row < 2048)
    picked = jnp.take(embed_table, jnp.clip(local_row, 0, 2047), axis=0)
    picked = jnp.where(inside[:, None], picked, jnp.zeros_like(picked)).reshape(32, 128, 896)
    embedded = jnp.sum(lax.all_to_all(picked, HOLDERS, 0, 0, tiled=True).astype(f32), axis=0).astype(bf16)
    partial = dot_nt(embedded, down)
    spread = jnp.broadcast_to(partial[None], (8, 128, KVW))
    latent = jnp.sum(lax.all_to_all(spread, TP, 0, 0, tiled=True), axis=0)
    index = jnp.arange(128, dtype=jnp.int32)
    mine = finish_keys(latent, latent_gain, group * 64 + index // 2)
    spread = jnp.broadcast_to(mine[None], (32, 128, KVW))
    prompts = lax.all_to_all(spread, HOLDERS, 0, 0, tiled=True).reshape(16, 2, 64, 2, KVW)[:, 0]
    prompts = jnp.transpose(prompts, (2, 0, 1, 3)).reshape(KEYS, KVW)
    own = lax.dynamic_slice_in_dim(latent, tp_index * 16, 16, 0)
    fresh = finish_keys(own, latent_gain, (cache_length[:, None] + jnp.arange(2, dtype=jnp.int32)[None]).reshape(-1))
    return prompts, jnp.concatenate([fresh, jnp.zeros((112, KVW), bf16)], axis=0)


def in_vmem(value):
    return pltpu.with_memory_space_constraint(value, VMEM)


def in_hbm(value):
    return pltpu.with_memory_space_constraint(value, pltpu.HBM)


def params(mebibytes):
    return pltpu.CompilerParams(vmem_limit_bytes=mebibytes * 1024 * 1024)


def shards(
    token_ids,
    embed_table,
    latent_down,
    latent_gain,
    prefill_query,
    decode_query,
    latent_cache,
    cache_length,
    prompt_owner,
):
    place = jnp.stack([lax.axis_index(name) for name in ("ylo", "z", "x", "core", "role")]).astype(jnp.int32)
    down = jnp.transpose(latent_down)
    whole = pl.BlockSpec(memory_space=VMEM)
    scalars = pl.BlockSpec(memory_space=SMEM)
    anywhere = pl.BlockSpec(memory_space=pl.ANY)
    shaped = jax.ShapeDtypeStruct

    spread = pl.pallas_call(
        spread_kernel,
        out_shape=shaped((32, 1, 128), jnp.int32),
        in_specs=[whole],
        out_specs=whole,
        compiler_params=params(4),
        name="spread_ids",
    )(token_ids)
    every = lax.all_to_all(spread, HOLDERS, 0, 0, tiled=True).reshape(32, 128)

    earlier, level = pl.pallas_call(
        cache_kernel,
        grid_spec=pltpu.PrefetchScalarGridSpec(
            num_scalar_prefetch=1,
            grid=(8,),
            in_specs=[
                pl.BlockSpec((1, 128, KVW), lambda row, lengths: (row, 0, 0)),
                pl.BlockSpec((1, KVW, 512), lambda row, lengths: (row, 0, 0)),
            ],
            out_specs=[
                pl.BlockSpec((128, LAT), lambda row, lengths: (row, 0)),
                pl.BlockSpec((128, 128), lambda row, lengths: (row, 0)),
            ],
        ),
        out_shape=(pltpu.HBM((1024, LAT), bf16), pltpu.HBM((1024, 128), f32)),
        compiler_params=params(12),
        cost_estimate=pl.CostEstimate(flops=12 * 10**8, bytes_accessed=7 * 10**6, transcendentals=524288),
        name="cache_rows",
    )(cache_length, in_hbm(decode_query.reshape(8, 128, KVW)), in_hbm(jnp.swapaxes(latent_cache, 1, 2)))
    every, earlier, level = lax.optimization_barrier((every, earlier, level))

    partial = pl.pallas_call(
        select_kernel,
        out_shape=shaped((8, SLOTS, KVW), f32),
        in_specs=[scalars, whole, anywhere, anywhere],
        out_specs=whole,
        scratch_shapes=[
            VMEM((16, 4096), bf16),
            VMEM((128, 4096), bf16),
            VMEM((8 * SLOTS, 2048), bf16),
            VMEM((2048, 896), bf16),
            VMEM((KVW, 896), bf16),
            pltpu.SemaphoreType.DMA((2,)),
        ],
        compiler_params=params(16),
        cost_estimate=pl.CostEstimate(flops=3 * 10**9, bytes_accessed=5 * 10**6, transcendentals=0),
        name="select_rows",
    )(place, every, in_hbm(embed_table), in_hbm(down))
    parts = lax.all_to_all(partial, TP, 0, 0, tiled=True)

    sheet = pl.pallas_call(
        rank_kernel,
        out_shape=shaped((104, 128), jnp.int32),
        in_specs=[whole],
        out_specs=whole,
        scratch_shapes=[VMEM((512, 4096), bf16), VMEM((128, 4096), bf16)],
        compiler_params=params(18),
        cost_estimate=pl.CostEstimate(flops=2 * 10**9, bytes_accessed=10**6, transcendentals=0),
        name="rank_rows",
    )(every)
    parts, sheet = lax.optimization_barrier((parts, sheet))
    sent = pl.pallas_call(
        finish_kernel,
        out_shape=shaped((8, SLOTS, WIDE), bf16),
        in_specs=[whole, whole],
        out_specs=whole,
        compiler_params=params(8),
        name="finish_rows",
    )(parts, latent_gain.reshape(1, LAT))
    arrived = lax.all_to_all(sent, "z", 0, 0, tiled=True)

    columns, kept, fits = pl.pallas_call(
        place_kernel,
        out_shape=(shaped((128, 128), jnp.int32), shaped((8, 128), f32), shaped((1, 1), jnp.int32)),
        in_specs=[scalars, whole],
        out_specs=(whole, whole, scalars),
        scratch_shapes=[
            VMEM((128, 19 * 128), bf16),
            VMEM((128, 19 * 128), bf16),
            VMEM((16, 2048), bf16),
            VMEM((64, 2048), bf16),
            VMEM((128, 128), f32),
        ],
        compiler_params=params(12),
        cost_estimate=pl.CostEstimate(flops=10**9, bytes_accessed=10**6, transcendentals=0),
        name="place_rows",
    )(place, sheet)
    handed = pl.pallas_call(
        keep_kernel,
        out_shape=shaped((16, KEPT, WIDE), bf16),
        in_specs=[whole] * 2,
        out_specs=whole,
        compiler_params=params(8),
        name="keep_rows",
    )(kept, arrived.reshape(8 * SLOTS, WIDE))
    handed, prompt_rows, decode_rows, lengths, earlier, level = lax.optimization_barrier(
        (handed, prefill_query, decode_query, cache_length, earlier, level)
    )
    slots = lax.all_to_all(handed, PLANE, 0, 0, tiled=True).reshape(SIDE, WIDE)

    def by_head(rows):
        return jnp.transpose(rows.reshape(16, 64, -1), (1, 0, 2)).reshape(1024, -1)

    row_query, earlier, level = by_head(decode_rows), by_head(earlier), by_head(level)
    new_position = (lengths[:, None] + jnp.arange(2, dtype=jnp.int32)[None]).reshape(-1)
    new_factors = jnp.pad(rope_factors(new_position.astype(f32)), ((0, 112), (0, 0)))
    prompt_query = jnp.transpose(prompt_rows.reshape(64, 2, 8, KVW), (1, 2, 0, 3)).reshape(1024, KVW)
    slots, prompt_query, row_query, earlier, level, new_factors = lax.optimization_barrier(
        (slots, prompt_query, row_query, earlier, level, new_factors)
    )
    others = lax.ppermute(slots, "core", [(0, 1), (1, 0)])

    spare, spare_new = lax.cond(
        fits[0, 0] == 1,
        lambda *unused: tuple(
            pl.pallas_call(
                empty_kernel,
                out_shape=[shaped((KEYS, KVW), bf16), shaped((128, KVW), bf16)],
                out_specs=[anywhere] * 2,
                name="no_keys",
            )()
        ),
        dense_keys,
        token_ids,
        place,
        embed_table,
        down,
        latent_gain,
        cache_length,
    )

    near = pl.pallas_call(
        near_kernel,
        out_shape=VMEM((KEYS + 128, WIDE), bf16),
        in_specs=[scalars, scalars, whole, whole],
        out_specs=whole,
        scratch_shapes=[VMEM((1024, SIDE), bf16)],
        compiler_params=params(12),
        cost_estimate=pl.CostEstimate(flops=2 * 10**9, bytes_accessed=10**6, transcendentals=0),
        name="near_keys",
    )(place, prompt_owner, slots, columns)
    factors = jnp.asarray(rope_factors(np.arange(1024, dtype=np.float32)))
    decoded = pl.pallas_call(
        decode_kernel,
        out_shape=pltpu.HBM((128, 4096), bf16),
        in_specs=[scalars] * 3 + [whole] * 4 + [anywhere] * 6,
        out_specs=anywhere,
        scratch_shapes=[
            VMEM((128, 4096), bf16),
            VMEM((1024, 128), f32),
            VMEM((1024, KVW), bf16),
            VMEM((1024, LAT), bf16),
            VMEM((1024, 128), f32),
            VMEM((KEYS + 128, KVW), bf16),
            VMEM((1024, SIDE), bf16),
            VMEM((1024, 128), f32),
            VMEM((1024, 128), f32),
            VMEM((1024, LAT), f32),
            pltpu.SemaphoreType.DMA,
            pltpu.SemaphoreType.DMA((4,)),
            pltpu.SemaphoreType.DMA((8,)),
        ],
        compiler_params=params(24),
        cost_estimate=pl.CostEstimate(flops=5 * 10**9, bytes_accessed=7 * 10**6, transcendentals=10**6),
        name="decode_rows",
    )(
        place, prompt_owner, fits, in_vmem(near), in_vmem(others), columns, new_factors, in_hbm(factors),
        in_hbm(row_query), in_hbm(earlier), in_hbm(level), in_hbm(spare), in_hbm(spare_new),
    )
    turned = lax.all_to_all(decoded.reshape(8, 16, 4096), TP, 0, 0, tiled=True).reshape(128, 4096)
    prefilled = pl.pallas_call(
        prefill_kernel,
        out_shape=pltpu.HBM((128, 4096), bf16),
        in_specs=[scalars] * 2 + [whole] * 5 + [anywhere],
        out_specs=whole,
        scratch_shapes=[
            VMEM((1024, KVW), bf16),
            VMEM((1024, SIDE), bf16),
            VMEM((4, 1024, 128), f32),
            VMEM((4, 128, 128), f32),
            pltpu.SemaphoreType.DMA,
        ],
        compiler_params=params(20),
        cost_estimate=pl.CostEstimate(flops=7 * 10**9, bytes_accessed=7 * 10**6, transcendentals=10**6),
        name="prefill_rows",
    )(place, fits, in_vmem(near), in_vmem(others), columns, in_vmem(factors), in_vmem(prompt_query), in_hbm(spare))
    out = pl.pallas_call(
        join_kernel,
        out_shape=pltpu.HBM((128, 4096), bf16),
        in_specs=[scalars] + [anywhere] * 2,
        out_specs=anywhere,
        scratch_shapes=[pltpu.SemaphoreType.DMA((4,))],
        input_output_aliases={1: 0},
        compiler_params=params(4),
        name="join_rows",
    )(place, in_hbm(prefilled), turned)
    return out[None]


def solution(mesh):
    fine_mesh = Mesh(mesh.devices.reshape(2, 8, 4, 2, 2), ("ylo", "z", "x", "core", "role"))
    ctx, tp = ("ylo", "z"), ("x", "core")
    in_specs = (
        P("role", ctx),
        P(ctx + ("role",), tp),
        P(tp, None),
        P(),
        P(ctx, tp, None),
        P(ctx + tp, None, None, None),
        P(ctx + tp, None, None),
        P(ctx + tp),
        P(),
    )
    out_specs = P("role", ctx, tp)
    return jax.shard_map(shards, mesh=fine_mesh, in_specs=in_specs, out_specs=out_specs, check_vma=False)
```

```python
import jax
import jax.numpy as jnp
import numpy as np
from jax import lax
from jax.experimental import pallas as pl
from jax.experimental.pallas import tpu as pltpu
from jax.sharding import Mesh
from jax.sharding import PartitionSpec as P

LAT = 512
KVW = 576
STEPS = 2
WIDE = 640
SLOTS = 16
KEPT = 48
SIDE = 16 * KEPT
KEYS = 2048

score_scale = 0.07216878364870322
base_two = score_scale * 1.4426950408889634
masked_fill = -1e30
norm_eps = 1e-06
rope_base = 10000.0
bf16 = jnp.bfloat16
f32 = jnp.float32
SMEM = pltpu.SMEM
VMEM = pltpu.VMEM

HOLDERS = ("ylo", "z", "role")
PLANE = ("ylo", "role", "x")
TP = ("x", "core")


def iota(shape, axis):
    return lax.broadcasted_iota(jnp.int32, shape, axis)


def ones_where(flags):
    return jnp.where(flags, 1.0, 0.0).astype(bf16)


def dot(left, right):
    return lax.dot_general(left, right, (((1,), (0,)), ((), ())), preferred_element_type=f32)


def dot_nt(left, right):
    return lax.dot_general(left, right, (((1,), (1,)), ((), ())), preferred_element_type=f32)


def whole_loop(count, body, unroll=1):
    def step(index, carry):
        body(index)
        return carry

    lax.fori_loop(0, count, step, 0, unroll=unroll)


def aligned(index, size):
    return pl.ds(pl.multiple_of(index * size, size), size)


def spread_kernel(ids, out):
    out[...] = jnp.broadcast_to(ids[...].reshape(1, 1, 128), out.shape)


def select_kernel(place, ids, table, down, partial, hots, lows, chosen, table_here, down_here, sems):
    holder = (place[0] * 8 + place[1]) * 2 + place[4]
    table_copy = pltpu.make_async_copy(table, table_here, sems.at[0])
    down_copy = pltpu.make_async_copy(down, down_here, sems.at[1])
    table_copy.start()
    down_copy.start()

    def mark(line):
        tokens = ids[pl.ds(line, 1), :]
        span = aligned((line & 1) * 16 + (line >> 1), 128)
        hots[:, span] = ones_where(iota((16, 128), 0) == (tokens >> 7) - holder * 16)
        lows[:, span] = ones_where(iota((128, 128), 0) == (tokens & 127))

    whole_loop(32, mark, 8)
    in_prompt = dot_nt(hots[:, :KEYS], lows[:, :KEYS]) > 0.5
    alone = (dot_nt(hots[:, KEYS:], lows[:, KEYS:]) > 0.5) & jnp.logical_not(in_prompt)
    upper = ones_where(iota((128, 128), 0) < iota((128, 128), 1))
    all_ones = jnp.ones((128, 128), bf16)
    row = iota((8 * SLOTS, 128), 0)
    wanted = ((row & 15) * 8 + (((row >> 4) - holder) & 7)).astype(f32)
    before = jnp.zeros((1, 128), f32)
    ranks = []
    for present in (in_prompt, alone):
        flags = ones_where(present)
        within = dot(flags, upper)
        totals = dot(flags, all_ones)
        lines = []
        for step in range(16):
            lines.append(within[step : step + 1, :] + before)
            before = before + totals[step : step + 1, :]
        ranks.append(lines)
    for step in range(16):
        rank = jnp.where(alone[step : step + 1, :], ranks[1][step], -1.0)
        rank = jnp.where(in_prompt[step : step + 1, :], ranks[0][step], rank)
        chosen[:, step * 128 : (step + 1) * 128] = ones_where(wanted == rank)
    table_copy.wait()
    rows = dot(chosen[...], table_here[...]).astype(bf16)
    down_copy.wait()
    partial[...] = dot_nt(rows, down_here[...]).reshape(partial.shape)


def rank_kernel(ids, sheet, highs, lows):
    square = (128, 128)
    lane = iota((8, 128), 1)
    sheet[0:16, :] = ids[pl.ds(0, 16, stride=2), :]
    sheet[16:32, :] = ids[pl.ds(1, 16, stride=2), :]
    target = iota(square, 1)
    mover = ones_where(iota(square, 0) == jnp.where(target < 64, 2 * target, 2 * target - 127))
    plain = sheet[0:16, :]
    decode_tokens = sheet[16:32, :]
    coarse = (plain >> 8).astype(f32).astype(bf16)
    fine = (plain & 255).astype(f32).astype(bf16)
    moved = dot(coarse, mover) * 256.0 + dot(fine, mover)
    sheet[0:16, :] = moved.astype(jnp.int32)
    even = sheet[pl.ds(0, 8, stride=2), :]
    odd = sheet[pl.ds(1, 8, stride=2), :]
    first = jnp.where(lane < 64, even, pltpu.roll(odd, 64, 1))
    second = jnp.where(lane < 64, pltpu.roll(even, 64, 1), odd)
    tokens = jnp.concatenate([first, second, decode_tokens], axis=0)
    sheet[0:32, :] = tokens

    def mark(block):
        line = sheet[pl.ds(block, 1), :]
        span = aligned(block, 128)
        highs[:, span] = ones_where(iota((512, 128), 0) == (line >> 7))
        lows[:, span] = ones_where(iota(square, 0) == (line & 127))

    whole_loop(32, mark, 8)
    in_prompt = dot_nt(lows[:, :KEYS], highs[:, :KEYS]) > 0.5
    alone = (dot_nt(lows[:, KEYS:], highs[:, KEYS:]) > 0.5) & jnp.logical_not(in_prompt)
    below = ones_where(iota(square, 1) < iota(square, 0))
    all_ones = jnp.ones(square, bf16)
    wide = (512, 512)
    same = (iota(wide, 0) >> 4) == (iota(wide, 1) >> 4)
    in_holder = ones_where(same & (iota(wide, 0) < iota(wide, 1)))
    prompt_flags = ones_where(in_prompt)
    alone_flags = ones_where(alone)
    prompt_columns = dot(all_ones, prompt_flags).astype(bf16)
    alone_columns = dot(all_ones, alone_flags).astype(bf16)
    prompt_rank = dot(below, prompt_flags) + dot(prompt_columns, in_holder)
    alone_rank = (
        dot(below, alone_flags) + dot(alone_columns, in_holder) + dot(prompt_columns, ones_where(same))
    )
    rank = jnp.where(in_prompt, prompt_rank, jnp.where(alone, alone_rank, 0.0))
    top_rank = jnp.max(jnp.max(rank, axis=0, keepdims=True), axis=1, keepdims=True).astype(jnp.int32)
    coded = (jnp.minimum(rank, 127.0) + jnp.where(in_prompt, 128.0, 0.0)).astype(bf16)
    pieces = []
    for chunk in range(4):
        span = slice(chunk * 1024, (chunk + 1) * 1024)
        looked = dot(coded, highs[:, span]) * lows[:, span].astype(f32)
        line = jnp.sum(looked, axis=0, keepdims=True)
        for part in range(8):
            pieces.append(line[:, part * 128 : (part + 1) * 128])
    value = jnp.concatenate(pieces, axis=0).astype(jnp.int32)
    ranks = value & 127
    holder = tokens >> 11
    tp_of = (ranks + holder) & 7
    quad = tp_of * 16 + (ranks >> 3)
    sheet[0:32, :] = quad
    sheet[32:64, :] = holder
    sheet[64:96, :] = jnp.where(value >= 128, -1, tp_of)
    sheet[96:104, :] = jnp.broadcast_to(top_rank, (8, 128))


def place_kernel(place, sheet, columns, kept, fits, quads, holders, hot_tp, hot_pool, sheet_b):
    ylo, zed, ex, core, section = place[0], place[1], place[2], place[3], place[4]
    square = (128, 128)

    def spot(block, source):
        span = aligned(block, 128)
        quads[:, span] = ones_where(iota(square, 0) == sheet[pl.ds(source, 1), :])
        holders[:, span] = ones_where(iota(square, 0) == sheet[pl.ds(source + 32, 1), :])

    whole_loop(16, lambda block: spot(block, block), 8)
    for part in range(2):
        spot(16 + part, 16 + part * 8 + zed)
    own = 16 + ylo * 8 + zed
    spot(18, own)
    up, down = iota(square, 0), iota(square, 1)
    same_tp = (up >> 4) == (down >> 4)
    same_pool = ((up >> 4) == (down >> 4)) & ((up & 1) == (down & 1))
    tp_ones = ones_where(same_tp)
    pool = ones_where(same_pool)
    before = ones_where(same_pool & (up < down))
    in_tp = ones_where(same_tp & (down < up))
    held = dot_nt(quads[:, :KEYS], holders[:, :KEYS]) > 0.5
    flags = ones_where(held)
    sums = dot(tp_ones, flags).astype(bf16)
    prompt_position = dot(in_tp, flags) + dot(sums, before)
    prompt_count = dot(sums, pool)
    positions = []
    for part in range(2):
        span = slice(KEYS + part * 128, KEYS + (part + 1) * 128)
        added = (dot_nt(quads[:, span], holders[:, span]) > 0.5) & jnp.logical_not(held)
        added_flags = ones_where(added)
        added_sums = dot(tp_ones, added_flags).astype(bf16)
        spots = dot(in_tp, added_flags) + dot(added_sums, before) + prompt_count
        spots = jnp.where(held, prompt_position, jnp.where(added, spots, 255.0))
        positions.append(jnp.minimum(spots, 255.0))
    position = jnp.where(ylo == 0, positions[0], positions[1])

    def pick(block):
        span = aligned(block, 128)
        hot_tp[:, span] = ones_where(iota((16, 128), 0) == sheet[pl.ds(block + 80, 1), :])
        line = sheet[pl.ds(block + 48, 1), :]
        line = ((line >> 4) * 2 + (line & 1)) + 4 * block
        hot_pool[:, span] = ones_where(iota((64, 128), 0) == line)

    whole_loop(16, pick, 8)
    gather_tp = ones_where(iota((16, 128), 0) == (iota((16, 128), 1) >> 4))
    base = dot(gather_tp, flags).astype(bf16)
    holder, column = iota((128, 64), 0), iota((128, 64), 1)
    pooled = ones_where((holder < 32) & (((holder >> 4) * 2 + (holder & 1)) == (column & 3)))
    needed = dot_nt(hot_tp[...], hot_pool[...]) + dot(base, pooled)
    needed = jnp.max(jnp.max(needed, axis=0, keepdims=True), axis=1, keepdims=True)
    enough = (sheet[96:97, 0:1] < 8 * SLOTS) & (needed <= float(KEPT))
    fits[0, 0] = jnp.max(jnp.where(enough, 1, 0))

    looked = dot(position.astype(bf16), holders[...]) * quads[...].astype(f32)
    line = jnp.sum(looked, axis=0, keepdims=True)
    found = [line[:, block * 128 : (block + 1) * 128] for block in range(19)]
    found = jnp.concatenate(found + [jnp.zeros((5, 128), f32)], axis=0)
    blank = jnp.zeros((5, 128), jnp.int32)
    quad_rows = jnp.concatenate([sheet[0:16, :], blank[:2], sheet[pl.ds(own, 1), :], blank], axis=0)
    holder_rows = jnp.concatenate([sheet[32:48, :], blank[:2], sheet[pl.ds(own + 32, 1), :], blank], axis=0)
    tp_rows = quad_rows >> 4
    source = ((holder_rows >> 4) * 2 + (holder_rows & 1)) * 4 + (tp_rows >> 1)
    side = jnp.where((tp_rows & 1) == core, 0, SIDE)
    final = found + (source * KEPT + side).astype(f32)
    tp_index = ex * 2 + core
    turned = pltpu.roll(final, (128 - tp_index * 16) % 128, 1)
    turned = jnp.where(iota((24, 128), 1) < 16, turned, -1.0)
    final = jnp.where(iota((24, 128), 0) == 18, turned, final)
    final = jnp.concatenate([final, jnp.zeros((104, 128), f32)], axis=0)
    columns[...] = jnp.transpose(final).astype(jnp.int32)
    few = (16, 128)
    for part in range(2):
        sheet_b[...] = positions[part]
        mine = sheet_b[pl.ds(pl.multiple_of(tp_index * 16, 16), 16), :].astype(bf16)
        spread = dot(mine, ones_where(up == (ylo * 8 + (down >> 4)) * 2 + section))
        spread = jnp.where((iota(few, 1) & 15) == iota(few, 0), spread, 0.0)
        kept[part : part + 1, :] = jnp.sum(spread, axis=0, keepdims=True)


def finish_kernel(parts, gain, sent):
    latent = parts[0]
    for tp in range(1, parts.shape[0]):
        latent = latent + parts[tp]
    plain = latent[:, :LAT]
    scaled = plain * lax.rsqrt(jnp.mean(plain * plain, axis=-1, keepdims=True) + norm_eps) * gain[...]
    rotary = latent[:, LAT:]
    coarse = rotary.astype(bf16)
    fine = (rotary - coarse.astype(f32)).astype(bf16)
    row = jnp.concatenate([scaled.astype(bf16), coarse, fine], axis=-1)
    for peer in range(sent.shape[0]):
        sent[peer] = row


def keep_kernel(kept, rows, sent):
    for ylo in range(2):
        chosen = iota((KEPT, 128), 0).astype(f32) == kept[ylo : ylo + 1, :]
        row = dot(ones_where(chosen), rows[...]).astype(bf16)
        for peer in range(8):
            sent[ylo * 8 + peer] = row


def cache_kernel(lengths, query, cache, out, level):
    length = lengths[pl.program_id(0)]
    scores = dot(query[0], cache[0]) * base_two
    scores = jnp.where(iota(scores.shape, 1) < length, scores, masked_fill)
    highest = jnp.max(scores, axis=-1, keepdims=True)
    weights = jnp.exp2(scores - highest)
    total = jnp.sum(weights, axis=-1, keepdims=True)
    out[...] = (dot_nt(weights.astype(bf16), cache[0, :LAT, :]) * (1.0 / total)).astype(bf16)
    level[...] = jnp.broadcast_to(highest + jnp.log2(total), level.shape)


def hot_rows(hot, columns, prompt, side, part):
    turned = pltpu.roll(columns[...], (128 - prompt * 8) % 128, 1) - side * SIDE
    for block in range(part * 4, part * 4 + 4):
        hot[block * 128 : (block + 1) * 128, :] = ones_where(iota((128, SIDE), 1) == turned[:, block : block + 1])
    return hot[part * 512 : (part + 1) * 512, :]


def fresh_hot(columns, side):
    return ones_where(iota((128, SIDE), 1) == columns[:, 18:19] - side * SIDE)


def empty_kernel(*refs):
    pass


def fresh_hot(columns, side):
    return ones_where(iota((128, SIDE), 1) == columns[:, 18:19] - side * SIDE)


def put_keys(keys, span, found, factor):
    turning = found[:, LAT:]
    turning = turning + pltpu.roll(turning, 64, 1)
    turned = turning * factor + pltpu.roll(turning, 32, 1) * pltpu.roll(factor, 64, 1)
    keys[span, :LAT] = found[:, :LAT].astype(bf16)
    keys[span, LAT:] = turned[:, : KVW - LAT].astype(bf16)


def copy_in(source, target, sem):
    copy = pltpu.make_async_copy(source, target, sem)
    copy.start()
    copy.wait()


def weigh(scores, old):
    new = jnp.maximum(old, jnp.max(scores, axis=-1, keepdims=True))
    weights = jnp.exp2(scores - new)
    return new, jnp.exp2(old - new), jnp.sum(weights, axis=-1, keepdims=True), weights.astype(bf16)


def near_kernel(place, owner, slots, columns, near, hot):
    group = place[0] * 8 + place[1]

    @pl.when(place[4] == 1)
    def _():
        near[KEYS : KEYS + 128, :] = dot(fresh_hot(columns, 0), slots[...]).astype(bf16)

    def open_prompt(prompt):
        @pl.when((place[4] == 0) | (owner[prompt] == group))
        def _():
            for part in range(2):
                some = hot_rows(hot, columns, prompt, 0, part)
                near[aligned(prompt * 2 + part, 512), :] = dot(some, slots[...]).astype(bf16)

    whole_loop(2, open_prompt)


def decode_kernel(
    place, owner, fits, near, others, columns, new_factors, factors_far, query_far, earlier_far, level_far, spare, spare_new,
    out, out_here, factors, query, earlier, level, keys, hot, highest, total, mixed, sem, in_sems, out_sems
):
    group = place[0] * 8 + place[1]
    fitting = fits[0, 0] == 1

    @pl.when(place[4] == 1)
    def _():
        loads = [
            pltpu.make_async_copy(source, target, in_sems.at[index])
            for index, (source, target) in enumerate(
                ((factors_far, factors), (query_far, query), (level_far, level), (earlier_far, earlier))
            )
        ]
        for load in loads:
            load.start()

        span = slice(KEYS, KEYS + 128)
        found = near[span, :].astype(f32) + dot(fresh_hot(columns, 1), others[...])
        put_keys(keys, span, found, new_factors[...])
        loads[0].wait()

        def open_prompt(prompt):
            @pl.when(owner[prompt] == group)
            def _():
                for part in range(2):
                    span = aligned(prompt * 2 + part, 512)
                    found = near[span, :].astype(f32) + dot(hot_rows(hot, columns, prompt, 1, part), others[...])
                    put_keys(keys, span, found, factors[part * 512 : (part + 1) * 512, :])

        whole_loop(2, open_prompt)

        @pl.when(jnp.logical_not(fitting))
        def _():
            copy_in(spare, keys.at[pl.ds(0, KEYS)], sem)
            copy_in(spare_new, keys.at[pl.ds(KEYS, 128)], sem)

        for load in loads[1:]:
            load.wait()
        newest = keys[KEYS : KEYS + 128, :]

        def begin(piece):
            span = aligned(piece, 256)
            scores = dot_nt(query[span, :], newest) * base_two
            key = iota(scores.shape, 1)
            row = iota(scores.shape, 0) & 15
            allowed = ((key >> 1) == (row >> 1)) & ((key & 1) <= (row & 1))
            scores = jnp.where(allowed, scores, masked_fill)
            new, factor, summed, weights = weigh(scores, level[span, 0:1])
            mixed[span, :] = earlier[span, :].astype(f32) * factor + dot(weights, newest[:, :LAT])
            highest[span, :] = jnp.broadcast_to(new, (256, 128))
            total[span, :] = jnp.broadcast_to(factor + summed, (256, 128))

        whole_loop(4, begin, 4)

        def add_prompt(prompt):
            @pl.when(owner[prompt] == group)
            def _():
                def add_part(piece):
                    span = aligned(piece, 256)
                    some = keys[aligned(prompt, 1024), :]
                    new, factor, summed, weights = weigh(dot_nt(query[span, :], some) * base_two, highest[span, 0:1])
                    mixed[span, :] = mixed[span, :] * factor + dot(weights, some[:, :LAT])
                    highest[span, :] = jnp.broadcast_to(new, (256, 128))
                    total[span, :] = total[span, :] * factor + summed

                whole_loop(4, add_part, 4)

        whole_loop(2, add_prompt)

        def out_copy(tp):
            rows = aligned(tp, 16)
            return pltpu.make_async_copy(out_here.at[rows], out.at[rows], out_sems.at[tp])

        def tp_rows(tp):
            for head in range(8):
                rows = pl.ds(pl.multiple_of(tp * 128 + head * 16, 16), 16)
                some = mixed[rows, :] * (1.0 / total[rows, 0:1])
                out_here[aligned(tp, 16), head * LAT : (head + 1) * LAT] = some.astype(bf16)
            out_copy(tp).start()

        whole_loop(8, tp_rows, 2)
        whole_loop(8, lambda tp: out_copy(tp).wait())


def prefill_kernel(place, fits, near, others, columns, factors, query, spare, out, keys, hot, mixed, pairs, sem):
    group = place[0] * 8 + place[1]
    fitting = fits[0, 0] == 1

    @pl.when(place[4] == 0)
    def _():
        def add_prompt(prompt):
            for part in range(2):
                span = slice(part * 512, (part + 1) * 512)
                found = near[aligned(prompt * 2 + part, 512), :].astype(f32)
                found = found + dot(hot_rows(hot, columns, prompt, 1, part), others[...])
                put_keys(keys, span, found, factors[span, :])

            @pl.when(jnp.logical_not(fitting))
            def _():
                copy_in(spare.at[pl.ds(prompt * 1024, 1024)], keys, sem)

            span = aligned(prompt, 512)
            some = keys[...]
            scores = dot_nt(query[span, :], some) * base_two
            last = (iota((512, 1), 0) & 63) + group * 64
            scores = jnp.where(iota(scores.shape, 1) <= last, scores, masked_fill)
            _, _, summed, weights = weigh(scores, jnp.full((512, 1), masked_fill, f32))
            added = dot(weights, some[:, :LAT]) * (1.0 / summed)
            for column in range(4):
                mixed[column, span, :] = added[:, column * 128 : (column + 1) * 128]

        whole_loop(2, add_prompt)

        def head_rows(head):
            for column in range(4):
                for prompt in range(2):
                    start = pl.multiple_of(prompt * 512 + head * 64, 64)
                    pairs[column, pl.ds(prompt, 64, stride=2), :] = mixed[column, pl.ds(start, 64), :]
                out[:, pl.ds(pl.multiple_of(head * LAT + column * 128, 128), 128)] = pairs[column].astype(bf16)

        whole_loop(8, head_rows, 2)


def join_kernel(place, prefilled, turned, out, sems):
    @pl.when(place[4] == 1)
    def _():
        copies = []
        for part in range(4):
            span = pl.ds(part * 32, 32)
            copies.append(pltpu.make_async_copy(turned.at[span], out.at[span], sems.at[part]))
        for copy in copies:
            copy.start()
        for copy in copies:
            copy.wait()


def rope_factors(position):
    frequency = np.float32(rope_base) ** (-np.arange(32, dtype=np.float32) / np.float32(32))
    angles = position[:, None] * frequency[None, :]
    if isinstance(position, np.ndarray):
        angles = angles.astype(np.float32).astype(np.float64)
        cosine, sine = np.cos(angles), np.sin(angles)
        return np.concatenate([cosine, cosine, -sine, sine], axis=-1).astype(np.float32)
    cosine, sine = jnp.cos(angles), jnp.sin(angles)
    return jnp.concatenate([cosine, cosine, -sine, sine], axis=-1)


def finish_keys(latent, latent_gain, position):
    plain = latent[:, :LAT]
    scaled = plain * lax.rsqrt(jnp.mean(plain * plain, axis=-1, keepdims=True) + norm_eps) * latent_gain
    factors = rope_factors(position.astype(f32))
    rotary = latent[:, LAT:]
    swapped = jnp.concatenate([rotary[:, 32:], rotary[:, :32]], axis=-1)
    turned = rotary * factors[:, :64] + swapped * factors[:, 64:]
    return jnp.concatenate([scaled, turned], axis=-1).astype(bf16)


def dense_keys(token_ids, place, embed_table, down, latent_gain, cache_length):
    group = place[0] * 8 + place[1]
    tp_index = place[2] * 2 + place[3]
    every = lax.all_to_all(jnp.broadcast_to(token_ids, (32, 128)).reshape(32, 1, 128), HOLDERS, 0, 0, tiled=True)
    local_row = every.reshape(-1) - (group * 2 + place[4]) * 2048
    inside = (local_row >= 0) & (local_row < 2048)
    picked = jnp.take(embed_table, jnp.clip(local_row, 0, 2047), axis=0)
    picked = jnp.where(inside[:, None], picked, jnp.zeros_like(picked)).reshape(32, 128, 896)
    embedded = jnp.sum(lax.all_to_all(picked, HOLDERS, 0, 0, tiled=True).astype(f32), axis=0).astype(bf16)
    partial = dot_nt(embedded, down)
    spread = jnp.broadcast_to(partial[None], (8, 128, KVW))
    latent = jnp.sum(lax.all_to_all(spread, TP, 0, 0, tiled=True), axis=0)
    index = jnp.arange(128, dtype=jnp.int32)
    mine = finish_keys(latent, latent_gain, group * 64 + index // 2)
    spread = jnp.broadcast_to(mine[None], (32, 128, KVW))
    prompts = lax.all_to_all(spread, HOLDERS, 0, 0, tiled=True).reshape(16, 2, 64, 2, KVW)[:, 0]
    prompts = jnp.transpose(prompts, (2, 0, 1, 3)).reshape(KEYS, KVW)
    own = lax.dynamic_slice_in_dim(latent, tp_index * 16, 16, 0)
    fresh = finish_keys(own, latent_gain, (cache_length[:, None] + jnp.arange(2, dtype=jnp.int32)[None]).reshape(-1))
    return prompts, jnp.concatenate([fresh, jnp.zeros((112, KVW), bf16)], axis=0)


def in_vmem(value):
    return pltpu.with_memory_space_constraint(value, VMEM)


def in_hbm(value):
    return pltpu.with_memory_space_constraint(value, pltpu.HBM)


def params(mebibytes):
    return pltpu.CompilerParams(vmem_limit_bytes=mebibytes * 1024 * 1024)


def shards(
    token_ids,
    embed_table,
    latent_down,
    latent_gain,
    prefill_query,
    decode_query,
    latent_cache,
    cache_length,
    prompt_owner,
):
    place = jnp.stack([lax.axis_index(name) for name in ("ylo", "z", "x", "core", "role")]).astype(jnp.int32)
    down = jnp.transpose(latent_down)
    whole = pl.BlockSpec(memory_space=VMEM)
    scalars = pl.BlockSpec(memory_space=SMEM)
    anywhere = pl.BlockSpec(memory_space=pl.ANY)
    shaped = jax.ShapeDtypeStruct

    spread = pl.pallas_call(
        spread_kernel,
        out_shape=shaped((32, 1, 128), jnp.int32),
        in_specs=[whole],
        out_specs=whole,
        compiler_params=params(4),
        name="spread_ids",
    )(token_ids)
    every = lax.all_to_all(spread, HOLDERS, 0, 0, tiled=True).reshape(32, 128)

    earlier, level = pl.pallas_call(
        cache_kernel,
        grid_spec=pltpu.PrefetchScalarGridSpec(
            num_scalar_prefetch=1,
            grid=(8,),
            in_specs=[
                pl.BlockSpec((1, 128, KVW), lambda row, lengths: (row, 0, 0)),
                pl.BlockSpec((1, KVW, 512), lambda row, lengths: (row, 0, 0)),
            ],
            out_specs=[
                pl.BlockSpec((128, LAT), lambda row, lengths: (row, 0)),
                pl.BlockSpec((128, 128), lambda row, lengths: (row, 0)),
            ],
        ),
        out_shape=(pltpu.HBM((1024, LAT), bf16), pltpu.HBM((1024, 128), f32)),
        compiler_params=params(12),
        cost_estimate=pl.CostEstimate(flops=12 * 10**8, bytes_accessed=7 * 10**6, transcendentals=524288),
        name="cache_rows",
    )(cache_length, in_hbm(decode_query.reshape(8, 128, KVW)), in_hbm(jnp.swapaxes(latent_cache, 1, 2)))
    every, earlier, level = lax.optimization_barrier((every, earlier, level))

    partial = pl.pallas_call(
        select_kernel,
        out_shape=shaped((8, SLOTS, KVW), f32),
        in_specs=[scalars, whole, anywhere, anywhere],
        out_specs=whole,
        scratch_shapes=[
            VMEM((16, 4096), bf16),
            VMEM((128, 4096), bf16),
            VMEM((8 * SLOTS, 2048), bf16),
            VMEM((2048, 896), bf16),
            VMEM((KVW, 896), bf16),
            pltpu.SemaphoreType.DMA((2,)),
        ],
        compiler_params=params(16),
        cost_estimate=pl.CostEstimate(flops=3 * 10**9, bytes_accessed=5 * 10**6, transcendentals=0),
        name="select_rows",
    )(place, every, in_hbm(embed_table), in_hbm(down))
    parts = lax.all_to_all(partial, TP, 0, 0, tiled=True)

    sheet = pl.pallas_call(
        rank_kernel,
        out_shape=shaped((104, 128), jnp.int32),
        in_specs=[whole],
        out_specs=whole,
        scratch_shapes=[VMEM((512, 4096), bf16), VMEM((128, 4096), bf16)],
        compiler_params=params(18),
        cost_estimate=pl.CostEstimate(flops=2 * 10**9, bytes_accessed=10**6, transcendentals=0),
        name="rank_rows",
    )(every)
    parts, sheet = lax.optimization_barrier((parts, sheet))
    sent = pl.pallas_call(
        finish_kernel,
        out_shape=shaped((8, SLOTS, WIDE), bf16),
        in_specs=[whole, whole],
        out_specs=whole,
        compiler_params=params(8),
        name="finish_rows",
    )(parts, latent_gain.reshape(1, LAT))
    arrived = lax.all_to_all(sent, "z", 0, 0, tiled=True)

    columns, kept, fits = pl.pallas_call(
        place_kernel,
        out_shape=(shaped((128, 128), jnp.int32), shaped((8, 128), f32), shaped((1, 1), jnp.int32)),
        in_specs=[scalars, whole],
        out_specs=(whole, whole, scalars),
        scratch_shapes=[
            VMEM((128, 19 * 128), bf16),
            VMEM((128, 19 * 128), bf16),
            VMEM((16, 2048), bf16),
            VMEM((64, 2048), bf16),
            VMEM((128, 128), f32),
        ],
        compiler_params=params(12),
        cost_estimate=pl.CostEstimate(flops=10**9, bytes_accessed=10**6, transcendentals=0),
        name="place_rows",
    )(place, sheet)
    handed = pl.pallas_call(
        keep_kernel,
        out_shape=shaped((16, KEPT, WIDE), bf16),
        in_specs=[whole] * 2,
        out_specs=whole,
        compiler_params=params(8),
        name="keep_rows",
    )(kept, arrived.reshape(8 * SLOTS, WIDE))
    handed, prompt_rows, decode_rows, lengths, earlier, level = lax.optimization_barrier(
        (handed, prefill_query, decode_query, cache_length, earlier, level)
    )
    slots = lax.all_to_all(handed, PLANE, 0, 0, tiled=True).reshape(SIDE, WIDE)

    def by_head(rows):
        return jnp.transpose(rows.reshape(16, 64, -1), (1, 0, 2)).reshape(1024, -1)

    row_query, earlier, level = by_head(decode_rows), by_head(earlier), by_head(level)
    new_position = (lengths[:, None] + jnp.arange(2, dtype=jnp.int32)[None]).reshape(-1)
    new_factors = jnp.pad(rope_factors(new_position.astype(f32)), ((0, 112), (0, 0)))
    prompt_query = jnp.transpose(prompt_rows.reshape(64, 2, 8, KVW), (1, 2, 0, 3)).reshape(1024, KVW)
    slots, prompt_query, row_query, earlier, level, new_factors = lax.optimization_barrier(
        (slots, prompt_query, row_query, earlier, level, new_factors)
    )
    others = lax.ppermute(slots, "core", [(0, 1), (1, 0)])

    spare, spare_new = lax.cond(
        fits[0, 0] == 1,
        lambda *unused: tuple(
            pl.pallas_call(
                empty_kernel,
                out_shape=[shaped((KEYS, KVW), bf16), shaped((128, KVW), bf16)],
                out_specs=[anywhere] * 2,
                name="no_keys",
            )()
        ),
        dense_keys,
        token_ids,
        place,
        embed_table,
        down,
        latent_gain,
        cache_length,
    )

    near = pl.pallas_call(
        near_kernel,
        out_shape=VMEM((KEYS + 128, WIDE), bf16),
        in_specs=[scalars, scalars, whole, whole],
        out_specs=whole,
        scratch_shapes=[VMEM((1024, SIDE), bf16)],
        compiler_params=params(12),
        cost_estimate=pl.CostEstimate(flops=2 * 10**9, bytes_accessed=10**6, transcendentals=0),
        name="near_keys",
    )(place, prompt_owner, slots, columns)
    factors = jnp.asarray(rope_factors(np.arange(1024, dtype=np.float32)))
    decoded = pl.pallas_call(
        decode_kernel,
        out_shape=pltpu.HBM((128, 4096), bf16),
        in_specs=[scalars] * 3 + [whole] * 4 + [anywhere] * 6,
        out_specs=anywhere,
        scratch_shapes=[
            VMEM((128, 4096), bf16),
            VMEM((1024, 128), f32),
            VMEM((1024, KVW), bf16),
            VMEM((1024, LAT), bf16),
            VMEM((1024, 128), f32),
            VMEM((KEYS + 128, KVW), bf16),
            VMEM((1024, SIDE), bf16),
            VMEM((1024, 128), f32),
            VMEM((1024, 128), f32),
            VMEM((1024, LAT), f32),
            pltpu.SemaphoreType.DMA,
            pltpu.SemaphoreType.DMA((4,)),
            pltpu.SemaphoreType.DMA((8,)),
        ],
        compiler_params=params(24),
        cost_estimate=pl.CostEstimate(flops=5 * 10**9, bytes_accessed=7 * 10**6, transcendentals=10**6),
        name="decode_rows",
    )(
        place, prompt_owner, fits, in_vmem(near), in_vmem(others), columns, new_factors, in_hbm(factors),
        in_hbm(row_query), in_hbm(earlier), in_hbm(level), in_hbm(spare), in_hbm(spare_new),
    )
    turned = lax.all_to_all(decoded.reshape(8, 16, 4096), TP, 0, 0, tiled=True).reshape(128, 4096)
    prefilled = pl.pallas_call(
        prefill_kernel,
        out_shape=pltpu.HBM((128, 4096), bf16),
        in_specs=[scalars] * 2 + [whole] * 5 + [anywhere],
        out_specs=whole,
        scratch_shapes=[
            VMEM((1024, KVW), bf16),
            VMEM((1024, SIDE), bf16),
            VMEM((4, 1024, 128), f32),
            VMEM((4, 128, 128), f32),
            pltpu.SemaphoreType.DMA,
        ],
        compiler_params=params(20),
        cost_estimate=pl.CostEstimate(flops=7 * 10**9, bytes_accessed=7 * 10**6, transcendentals=10**6),
        name="prefill_rows",
    )(place, fits, in_vmem(near), in_vmem(others), columns, in_vmem(factors), in_vmem(prompt_query), in_hbm(spare))
    out = pl.pallas_call(
        join_kernel,
        out_shape=pltpu.HBM((128, 4096), bf16),
        in_specs=[scalars] + [anywhere] * 2,
        out_specs=anywhere,
        scratch_shapes=[pltpu.SemaphoreType.DMA((4,))],
        input_output_aliases={1: 0},
        compiler_params=params(4),
        name="join_rows",
    )(place, in_hbm(prefilled), turned)
    return out[None]


def solution(mesh):
    fine_mesh = Mesh(mesh.devices.reshape(2, 8, 4, 2, 2), ("ylo", "z", "x", "core", "role"))
    ctx, tp = ("ylo", "z"), ("x", "core")
    in_specs = (
        P("role", ctx),
        P(ctx + ("role",), tp),
        P(tp, None),
        P(),
        P(ctx, tp, None),
        P(ctx + tp, None, None, None),
        P(ctx + tp, None, None),
        P(ctx + tp),
        P(),
    )
    out_specs = P("role", ctx, tp)
    return jax.shard_map(shards, mesh=fine_mesh, in_specs=in_specs, out_specs=out_specs, check_vma=False)
```

```python
import jax
import jax.numpy as jnp
import numpy as np
from jax import lax
from jax.experimental import pallas as pl
from jax.experimental.pallas import tpu as pltpu
from jax.sharding import Mesh
from jax.sharding import PartitionSpec as P

LAT = 512
KVW = 576
STEPS = 2
WIDE = 640
SLOTS = 16
KEPT = 48
SIDE = 16 * KEPT
KEYS = 2048

score_scale = 0.07216878364870322
base_two = score_scale * 1.4426950408889634
masked_fill = -1e30
norm_eps = 1e-06
rope_base = 10000.0
bf16 = jnp.bfloat16
f32 = jnp.float32
SMEM = pltpu.SMEM
VMEM = pltpu.VMEM

HOLDERS = ("ylo", "z", "role")
PLANE = ("ylo", "role", "x")
TP = ("x", "core")


def iota(shape, axis):
    return lax.broadcasted_iota(jnp.int32, shape, axis)


def ones_where(flags):
    return jnp.where(flags, 1.0, 0.0).astype(bf16)


def dot(left, right):
    return lax.dot_general(left, right, (((1,), (0,)), ((), ())), preferred_element_type=f32)


def dot_nt(left, right):
    return lax.dot_general(left, right, (((1,), (1,)), ((), ())), preferred_element_type=f32)


def whole_loop(count, body, unroll=1):
    def step(index, carry):
        body(index)
        return carry

    lax.fori_loop(0, count, step, 0, unroll=unroll)


def aligned(index, size):
    return pl.ds(pl.multiple_of(index * size, size), size)


def spread_kernel(ids, out):
    out[...] = jnp.broadcast_to(ids[...].reshape(1, 1, 128), out.shape)


def select_kernel(place, ids, table, down, partial, hots, lows, chosen, table_here, down_here, sems):
    holder = (place[0] * 8 + place[1]) * 2 + place[4]
    table_copy = pltpu.make_async_copy(table, table_here, sems.at[0])
    down_copy = pltpu.make_async_copy(down, down_here, sems.at[1])
    table_copy.start()
    down_copy.start()

    def mark(line):
        tokens = ids[pl.ds(line, 1), :]
        span = aligned((line & 1) * 16 + (line >> 1), 128)
        hots[:, span] = ones_where(iota((16, 128), 0) == (tokens >> 7) - holder * 16)
        lows[:, span] = ones_where(iota((128, 128), 0) == (tokens & 127))

    whole_loop(32, mark, 8)
    in_prompt = dot_nt(hots[:, :KEYS], lows[:, :KEYS]) > 0.5
    alone = (dot_nt(hots[:, KEYS:], lows[:, KEYS:]) > 0.5) & jnp.logical_not(in_prompt)
    upper = ones_where(iota((128, 128), 0) < iota((128, 128), 1))
    all_ones = jnp.ones((128, 128), bf16)
    row = iota((8 * SLOTS, 128), 0)
    wanted = ((row & 15) * 8 + (((row >> 4) - holder) & 7)).astype(f32)
    before = jnp.zeros((1, 128), f32)
    ranks = []
    for present in (in_prompt, alone):
        flags = ones_where(present)
        within = dot(flags, upper)
        totals = dot(flags, all_ones)
        lines = []
        for step in range(16):
            lines.append(within[step : step + 1, :] + before)
            before = before + totals[step : step + 1, :]
        ranks.append(lines)
    for step in range(16):
        rank = jnp.where(alone[step : step + 1, :], ranks[1][step], -1.0)
        rank = jnp.where(in_prompt[step : step + 1, :], ranks[0][step], rank)
        chosen[:, step * 128 : (step + 1) * 128] = ones_where(wanted == rank)
    table_copy.wait()
    rows = dot(chosen[...], table_here[...]).astype(bf16)
    down_copy.wait()
    partial[...] = dot_nt(rows, down_here[...]).reshape(partial.shape)


def rank_kernel(ids, sheet, highs, lows):
    square = (128, 128)
    lane = iota((8, 128), 1)
    sheet[0:16, :] = ids[pl.ds(0, 16, stride=2), :]
    sheet[16:32, :] = ids[pl.ds(1, 16, stride=2), :]
    target = iota(square, 1)
    mover = ones_where(iota(square, 0) == jnp.where(target < 64, 2 * target, 2 * target - 127))
    plain = sheet[0:16, :]
    decode_tokens = sheet[16:32, :]
    coarse = (plain >> 8).astype(f32).astype(bf16)
    fine = (plain & 255).astype(f32).astype(bf16)
    moved = dot(coarse, mover) * 256.0 + dot(fine, mover)
    sheet[0:16, :] = moved.astype(jnp.int32)
    even = sheet[pl.ds(0, 8, stride=2), :]
    odd = sheet[pl.ds(1, 8, stride=2), :]
    first = jnp.where(lane < 64, even, pltpu.roll(odd, 64, 1))
    second = jnp.where(lane < 64, pltpu.roll(even, 64, 1), odd)
    tokens = jnp.concatenate([first, second, decode_tokens], axis=0)
    sheet[0:32, :] = tokens

    def mark(block):
        line = sheet[pl.ds(block, 1), :]
        span = aligned(block, 128)
        highs[:, span] = ones_where(iota((512, 128), 0) == (line >> 7))
        lows[:, span] = ones_where(iota(square, 0) == (line & 127))

    whole_loop(32, mark, 8)
    in_prompt = dot_nt(lows[:, :KEYS], highs[:, :KEYS]) > 0.5
    alone = (dot_nt(lows[:, KEYS:], highs[:, KEYS:]) > 0.5) & jnp.logical_not(in_prompt)
    below = ones_where(iota(square, 1) < iota(square, 0))
    all_ones = jnp.ones(square, bf16)
    wide = (512, 512)
    same = (iota(wide, 0) >> 4) == (iota(wide, 1) >> 4)
    in_holder = ones_where(same & (iota(wide, 0) < iota(wide, 1)))
    prompt_flags = ones_where(in_prompt)
    alone_flags = ones_where(alone)
    prompt_columns = dot(all_ones, prompt_flags).astype(bf16)
    alone_columns = dot(all_ones, alone_flags).astype(bf16)
    prompt_rank = dot(below, prompt_flags) + dot(prompt_columns, in_holder)
    alone_rank = (
        dot(below, alone_flags) + dot(alone_columns, in_holder) + dot(prompt_columns, ones_where(same))
    )
    rank = jnp.where(in_prompt, prompt_rank, jnp.where(alone, alone_rank, 0.0))
    top_rank = jnp.max(jnp.max(rank, axis=0, keepdims=True), axis=1, keepdims=True).astype(jnp.int32)
    coded = (jnp.minimum(rank, 127.0) + jnp.where(in_prompt, 128.0, 0.0)).astype(bf16)
    pieces = []
    for chunk in range(4):
        span = slice(chunk * 1024, (chunk + 1) * 1024)
        looked = dot(coded, highs[:, span]) * lows[:, span].astype(f32)
        line = jnp.sum(looked, axis=0, keepdims=True)
        for part in range(8):
            pieces.append(line[:, part * 128 : (part + 1) * 128])
    value = jnp.concatenate(pieces, axis=0).astype(jnp.int32)
    ranks = value & 127
    holder = tokens >> 11
    tp_of = (ranks + holder) & 7
    quad = tp_of * 16 + (ranks >> 3)
    sheet[0:32, :] = quad
    sheet[32:64, :] = holder
    sheet[64:96, :] = jnp.where(value >= 128, -1, tp_of)
    sheet[96:104, :] = jnp.broadcast_to(top_rank, (8, 128))


def place_kernel(place, sheet, columns, kept, fits, quads, holders, hot_tp, hot_pool, sheet_b):
    ylo, zed, ex, core, section = place[0], place[1], place[2], place[3], place[4]
    square = (128, 128)

    def spot(block, source):
        span = aligned(block, 128)
        quads[:, span] = ones_where(iota(square, 0) == sheet[pl.ds(source, 1), :])
        holders[:, span] = ones_where(iota(square, 0) == sheet[pl.ds(source + 32, 1), :])

    whole_loop(16, lambda block: spot(block, block), 8)
    for part in range(2):
        spot(16 + part, 16 + part * 8 + zed)
    own = 16 + ylo * 8 + zed
    spot(18, own)
    up, down = iota(square, 0), iota(square, 1)
    same_tp = (up >> 4) == (down >> 4)
    same_pool = ((up >> 4) == (down >> 4)) & ((up & 1) == (down & 1))
    tp_ones = ones_where(same_tp)
    pool = ones_where(same_pool)
    before = ones_where(same_pool & (up < down))
    in_tp = ones_where(same_tp & (down < up))
    held = dot_nt(quads[:, :KEYS], holders[:, :KEYS]) > 0.5
    flags = ones_where(held)
    sums = dot(tp_ones, flags).astype(bf16)
    prompt_position = dot(in_tp, flags) + dot(sums, before)
    prompt_count = dot(sums, pool)
    positions = []
    for part in range(2):
        span = slice(KEYS + part * 128, KEYS + (part + 1) * 128)
        added = (dot_nt(quads[:, span], holders[:, span]) > 0.5) & jnp.logical_not(held)
        added_flags = ones_where(added)
        added_sums = dot(tp_ones, added_flags).astype(bf16)
        spots = dot(in_tp, added_flags) + dot(added_sums, before) + prompt_count
        spots = jnp.where(held, prompt_position, jnp.where(added, spots, 255.0))
        positions.append(jnp.minimum(spots, 255.0))
    position = jnp.where(ylo == 0, positions[0], positions[1])

    def pick(block):
        span = aligned(block, 128)
        hot_tp[:, span] = ones_where(iota((16, 128), 0) == sheet[pl.ds(block + 80, 1), :])
        line = sheet[pl.ds(block + 48, 1), :]
        line = ((line >> 4) * 2 + (line & 1)) + 4 * block
        hot_pool[:, span] = ones_where(iota((64, 128), 0) == line)

    whole_loop(16, pick, 8)
    gather_tp = ones_where(iota((16, 128), 0) == (iota((16, 128), 1) >> 4))
    base = dot(gather_tp, flags).astype(bf16)
    holder, column = iota((128, 64), 0), iota((128, 64), 1)
    pooled = ones_where((holder < 32) & (((holder >> 4) * 2 + (holder & 1)) == (column & 3)))
    needed = dot_nt(hot_tp[...], hot_pool[...]) + dot(base, pooled)
    needed = jnp.max(jnp.max(needed, axis=0, keepdims=True), axis=1, keepdims=True)
    enough = (sheet[96:97, 0:1] < 8 * SLOTS) & (needed <= float(KEPT))
    fits[0, 0] = jnp.max(jnp.where(enough, 1, 0))

    looked = dot(position.astype(bf16), holders[...]) * quads[...].astype(f32)
    line = jnp.sum(looked, axis=0, keepdims=True)
    found = [line[:, block * 128 : (block + 1) * 128] for block in range(19)]
    found = jnp.concatenate(found + [jnp.zeros((5, 128), f32)], axis=0)
    blank = jnp.zeros((5, 128), jnp.int32)
    quad_rows = jnp.concatenate([sheet[0:16, :], blank[:2], sheet[pl.ds(own, 1), :], blank], axis=0)
    holder_rows = jnp.concatenate([sheet[32:48, :], blank[:2], sheet[pl.ds(own + 32, 1), :], blank], axis=0)
    tp_rows = quad_rows >> 4
    source = ((holder_rows >> 4) * 2 + (holder_rows & 1)) * 4 + (tp_rows >> 1)
    side = jnp.where((tp_rows & 1) == core, 0, SIDE)
    final = found + (source * KEPT + side).astype(f32)
    tp_index = ex * 2 + core
    turned = pltpu.roll(final, (128 - tp_index * 16) % 128, 1)
    turned = jnp.where(iota((24, 128), 1) < 16, turned, -1.0)
    final = jnp.where(iota((24, 128), 0) == 18, turned, final)
    final = jnp.concatenate([final, jnp.zeros((104, 128), f32)], axis=0)
    columns[...] = jnp.transpose(final).astype(jnp.int32)
    few = (16, 128)
    for part in range(2):
        sheet_b[...] = positions[part]
        mine = sheet_b[pl.ds(pl.multiple_of(tp_index * 16, 16), 16), :].astype(bf16)
        spread = dot(mine, ones_where(up == (ylo * 8 + (down >> 4)) * 2 + section))
        spread = jnp.where((iota(few, 1) & 15) == iota(few, 0), spread, 0.0)
        kept[part : part + 1, :] = jnp.sum(spread, axis=0, keepdims=True)


def finish_kernel(parts, gain, sent):
    latent = parts[0]
    for tp in range(1, parts.shape[0]):
        latent = latent + parts[tp]
    plain = latent[:, :LAT]
    scaled = plain * lax.rsqrt(jnp.mean(plain * plain, axis=-1, keepdims=True) + norm_eps) * gain[...]
    rotary = latent[:, LAT:]
    coarse = rotary.astype(bf16)
    fine = (rotary - coarse.astype(f32)).astype(bf16)
    row = jnp.concatenate([scaled.astype(bf16), coarse, fine], axis=-1)
    for peer in range(sent.shape[0]):
        sent[peer] = row


def keep_kernel(kept, rows, sent):
    for ylo in range(2):
        chosen = iota((KEPT, 128), 0).astype(f32) == kept[ylo : ylo + 1, :]
        row = dot(ones_where(chosen), rows[...]).astype(bf16)
        for peer in range(8):
            sent[ylo * 8 + peer] = row


def cache_kernel(lengths, query, cache, out, level):
    length = lengths[pl.program_id(0)]
    scores = dot(query[0], cache[0]) * base_two
    scores = jnp.where(iota(scores.shape, 1) < length, scores, masked_fill)
    highest = jnp.max(scores, axis=-1, keepdims=True)
    weights = jnp.exp2(scores - highest)
    total = jnp.sum(weights, axis=-1, keepdims=True)
    out[...] = (dot_nt(weights.astype(bf16), cache[0, :LAT, :]) * (1.0 / total)).astype(bf16)
    level[...] = jnp.broadcast_to(highest + jnp.log2(total), level.shape)


def hot_rows(hot, columns, prompt, side, part):
    turned = pltpu.roll(columns[...], (128 - prompt * 8) % 128, 1) - side * SIDE
    for block in range(part * 4, part * 4 + 4):
        hot[block * 128 : (block + 1) * 128, :] = ones_where(iota((128, SIDE), 1) == turned[:, block : block + 1])
    return hot[part * 512 : (part + 1) * 512, :]


def fresh_hot(columns, side):
    return ones_where(iota((128, SIDE), 1) == columns[:, 18:19] - side * SIDE)


def empty_kernel(*refs):
    pass


def fresh_hot(columns, side):
    return ones_where(iota((128, SIDE), 1) == columns[:, 18:19] - side * SIDE)


def put_keys(keys, span, found, factor):
    turning = found[:, LAT:]
    turning = turning + pltpu.roll(turning, 64, 1)
    turned = turning * factor + pltpu.roll(turning, 32, 1) * pltpu.roll(factor, 64, 1)
    keys[span, :LAT] = found[:, :LAT].astype(bf16)
    keys[span, LAT:] = turned[:, : KVW - LAT].astype(bf16)


def copy_in(source, target, sem):
    copy = pltpu.make_async_copy(source, target, sem)
    copy.start()
    copy.wait()


def weigh(scores, old):
    new = jnp.maximum(old, jnp.max(scores, axis=-1, keepdims=True))
    weights = jnp.exp2(scores - new)
    return new, jnp.exp2(old - new), jnp.sum(weights, axis=-1, keepdims=True), weights.astype(bf16)


def near_kernel(place, slots, columns, near, hot):
    group = place[0] * 8 + place[1]

    @pl.when(place[4] == 1)
    def _():
        near[KEYS : KEYS + 128, :] = dot(fresh_hot(columns, 0), slots[...]).astype(bf16)

    def open_prompt(prompt):
        @pl.when((place[4] == 0) | (place[5 + prompt] == group))
        def _():
            for part in range(2):
                some = hot_rows(hot, columns, prompt, 0, part)
                near[aligned(prompt * 2 + part, 512), :] = dot(some, slots[...]).astype(bf16)

    whole_loop(2, open_prompt)


def decode_kernel(
    place, fits, near, others, columns, new_factors, factors_far, query_far, earlier_far, level_far, spare, spare_new,
    out, out_here, factors, query, earlier, level, keys, hot, highest, total, mixed, sem, in_sems, out_sems
):
    group = place[0] * 8 + place[1]
    fitting = fits[0, 0] == 1

    @pl.when(place[4] == 1)
    def _():
        loads = [
            pltpu.make_async_copy(source, target, in_sems.at[index])
            for index, (source, target) in enumerate(
                ((factors_far, factors), (query_far, query), (level_far, level), (earlier_far, earlier))
            )
        ]
        for load in loads:
            load.start()

        span = slice(KEYS, KEYS + 128)
        found = near[span, :].astype(f32) + dot(fresh_hot(columns, 1), others[...])
        put_keys(keys, span, found, new_factors[...])
        loads[0].wait()

        def open_prompt(prompt):
            @pl.when(place[5 + prompt] == group)
            def _():
                for part in range(2):
                    span = aligned(prompt * 2 + part, 512)
                    found = near[span, :].astype(f32) + dot(hot_rows(hot, columns, prompt, 1, part), others[...])
                    put_keys(keys, span, found, factors[part * 512 : (part + 1) * 512, :])

        whole_loop(2, open_prompt)

        @pl.when(jnp.logical_not(fitting))
        def _():
            copy_in(spare, keys.at[pl.ds(0, KEYS)], sem)
            copy_in(spare_new, keys.at[pl.ds(KEYS, 128)], sem)

        for load in loads[1:]:
            load.wait()
        newest = keys[KEYS : KEYS + 128, :]

        def begin(piece):
            span = aligned(piece, 256)
            scores = dot_nt(query[span, :], newest) * base_two
            key = iota(scores.shape, 1)
            row = iota(scores.shape, 0) & 15
            allowed = ((key >> 1) == (row >> 1)) & ((key & 1) <= (row & 1))
            scores = jnp.where(allowed, scores, masked_fill)
            new, factor, summed, weights = weigh(scores, level[span, 0:1])
            mixed[span, :] = earlier[span, :].astype(f32) * factor + dot(weights, newest[:, :LAT])
            highest[span, :] = jnp.broadcast_to(new, (256, 128))
            total[span, :] = jnp.broadcast_to(factor + summed, (256, 128))

        whole_loop(4, begin, 4)

        def add_prompt(prompt):
            @pl.when(place[5 + prompt] == group)
            def _():
                def add_part(piece):
                    span = aligned(piece, 256)
                    some = keys[aligned(prompt, 1024), :]
                    new, factor, summed, weights = weigh(dot_nt(query[span, :], some) * base_two, highest[span, 0:1])
                    mixed[span, :] = mixed[span, :] * factor + dot(weights, some[:, :LAT])
                    highest[span, :] = jnp.broadcast_to(new, (256, 128))
                    total[span, :] = total[span, :] * factor + summed

                whole_loop(4, add_part, 4)

        whole_loop(2, add_prompt)

        def out_copy(tp):
            rows = aligned(tp, 16)
            return pltpu.make_async_copy(out_here.at[rows], out.at[rows], out_sems.at[tp])

        def tp_rows(tp):
            for head in range(8):
                rows = pl.ds(pl.multiple_of(tp * 128 + head * 16, 16), 16)
                some = mixed[rows, :] * (1.0 / total[rows, 0:1])
                out_here[aligned(tp, 16), head * LAT : (head + 1) * LAT] = some.astype(bf16)
            out_copy(tp).start()

        whole_loop(8, tp_rows, 2)
        whole_loop(8, lambda tp: out_copy(tp).wait())


def prefill_kernel(place, fits, near, others, columns, factors, query, spare, out, keys, hot, mixed, pairs, sem):
    group = place[0] * 8 + place[1]
    fitting = fits[0, 0] == 1

    @pl.when(place[4] == 0)
    def _():
        def add_prompt(prompt):
            for part in range(2):
                span = slice(part * 512, (part + 1) * 512)
                found = near[aligned(prompt * 2 + part, 512), :].astype(f32)
                found = found + dot(hot_rows(hot, columns, prompt, 1, part), others[...])
                put_keys(keys, span, found, factors[span, :])

            @pl.when(jnp.logical_not(fitting))
            def _():
                copy_in(spare.at[pl.ds(prompt * 1024, 1024)], keys, sem)

            span = aligned(prompt, 512)
            some = keys[...]
            scores = dot_nt(query[span, :], some) * base_two
            last = (iota((512, 1), 0) & 63) + group * 64
            scores = jnp.where(iota(scores.shape, 1) <= last, scores, masked_fill)
            _, _, summed, weights = weigh(scores, jnp.full((512, 1), masked_fill, f32))
            added = dot(weights, some[:, :LAT]) * (1.0 / summed)
            for column in range(4):
                mixed[column, span, :] = added[:, column * 128 : (column + 1) * 128]

        whole_loop(2, add_prompt)

        def head_rows(head):
            for column in range(4):
                for prompt in range(2):
                    start = pl.multiple_of(prompt * 512 + head * 64, 64)
                    pairs[column, pl.ds(prompt, 64, stride=2), :] = mixed[column, pl.ds(start, 64), :]
                out[:, pl.ds(pl.multiple_of(head * LAT + column * 128, 128), 128)] = pairs[column].astype(bf16)

        whole_loop(8, head_rows, 2)


def join_kernel(place, prefilled, turned, out, sems):
    @pl.when(place[4] == 1)
    def _():
        copies = []
        for part in range(4):
            span = pl.ds(part * 32, 32)
            copies.append(pltpu.make_async_copy(turned.at[span], out.at[span], sems.at[part]))
        for copy in copies:
            copy.start()
        for copy in copies:
            copy.wait()


def rope_factors(position):
    frequency = np.float32(rope_base) ** (-np.arange(32, dtype=np.float32) / np.float32(32))
    angles = position[:, None] * frequency[None, :]
    if isinstance(position, np.ndarray):
        angles = angles.astype(np.float32).astype(np.float64)
        cosine, sine = np.cos(angles), np.sin(angles)
        return np.concatenate([cosine, cosine, -sine, sine], axis=-1).astype(np.float32)
    cosine, sine = jnp.cos(angles), jnp.sin(angles)
    return jnp.concatenate([cosine, cosine, -sine, sine], axis=-1)


def finish_keys(latent, latent_gain, position):
    plain = latent[:, :LAT]
    scaled = plain * lax.rsqrt(jnp.mean(plain * plain, axis=-1, keepdims=True) + norm_eps) * latent_gain
    factors = rope_factors(position.astype(f32))
    rotary = latent[:, LAT:]
    swapped = jnp.concatenate([rotary[:, 32:], rotary[:, :32]], axis=-1)
    turned = rotary * factors[:, :64] + swapped * factors[:, 64:]
    return jnp.concatenate([scaled, turned], axis=-1).astype(bf16)


def dense_keys(token_ids, place, embed_table, down, latent_gain, cache_length):
    group = place[0] * 8 + place[1]
    tp_index = place[2] * 2 + place[3]
    every = lax.all_to_all(jnp.broadcast_to(token_ids, (32, 128)).reshape(32, 1, 128), HOLDERS, 0, 0, tiled=True)
    local_row = every.reshape(-1) - (group * 2 + place[4]) * 2048
    inside = (local_row >= 0) & (local_row < 2048)
    picked = jnp.take(embed_table, jnp.clip(local_row, 0, 2047), axis=0)
    picked = jnp.where(inside[:, None], picked, jnp.zeros_like(picked)).reshape(32, 128, 896)
    embedded = jnp.sum(lax.all_to_all(picked, HOLDERS, 0, 0, tiled=True).astype(f32), axis=0).astype(bf16)
    partial = dot_nt(embedded, down)
    spread = jnp.broadcast_to(partial[None], (8, 128, KVW))
    latent = jnp.sum(lax.all_to_all(spread, TP, 0, 0, tiled=True), axis=0)
    index = jnp.arange(128, dtype=jnp.int32)
    mine = finish_keys(latent, latent_gain, group * 64 + index // 2)
    spread = jnp.broadcast_to(mine[None], (32, 128, KVW))
    prompts = lax.all_to_all(spread, HOLDERS, 0, 0, tiled=True).reshape(16, 2, 64, 2, KVW)[:, 0]
    prompts = jnp.transpose(prompts, (2, 0, 1, 3)).reshape(KEYS, KVW)
    own = lax.dynamic_slice_in_dim(latent, tp_index * 16, 16, 0)
    fresh = finish_keys(own, latent_gain, (cache_length[:, None] + jnp.arange(2, dtype=jnp.int32)[None]).reshape(-1))
    return prompts, jnp.concatenate([fresh, jnp.zeros((112, KVW), bf16)], axis=0)


def in_vmem(value):
    return pltpu.with_memory_space_constraint(value, VMEM)


def in_hbm(value):
    return pltpu.with_memory_space_constraint(value, pltpu.HBM)


def params(mebibytes):
    return pltpu.CompilerParams(vmem_limit_bytes=mebibytes * 1024 * 1024)


def shards(
    token_ids,
    embed_table,
    latent_down,
    latent_gain,
    prefill_query,
    decode_query,
    latent_cache,
    cache_length,
    prompt_owner,
):
    place = jnp.stack([lax.axis_index(name) for name in ("ylo", "z", "x", "core", "role")]).astype(jnp.int32)
    place = jnp.concatenate([place, prompt_owner])
    down = jnp.transpose(latent_down)
    whole = pl.BlockSpec(memory_space=VMEM)
    scalars = pl.BlockSpec(memory_space=SMEM)
    anywhere = pl.BlockSpec(memory_space=pl.ANY)
    shaped = jax.ShapeDtypeStruct

    spread = pl.pallas_call(
        spread_kernel,
        out_shape=shaped((32, 1, 128), jnp.int32),
        in_specs=[whole],
        out_specs=whole,
        compiler_params=params(4),
        name="spread_ids",
    )(token_ids)
    every = lax.all_to_all(spread, HOLDERS, 0, 0, tiled=True).reshape(32, 128)

    earlier, level = pl.pallas_call(
        cache_kernel,
        grid_spec=pltpu.PrefetchScalarGridSpec(
            num_scalar_prefetch=1,
            grid=(8,),
            in_specs=[
                pl.BlockSpec((1, 128, KVW), lambda row, lengths: (row, 0, 0)),
                pl.BlockSpec((1, KVW, 512), lambda row, lengths: (row, 0, 0)),
            ],
            out_specs=[
                pl.BlockSpec((128, LAT), lambda row, lengths: (row, 0)),
                pl.BlockSpec((128, 128), lambda row, lengths: (row, 0)),
            ],
        ),
        out_shape=(pltpu.HBM((1024, LAT), bf16), pltpu.HBM((1024, 128), f32)),
        compiler_params=params(12),
        cost_estimate=pl.CostEstimate(flops=12 * 10**8, bytes_accessed=7 * 10**6, transcendentals=524288),
        name="cache_rows",
    )(cache_length, in_hbm(decode_query.reshape(8, 128, KVW)), in_hbm(jnp.swapaxes(latent_cache, 1, 2)))
    every, earlier, level = lax.optimization_barrier((every, earlier, level))

    partial = pl.pallas_call(
        select_kernel,
        out_shape=shaped((8, SLOTS, KVW), f32),
        in_specs=[scalars, whole, anywhere, anywhere],
        out_specs=whole,
        scratch_shapes=[
            VMEM((16, 4096), bf16),
            VMEM((128, 4096), bf16),
            VMEM((8 * SLOTS, 2048), bf16),
            VMEM((2048, 896), bf16),
            VMEM((KVW, 896), bf16),
            pltpu.SemaphoreType.DMA((2,)),
        ],
        compiler_params=params(16),
        cost_estimate=pl.CostEstimate(flops=3 * 10**9, bytes_accessed=5 * 10**6, transcendentals=0),
        name="select_rows",
    )(place, every, in_hbm(embed_table), in_hbm(down))
    parts = lax.all_to_all(partial, TP, 0, 0, tiled=True)

    sheet = pl.pallas_call(
        rank_kernel,
        out_shape=shaped((104, 128), jnp.int32),
        in_specs=[whole],
        out_specs=whole,
        scratch_shapes=[VMEM((512, 4096), bf16), VMEM((128, 4096), bf16)],
        compiler_params=params(18),
        cost_estimate=pl.CostEstimate(flops=2 * 10**9, bytes_accessed=10**6, transcendentals=0),
        name="rank_rows",
    )(every)
    parts, sheet = lax.optimization_barrier((parts, sheet))
    sent = pl.pallas_call(
        finish_kernel,
        out_shape=shaped((8, SLOTS, WIDE), bf16),
        in_specs=[whole, whole],
        out_specs=whole,
        compiler_params=params(8),
        name="finish_rows",
    )(parts, latent_gain.reshape(1, LAT))
    arrived = lax.all_to_all(sent, "z", 0, 0, tiled=True)

    columns, kept, fits = pl.pallas_call(
        place_kernel,
        out_shape=(shaped((128, 128), jnp.int32), shaped((8, 128), f32), shaped((1, 1), jnp.int32)),
        in_specs=[scalars, whole],
        out_specs=(whole, whole, scalars),
        scratch_shapes=[
            VMEM((128, 19 * 128), bf16),
            VMEM((128, 19 * 128), bf16),
            VMEM((16, 2048), bf16),
            VMEM((64, 2048), bf16),
            VMEM((128, 128), f32),
        ],
        compiler_params=params(12),
        cost_estimate=pl.CostEstimate(flops=10**9, bytes_accessed=10**6, transcendentals=0),
        name="place_rows",
    )(place, sheet)
    handed = pl.pallas_call(
        keep_kernel,
        out_shape=shaped((16, KEPT, WIDE), bf16),
        in_specs=[whole] * 2,
        out_specs=whole,
        compiler_params=params(8),
        name="keep_rows",
    )(kept, arrived.reshape(8 * SLOTS, WIDE))
    handed, prompt_rows, decode_rows, lengths, earlier, level = lax.optimization_barrier(
        (handed, prefill_query, decode_query, cache_length, earlier, level)
    )
    slots = lax.all_to_all(handed, PLANE, 0, 0, tiled=True).reshape(SIDE, WIDE)

    def by_head(rows):
        return jnp.transpose(rows.reshape(16, 64, -1), (1, 0, 2)).reshape(1024, -1)

    row_query, earlier, level = by_head(decode_rows), by_head(earlier), by_head(level)
    new_position = (lengths[:, None] + jnp.arange(2, dtype=jnp.int32)[None]).reshape(-1)
    new_factors = jnp.pad(rope_factors(new_position.astype(f32)), ((0, 112), (0, 0)))
    prompt_query = jnp.transpose(prompt_rows.reshape(64, 2, 8, KVW), (1, 2, 0, 3)).reshape(1024, KVW)
    slots, prompt_query, row_query, earlier, level, new_factors = lax.optimization_barrier(
        (slots, prompt_query, row_query, earlier, level, new_factors)
    )
    others = lax.ppermute(slots, "core", [(0, 1), (1, 0)])

    spare, spare_new = lax.cond(
        fits[0, 0] == 1,
        lambda *unused: tuple(
            pl.pallas_call(
                empty_kernel,
                out_shape=[shaped((KEYS, KVW), bf16), shaped((128, KVW), bf16)],
                out_specs=[anywhere] * 2,
                name="no_keys",
            )()
        ),
        dense_keys,
        token_ids,
        place,
        embed_table,
        down,
        latent_gain,
        cache_length,
    )

    near = pl.pallas_call(
        near_kernel,
        out_shape=VMEM((KEYS + 128, WIDE), bf16),
        in_specs=[scalars, whole, whole],
        out_specs=whole,
        scratch_shapes=[VMEM((1024, SIDE), bf16)],
        compiler_params=params(12),
        cost_estimate=pl.CostEstimate(flops=2 * 10**9, bytes_accessed=10**6, transcendentals=0),
        name="near_keys",
    )(place, slots, columns)
    factors = jnp.asarray(rope_factors(np.arange(1024, dtype=np.float32)))
    decoded = pl.pallas_call(
        decode_kernel,
        out_shape=pltpu.HBM((128, 4096), bf16),
        in_specs=[scalars] * 2 + [whole] * 4 + [anywhere] * 6,
        out_specs=anywhere,
        scratch_shapes=[
            VMEM((128, 4096), bf16),
            VMEM((1024, 128), f32),
            VMEM((1024, KVW), bf16),
            VMEM((1024, LAT), bf16),
            VMEM((1024, 128), f32),
            VMEM((KEYS + 128, KVW), bf16),
            VMEM((1024, SIDE), bf16),
            VMEM((1024, 128), f32),
            VMEM((1024, 128), f32),
            VMEM((1024, LAT), f32),
            pltpu.SemaphoreType.DMA,
            pltpu.SemaphoreType.DMA((4,)),
            pltpu.SemaphoreType.DMA((8,)),
        ],
        compiler_params=params(24),
        cost_estimate=pl.CostEstimate(flops=5 * 10**9, bytes_accessed=7 * 10**6, transcendentals=10**6),
        name="decode_rows",
    )(
        place, fits, in_vmem(near), in_vmem(others), columns, new_factors, in_hbm(factors),
        in_hbm(row_query), in_hbm(earlier), in_hbm(level), in_hbm(spare), in_hbm(spare_new),
    )
    turned = lax.all_to_all(decoded.reshape(8, 16, 4096), TP, 0, 0, tiled=True).reshape(128, 4096)
    prefilled = pl.pallas_call(
        prefill_kernel,
        out_shape=pltpu.HBM((128, 4096), bf16),
        in_specs=[scalars] * 2 + [whole] * 5 + [anywhere],
        out_specs=whole,
        scratch_shapes=[
            VMEM((1024, KVW), bf16),
            VMEM((1024, SIDE), bf16),
            VMEM((4, 1024, 128), f32),
            VMEM((4, 128, 128), f32),
            pltpu.SemaphoreType.DMA,
        ],
        compiler_params=params(20),
        cost_estimate=pl.CostEstimate(flops=7 * 10**9, bytes_accessed=7 * 10**6, transcendentals=10**6),
        name="prefill_rows",
    )(place, fits, in_vmem(near), in_vmem(others), columns, in_vmem(factors), in_vmem(prompt_query), in_hbm(spare))
    out = pl.pallas_call(
        join_kernel,
        out_shape=pltpu.HBM((128, 4096), bf16),
        in_specs=[scalars] + [anywhere] * 2,
        out_specs=anywhere,
        scratch_shapes=[pltpu.SemaphoreType.DMA((4,))],
        input_output_aliases={1: 0},
        compiler_params=params(4),
        name="join_rows",
    )(place, in_hbm(prefilled), turned)
    return out[None]


def solution(mesh):
    fine_mesh = Mesh(mesh.devices.reshape(2, 8, 4, 2, 2), ("ylo", "z", "x", "core", "role"))
    ctx, tp = ("ylo", "z"), ("x", "core")
    in_specs = (
        P("role", ctx),
        P(ctx + ("role",), tp),
        P(tp, None),
        P(),
        P(ctx, tp, None),
        P(ctx + tp, None, None, None),
        P(ctx + tp, None, None),
        P(ctx + tp),
        P(),
    )
    out_specs = P("role", ctx, tp)
    return jax.shard_map(shards, mesh=fine_mesh, in_specs=in_specs, out_specs=out_specs, check_vma=False)
```

```python
import jax
import jax.numpy as jnp
import numpy as np
from jax import lax
from jax.experimental import pallas as pl
from jax.experimental.pallas import tpu as pltpu
from jax.sharding import Mesh
from jax.sharding import PartitionSpec as P

LAT = 512
KVW = 576
STEPS = 2
WIDE = 640
SLOTS = 16
KEPT = 48
SIDE = 16 * KEPT
KEYS = 2048

score_scale = 0.07216878364870322
base_two = score_scale * 1.4426950408889634
masked_fill = -1e30
norm_eps = 1e-06
rope_base = 10000.0
bf16 = jnp.bfloat16
f32 = jnp.float32
SMEM = pltpu.SMEM
VMEM = pltpu.VMEM

HOLDERS = ("ylo", "z", "role")
PLANE = ("ylo", "role", "x")
TP = ("x", "core")


def iota(shape, axis):
    return lax.broadcasted_iota(jnp.int32, shape, axis)


def ones_where(flags):
    return jnp.where(flags, 1.0, 0.0).astype(bf16)


def dot(left, right):
    return lax.dot_general(left, right, (((1,), (0,)), ((), ())), preferred_element_type=f32)


def dot_nt(left, right):
    return lax.dot_general(left, right, (((1,), (1,)), ((), ())), preferred_element_type=f32)


def whole_loop(count, body, unroll=1):
    def step(index, carry):
        body(index)
        return carry

    lax.fori_loop(0, count, step, 0, unroll=unroll)


def aligned(index, size):
    return pl.ds(pl.multiple_of(index * size, size), size)


def spread_kernel(ids, out):
    out[...] = jnp.broadcast_to(ids[...].reshape(1, 1, 128), out.shape)


def select_kernel(place, ids, table, down, partial, hots, lows, chosen, table_here, down_here, sems):
    holder = (place[0] * 8 + place[1]) * 2 + place[4]
    table_copy = pltpu.make_async_copy(table, table_here, sems.at[0])
    down_copy = pltpu.make_async_copy(down, down_here, sems.at[1])
    table_copy.start()
    down_copy.start()

    def mark(line):
        tokens = ids[pl.ds(line, 1), :]
        span = aligned((line & 1) * 16 + (line >> 1), 128)
        hots[:, span] = ones_where(iota((16, 128), 0) == (tokens >> 7) - holder * 16)
        lows[:, span] = ones_where(iota((128, 128), 0) == (tokens & 127))

    whole_loop(32, mark, 8)
    in_prompt = dot_nt(hots[:, :KEYS], lows[:, :KEYS]) > 0.5
    alone = (dot_nt(hots[:, KEYS:], lows[:, KEYS:]) > 0.5) & jnp.logical_not(in_prompt)
    upper = ones_where(iota((128, 128), 0) < iota((128, 128), 1))
    all_ones = jnp.ones((128, 128), bf16)
    row = iota((8 * SLOTS, 128), 0)
    wanted = ((row & 15) * 8 + (((row >> 4) - holder) & 7)).astype(f32)
    before = jnp.zeros((1, 128), f32)
    ranks = []
    for present in (in_prompt, alone):
        flags = ones_where(present)
        within = dot(flags, upper)
        totals = dot(flags, all_ones)
        lines = []
        for step in range(16):
            lines.append(within[step : step + 1, :] + before)
            before = before + totals[step : step + 1, :]
        ranks.append(lines)
    for step in range(16):
        rank = jnp.where(alone[step : step + 1, :], ranks[1][step], -1.0)
        rank = jnp.where(in_prompt[step : step + 1, :], ranks[0][step], rank)
        chosen[:, step * 128 : (step + 1) * 128] = ones_where(wanted == rank)
    table_copy.wait()
    rows = dot(chosen[...], table_here[...]).astype(bf16)
    down_copy.wait()
    partial[...] = dot_nt(rows, down_here[...]).reshape(partial.shape)


def rank_kernel(ids, sheet, highs, lows):
    square = (128, 128)
    lane = iota((8, 128), 1)
    sheet[0:16, :] = ids[pl.ds(0, 16, stride=2), :]
    sheet[16:32, :] = ids[pl.ds(1, 16, stride=2), :]
    target = iota(square, 1)
    mover = ones_where(iota(square, 0) == jnp.where(target < 64, 2 * target, 2 * target - 127))
    plain = sheet[0:16, :]
    decode_tokens = sheet[16:32, :]
    coarse = (plain >> 8).astype(f32).astype(bf16)
    fine = (plain & 255).astype(f32).astype(bf16)
    moved = dot(coarse, mover) * 256.0 + dot(fine, mover)
    sheet[0:16, :] = moved.astype(jnp.int32)
    even = sheet[pl.ds(0, 8, stride=2), :]
    odd = sheet[pl.ds(1, 8, stride=2), :]
    first = jnp.where(lane < 64, even, pltpu.roll(odd, 64, 1))
    second = jnp.where(lane < 64, pltpu.roll(even, 64, 1), odd)
    tokens = jnp.concatenate([first, second, decode_tokens], axis=0)
    sheet[0:32, :] = tokens

    def mark(block):
        line = sheet[pl.ds(block, 1), :]
        span = aligned(block, 128)
        highs[:, span] = ones_where(iota((512, 128), 0) == (line >> 7))
        lows[:, span] = ones_where(iota(square, 0) == (line & 127))

    whole_loop(32, mark, 8)
    in_prompt = dot_nt(lows[:, :KEYS], highs[:, :KEYS]) > 0.5
    alone = (dot_nt(lows[:, KEYS:], highs[:, KEYS:]) > 0.5) & jnp.logical_not(in_prompt)
    below = ones_where(iota(square, 1) < iota(square, 0))
    all_ones = jnp.ones(square, bf16)
    wide = (512, 512)
    same = (iota(wide, 0) >> 4) == (iota(wide, 1) >> 4)
    in_holder = ones_where(same & (iota(wide, 0) < iota(wide, 1)))
    prompt_flags = ones_where(in_prompt)
    alone_flags = ones_where(alone)
    prompt_columns = dot(all_ones, prompt_flags).astype(bf16)
    alone_columns = dot(all_ones, alone_flags).astype(bf16)
    prompt_rank = dot(below, prompt_flags) + dot(prompt_columns, in_holder)
    alone_rank = (
        dot(below, alone_flags) + dot(alone_columns, in_holder) + dot(prompt_columns, ones_where(same))
    )
    rank = jnp.where(in_prompt, prompt_rank, jnp.where(alone, alone_rank, 0.0))
    top_rank = jnp.max(jnp.max(rank, axis=0, keepdims=True), axis=1, keepdims=True).astype(jnp.int32)
    coded = (jnp.minimum(rank, 127.0) + jnp.where(in_prompt, 128.0, 0.0)).astype(bf16)
    pieces = []
    for chunk in range(4):
        span = slice(chunk * 1024, (chunk + 1) * 1024)
        looked = dot(coded, highs[:, span]) * lows[:, span].astype(f32)
        line = jnp.sum(looked, axis=0, keepdims=True)
        for part in range(8):
            pieces.append(line[:, part * 128 : (part + 1) * 128])
    value = jnp.concatenate(pieces, axis=0).astype(jnp.int32)
    ranks = value & 127
    holder = tokens >> 11
    tp_of = (ranks + holder) & 7
    quad = tp_of * 16 + (ranks >> 3)
    sheet[0:32, :] = quad
    sheet[32:64, :] = holder
    sheet[64:96, :] = jnp.where(value >= 128, -1, tp_of)
    sheet[96:104, :] = jnp.broadcast_to(top_rank, (8, 128))


def place_kernel(place, sheet, columns, kept, fits, quads, holders, hot_tp, hot_pool, sheet_b):
    ylo, zed, ex, core, section = place[0], place[1], place[2], place[3], place[4]
    square = (128, 128)

    def spot(block, source):
        span = aligned(block, 128)
        quads[:, span] = ones_where(iota(square, 0) == sheet[pl.ds(source, 1), :])
        holders[:, span] = ones_where(iota(square, 0) == sheet[pl.ds(source + 32, 1), :])

    whole_loop(16, lambda block: spot(block, block), 8)
    for part in range(2):
        spot(16 + part, 16 + part * 8 + zed)
    own = 16 + ylo * 8 + zed
    spot(18, own)
    up, down = iota(square, 0), iota(square, 1)
    same_tp = (up >> 4) == (down >> 4)
    same_pool = ((up >> 4) == (down >> 4)) & ((up & 1) == (down & 1))
    tp_ones = ones_where(same_tp)
    pool = ones_where(same_pool)
    before = ones_where(same_pool & (up < down))
    in_tp = ones_where(same_tp & (down < up))
    held = dot_nt(quads[:, :KEYS], holders[:, :KEYS]) > 0.5
    flags = ones_where(held)
    sums = dot(tp_ones, flags).astype(bf16)
    prompt_position = dot(in_tp, flags) + dot(sums, before)
    prompt_count = dot(sums, pool)
    positions = []
    for part in range(2):
        span = slice(KEYS + part * 128, KEYS + (part + 1) * 128)
        added = (dot_nt(quads[:, span], holders[:, span]) > 0.5) & jnp.logical_not(held)
        added_flags = ones_where(added)
        added_sums = dot(tp_ones, added_flags).astype(bf16)
        spots = dot(in_tp, added_flags) + dot(added_sums, before) + prompt_count
        spots = jnp.where(held, prompt_position, jnp.where(added, spots, 255.0))
        positions.append(jnp.minimum(spots, 255.0))
    position = jnp.where(ylo == 0, positions[0], positions[1])

    def pick(block):
        span = aligned(block, 128)
        hot_tp[:, span] = ones_where(iota((16, 128), 0) == sheet[pl.ds(block + 80, 1), :])
        line = sheet[pl.ds(block + 48, 1), :]
        line = ((line >> 4) * 2 + (line & 1)) + 4 * block
        hot_pool[:, span] = ones_where(iota((64, 128), 0) == line)

    whole_loop(16, pick, 8)
    gather_tp = ones_where(iota((16, 128), 0) == (iota((16, 128), 1) >> 4))
    base = dot(gather_tp, flags).astype(bf16)
    holder, column = iota((128, 64), 0), iota((128, 64), 1)
    pooled = ones_where((holder < 32) & (((holder >> 4) * 2 + (holder & 1)) == (column & 3)))
    needed = dot_nt(hot_tp[...], hot_pool[...]) + dot(base, pooled)
    needed = jnp.max(jnp.max(needed, axis=0, keepdims=True), axis=1, keepdims=True)
    enough = (sheet[96:97, 0:1] < 8 * SLOTS) & (needed <= float(KEPT))
    fits[0, 0] = jnp.max(jnp.where(enough, 1, 0))

    looked = dot(position.astype(bf16), holders[...]) * quads[...].astype(f32)
    line = jnp.sum(looked, axis=0, keepdims=True)
    found = [line[:, block * 128 : (block + 1) * 128] for block in range(19)]
    found = jnp.concatenate(found + [jnp.zeros((5, 128), f32)], axis=0)
    blank = jnp.zeros((5, 128), jnp.int32)
    quad_rows = jnp.concatenate([sheet[0:16, :], blank[:2], sheet[pl.ds(own, 1), :], blank], axis=0)
    holder_rows = jnp.concatenate([sheet[32:48, :], blank[:2], sheet[pl.ds(own + 32, 1), :], blank], axis=0)
    tp_rows = quad_rows >> 4
    source = ((holder_rows >> 4) * 2 + (holder_rows & 1)) * 4 + (tp_rows >> 1)
    side = jnp.where((tp_rows & 1) == core, 0, SIDE)
    final = found + (source * KEPT + side).astype(f32)
    tp_index = ex * 2 + core
    turned = pltpu.roll(final, (128 - tp_index * 16) % 128, 1)
    turned = jnp.where(iota((24, 128), 1) < 16, turned, -1.0)
    final = jnp.where(iota((24, 128), 0) == 18, turned, final)
    final = jnp.concatenate([final, jnp.zeros((104, 128), f32)], axis=0)
    columns[...] = jnp.transpose(final).astype(jnp.int32)
    few = (16, 128)
    for part in range(2):
        sheet_b[...] = positions[part]
        mine = sheet_b[pl.ds(pl.multiple_of(tp_index * 16, 16), 16), :].astype(bf16)
        spread = dot(mine, ones_where(up == (ylo * 8 + (down >> 4)) * 2 + section))
        spread = jnp.where((iota(few, 1) & 15) == iota(few, 0), spread, 0.0)
        kept[part : part + 1, :] = jnp.sum(spread, axis=0, keepdims=True)


def finish_kernel(parts, gain, sent):
    latent = parts[0]
    for tp in range(1, parts.shape[0]):
        latent = latent + parts[tp]
    plain = latent[:, :LAT]
    scaled = plain * lax.rsqrt(jnp.mean(plain * plain, axis=-1, keepdims=True) + norm_eps) * gain[...]
    rotary = latent[:, LAT:]
    coarse = rotary.astype(bf16)
    fine = (rotary - coarse.astype(f32)).astype(bf16)
    row = jnp.concatenate([scaled.astype(bf16), coarse, fine], axis=-1)
    for peer in range(sent.shape[0]):
        sent[peer] = row


def keep_kernel(kept, rows, sent, here, sems):
    copies = []
    for ylo in range(2):
        chosen = iota((KEPT, 128), 0).astype(f32) == kept[ylo : ylo + 1, :]
        here[ylo] = dot(ones_where(chosen), rows[...]).astype(bf16)
        for peer in range(8):
            place = ylo * 8 + peer
            copies.append(pltpu.make_async_copy(here.at[ylo], sent.at[place], sems.at[place]))
            copies[-1].start()
    for copy in copies:
        copy.wait()


def cache_kernel(lengths, query, cache, out, level):
    length = lengths[pl.program_id(0)]
    scores = dot(query[0], cache[0]) * base_two
    scores = jnp.where(iota(scores.shape, 1) < length, scores, masked_fill)
    highest = jnp.max(scores, axis=-1, keepdims=True)
    weights = jnp.exp2(scores - highest)
    total = jnp.sum(weights, axis=-1, keepdims=True)
    out[...] = (dot_nt(weights.astype(bf16), cache[0, :LAT, :]) * (1.0 / total)).astype(bf16)
    level[...] = jnp.broadcast_to(highest + jnp.log2(total), level.shape)


def hot_rows(hot, columns, prompt, side, part):
    turned = pltpu.roll(columns[...], (128 - prompt * 8) % 128, 1) - side * SIDE
    for block in range(part * 4, part * 4 + 4):
        hot[block * 128 : (block + 1) * 128, :] = ones_where(iota((128, SIDE), 1) == turned[:, block : block + 1])
    return hot[part * 512 : (part + 1) * 512, :]


def fresh_hot(columns, side):
    return ones_where(iota((128, SIDE), 1) == columns[:, 18:19] - side * SIDE)


def empty_kernel(*refs):
    pass


def fresh_hot(columns, side):
    return ones_where(iota((128, SIDE), 1) == columns[:, 18:19] - side * SIDE)


def put_keys(keys, span, found, factor):
    turning = found[:, LAT:]
    turning = turning + pltpu.roll(turning, 64, 1)
    turned = turning * factor + pltpu.roll(turning, 32, 1) * pltpu.roll(factor, 64, 1)
    keys[span, :LAT] = found[:, :LAT].astype(bf16)
    keys[span, LAT:] = turned[:, : KVW - LAT].astype(bf16)


def copy_in(source, target, sem):
    copy = pltpu.make_async_copy(source, target, sem)
    copy.start()
    copy.wait()


def weigh(scores, old):
    new = jnp.maximum(old, jnp.max(scores, axis=-1, keepdims=True))
    weights = jnp.exp2(scores - new)
    return new, jnp.exp2(old - new), jnp.sum(weights, axis=-1, keepdims=True), weights.astype(bf16)


def near_kernel(place, slots, columns, near, hot):
    group = place[0] * 8 + place[1]

    @pl.when(place[4] == 1)
    def _():
        near[KEYS : KEYS + 128, :] = dot(fresh_hot(columns, 0), slots[...]).astype(bf16)

    def open_prompt(prompt):
        @pl.when((place[4] == 0) | (place[5 + prompt] == group))
        def _():
            for part in range(2):
                some = hot_rows(hot, columns, prompt, 0, part)
                near[aligned(prompt * 2 + part, 512), :] = dot(some, slots[...]).astype(bf16)

    whole_loop(2, open_prompt)


def decode_kernel(
    place, fits, near, others, columns, new_factors, factors_far, query_far, earlier_far, level_far, spare, spare_new,
    out, out_here, factors, query, earlier, level, keys, hot, highest, total, mixed, sem, in_sems, out_sems
):
    group = place[0] * 8 + place[1]
    fitting = fits[0, 0] == 1

    @pl.when(place[4] == 1)
    def _():
        loads = [
            pltpu.make_async_copy(source, target, in_sems.at[index])
            for index, (source, target) in enumerate(
                ((factors_far, factors), (query_far, query), (level_far, level), (earlier_far, earlier))
            )
        ]
        for load in loads:
            load.start()

        span = slice(KEYS, KEYS + 128)
        found = near[span, :].astype(f32) + dot(fresh_hot(columns, 1), others[...])
        put_keys(keys, span, found, new_factors[...])
        loads[0].wait()

        def open_prompt(prompt):
            @pl.when(place[5 + prompt] == group)
            def _():
                for part in range(2):
                    span = aligned(prompt * 2 + part, 512)
                    found = near[span, :].astype(f32) + dot(hot_rows(hot, columns, prompt, 1, part), others[...])
                    put_keys(keys, span, found, factors[part * 512 : (part + 1) * 512, :])

        whole_loop(2, open_prompt)

        @pl.when(jnp.logical_not(fitting))
        def _():
            copy_in(spare, keys.at[pl.ds(0, KEYS)], sem)
            copy_in(spare_new, keys.at[pl.ds(KEYS, 128)], sem)

        for load in loads[1:]:
            load.wait()
        newest = keys[KEYS : KEYS + 128, :]

        def begin(piece):
            span = aligned(piece, 256)
            scores = dot_nt(query[span, :], newest) * base_two
            key = iota(scores.shape, 1)
            row = iota(scores.shape, 0) & 15
            allowed = ((key >> 1) == (row >> 1)) & ((key & 1) <= (row & 1))
            scores = jnp.where(allowed, scores, masked_fill)
            new, factor, summed, weights = weigh(scores, level[span, 0:1])
            mixed[span, :] = earlier[span, :].astype(f32) * factor + dot(weights, newest[:, :LAT])
            highest[span, :] = jnp.broadcast_to(new, (256, 128))
            total[span, :] = jnp.broadcast_to(factor + summed, (256, 128))

        whole_loop(4, begin, 4)

        def add_prompt(prompt):
            @pl.when(place[5 + prompt] == group)
            def _():
                def add_part(piece):
                    span = aligned(piece, 256)
                    some = keys[aligned(prompt, 1024), :]
                    new, factor, summed, weights = weigh(dot_nt(query[span, :], some) * base_two, highest[span, 0:1])
                    mixed[span, :] = mixed[span, :] * factor + dot(weights, some[:, :LAT])
                    highest[span, :] = jnp.broadcast_to(new, (256, 128))
                    total[span, :] = total[span, :] * factor + summed

                whole_loop(4, add_part, 4)

        whole_loop(2, add_prompt)

        def out_copy(tp):
            rows = aligned(tp, 16)
            return pltpu.make_async_copy(out_here.at[rows], out.at[rows], out_sems.at[tp])

        def tp_rows(tp):
            for head in range(8):
                rows = pl.ds(pl.multiple_of(tp * 128 + head * 16, 16), 16)
                some = mixed[rows, :] * (1.0 / total[rows, 0:1])
                out_here[aligned(tp, 16), head * LAT : (head + 1) * LAT] = some.astype(bf16)
            out_copy(tp).start()

        whole_loop(8, tp_rows, 2)
        whole_loop(8, lambda tp: out_copy(tp).wait())


def prefill_kernel(place, fits, near, others, columns, factors, query, spare, out, keys, hot, mixed, pairs, sem):
    group = place[0] * 8 + place[1]
    fitting = fits[0, 0] == 1

    @pl.when(place[4] == 0)
    def _():
        def add_prompt(prompt):
            for part in range(2):
                span = slice(part * 512, (part + 1) * 512)
                found = near[aligned(prompt * 2 + part, 512), :].astype(f32)
                found = found + dot(hot_rows(hot, columns, prompt, 1, part), others[...])
                put_keys(keys, span, found, factors[span, :])

            @pl.when(jnp.logical_not(fitting))
            def _():
                copy_in(spare.at[pl.ds(prompt * 1024, 1024)], keys, sem)

            span = aligned(prompt, 512)
            some = keys[...]
            scores = dot_nt(query[span, :], some) * base_two
            last = (iota((512, 1), 0) & 63) + group * 64
            scores = jnp.where(iota(scores.shape, 1) <= last, scores, masked_fill)
            _, _, summed, weights = weigh(scores, jnp.full((512, 1), masked_fill, f32))
            added = dot(weights, some[:, :LAT]) * (1.0 / summed)
            for column in range(4):
                mixed[column, span, :] = added[:, column * 128 : (column + 1) * 128]

        whole_loop(2, add_prompt)

        def head_rows(head):
            for column in range(4):
                for prompt in range(2):
                    start = pl.multiple_of(prompt * 512 + head * 64, 64)
                    pairs[column, pl.ds(prompt, 64, stride=2), :] = mixed[column, pl.ds(start, 64), :]
                out[:, pl.ds(pl.multiple_of(head * LAT + column * 128, 128), 128)] = pairs[column].astype(bf16)

        whole_loop(8, head_rows, 2)


def join_kernel(place, prefilled, turned, out, sems):
    @pl.when(place[4] == 1)
    def _():
        copies = []
        for part in range(4):
            span = pl.ds(part * 32, 32)
            copies.append(pltpu.make_async_copy(turned.at[span], out.at[span], sems.at[part]))
        for copy in copies:
            copy.start()
        for copy in copies:
            copy.wait()


def rope_factors(position):
    frequency = np.float32(rope_base) ** (-np.arange(32, dtype=np.float32) / np.float32(32))
    angles = position[:, None] * frequency[None, :]
    if isinstance(position, np.ndarray):
        angles = angles.astype(np.float32).astype(np.float64)
        cosine, sine = np.cos(angles), np.sin(angles)
        return np.concatenate([cosine, cosine, -sine, sine], axis=-1).astype(np.float32)
    cosine, sine = jnp.cos(angles), jnp.sin(angles)
    return jnp.concatenate([cosine, cosine, -sine, sine], axis=-1)


def finish_keys(latent, latent_gain, position):
    plain = latent[:, :LAT]
    scaled = plain * lax.rsqrt(jnp.mean(plain * plain, axis=-1, keepdims=True) + norm_eps) * latent_gain
    factors = rope_factors(position.astype(f32))
    rotary = latent[:, LAT:]
    swapped = jnp.concatenate([rotary[:, 32:], rotary[:, :32]], axis=-1)
    turned = rotary * factors[:, :64] + swapped * factors[:, 64:]
    return jnp.concatenate([scaled, turned], axis=-1).astype(bf16)


def dense_keys(token_ids, place, embed_table, down, latent_gain, cache_length):
    group = place[0] * 8 + place[1]
    tp_index = place[2] * 2 + place[3]
    every = lax.all_to_all(jnp.broadcast_to(token_ids, (32, 128)).reshape(32, 1, 128), HOLDERS, 0, 0, tiled=True)
    local_row = every.reshape(-1) - (group * 2 + place[4]) * 2048
    inside = (local_row >= 0) & (local_row < 2048)
    picked = jnp.take(embed_table, jnp.clip(local_row, 0, 2047), axis=0)
    picked = jnp.where(inside[:, None], picked, jnp.zeros_like(picked)).reshape(32, 128, 896)
    embedded = jnp.sum(lax.all_to_all(picked, HOLDERS, 0, 0, tiled=True).astype(f32), axis=0).astype(bf16)
    partial = dot_nt(embedded, down)
    spread = jnp.broadcast_to(partial[None], (8, 128, KVW))
    latent = jnp.sum(lax.all_to_all(spread, TP, 0, 0, tiled=True), axis=0)
    index = jnp.arange(128, dtype=jnp.int32)
    mine = finish_keys(latent, latent_gain, group * 64 + index // 2)
    spread = jnp.broadcast_to(mine[None], (32, 128, KVW))
    prompts = lax.all_to_all(spread, HOLDERS, 0, 0, tiled=True).reshape(16, 2, 64, 2, KVW)[:, 0]
    prompts = jnp.transpose(prompts, (2, 0, 1, 3)).reshape(KEYS, KVW)
    own = lax.dynamic_slice_in_dim(latent, tp_index * 16, 16, 0)
    fresh = finish_keys(own, latent_gain, (cache_length[:, None] + jnp.arange(2, dtype=jnp.int32)[None]).reshape(-1))
    return prompts, jnp.concatenate([fresh, jnp.zeros((112, KVW), bf16)], axis=0)


def in_vmem(value):
    return pltpu.with_memory_space_constraint(value, VMEM)


def in_hbm(value):
    return pltpu.with_memory_space_constraint(value, pltpu.HBM)


def params(mebibytes):
    return pltpu.CompilerParams(vmem_limit_bytes=mebibytes * 1024 * 1024)


def shards(
    token_ids,
    embed_table,
    latent_down,
    latent_gain,
    prefill_query,
    decode_query,
    latent_cache,
    cache_length,
    prompt_owner,
):
    place = jnp.stack([lax.axis_index(name) for name in ("ylo", "z", "x", "core", "role")]).astype(jnp.int32)
    place = jnp.concatenate([place, prompt_owner])
    down = jnp.transpose(latent_down)
    whole = pl.BlockSpec(memory_space=VMEM)
    scalars = pl.BlockSpec(memory_space=SMEM)
    anywhere = pl.BlockSpec(memory_space=pl.ANY)
    shaped = jax.ShapeDtypeStruct

    spread = pl.pallas_call(
        spread_kernel,
        out_shape=shaped((32, 1, 128), jnp.int32),
        in_specs=[whole],
        out_specs=whole,
        compiler_params=params(4),
        name="spread_ids",
    )(token_ids)
    every = lax.all_to_all(spread, HOLDERS, 0, 0, tiled=True).reshape(32, 128)

    earlier, level = pl.pallas_call(
        cache_kernel,
        grid_spec=pltpu.PrefetchScalarGridSpec(
            num_scalar_prefetch=1,
            grid=(8,),
            in_specs=[
                pl.BlockSpec((1, 128, KVW), lambda row, lengths: (row, 0, 0)),
                pl.BlockSpec((1, KVW, 512), lambda row, lengths: (row, 0, 0)),
            ],
            out_specs=[
                pl.BlockSpec((128, LAT), lambda row, lengths: (row, 0)),
                pl.BlockSpec((128, 128), lambda row, lengths: (row, 0)),
            ],
        ),
        out_shape=(pltpu.HBM((1024, LAT), bf16), pltpu.HBM((1024, 128), f32)),
        compiler_params=params(12),
        cost_estimate=pl.CostEstimate(flops=12 * 10**8, bytes_accessed=7 * 10**6, transcendentals=524288),
        name="cache_rows",
    )(cache_length, in_hbm(decode_query.reshape(8, 128, KVW)), in_hbm(jnp.swapaxes(latent_cache, 1, 2)))
    every, earlier, level = lax.optimization_barrier((every, earlier, level))

    partial = pl.pallas_call(
        select_kernel,
        out_shape=shaped((8, SLOTS, KVW), f32),
        in_specs=[scalars, whole, anywhere, anywhere],
        out_specs=whole,
        scratch_shapes=[
            VMEM((16, 4096), bf16),
            VMEM((128, 4096), bf16),
            VMEM((8 * SLOTS, 2048), bf16),
            VMEM((2048, 896), bf16),
            VMEM((KVW, 896), bf16),
            pltpu.SemaphoreType.DMA((2,)),
        ],
        compiler_params=params(16),
        cost_estimate=pl.CostEstimate(flops=3 * 10**9, bytes_accessed=5 * 10**6, transcendentals=0),
        name="select_rows",
    )(place, every, in_hbm(embed_table), in_hbm(down))
    parts = lax.all_to_all(partial, TP, 0, 0, tiled=True)

    sheet = pl.pallas_call(
        rank_kernel,
        out_shape=shaped((104, 128), jnp.int32),
        in_specs=[whole],
        out_specs=whole,
        scratch_shapes=[VMEM((512, 4096), bf16), VMEM((128, 4096), bf16)],
        compiler_params=params(18),
        cost_estimate=pl.CostEstimate(flops=2 * 10**9, bytes_accessed=10**6, transcendentals=0),
        name="rank_rows",
    )(every)
    parts, sheet = lax.optimization_barrier((parts, sheet))
    sent = pl.pallas_call(
        finish_kernel,
        out_shape=shaped((8, SLOTS, WIDE), bf16),
        in_specs=[whole, whole],
        out_specs=whole,
        compiler_params=params(8),
        name="finish_rows",
    )(parts, latent_gain.reshape(1, LAT))
    arrived = lax.all_to_all(sent, "z", 0, 0, tiled=True)

    columns, kept, fits = pl.pallas_call(
        place_kernel,
        out_shape=(shaped((128, 128), jnp.int32), shaped((8, 128), f32), shaped((1, 1), jnp.int32)),
        in_specs=[scalars, whole],
        out_specs=(whole, whole, scalars),
        scratch_shapes=[
            VMEM((128, 19 * 128), bf16),
            VMEM((128, 19 * 128), bf16),
            VMEM((16, 2048), bf16),
            VMEM((64, 2048), bf16),
            VMEM((128, 128), f32),
        ],
        compiler_params=params(12),
        cost_estimate=pl.CostEstimate(flops=10**9, bytes_accessed=10**6, transcendentals=0),
        name="place_rows",
    )(place, sheet)
    handed = pl.pallas_call(
        keep_kernel,
        out_shape=pltpu.HBM((16, KEPT, WIDE), bf16),
        in_specs=[whole] * 2,
        out_specs=anywhere,
        scratch_shapes=[VMEM((2, KEPT, WIDE), bf16), pltpu.SemaphoreType.DMA((16,))],
        compiler_params=params(8),
        name="keep_rows",
    )(kept, arrived.reshape(8 * SLOTS, WIDE))
    handed, prompt_rows, decode_rows, lengths, earlier, level = lax.optimization_barrier(
        (handed, prefill_query, decode_query, cache_length, earlier, level)
    )
    slots = lax.all_to_all(handed, PLANE, 0, 0, tiled=True).reshape(SIDE, WIDE)

    def by_head(rows):
        return jnp.transpose(rows.reshape(16, 64, -1), (1, 0, 2)).reshape(1024, -1)

    row_query, earlier, level = by_head(decode_rows), by_head(earlier), by_head(level)
    new_position = (lengths[:, None] + jnp.arange(2, dtype=jnp.int32)[None]).reshape(-1)
    new_factors = jnp.pad(rope_factors(new_position.astype(f32)), ((0, 112), (0, 0)))
    prompt_query = jnp.transpose(prompt_rows.reshape(64, 2, 8, KVW), (1, 2, 0, 3)).reshape(1024, KVW)
    slots, prompt_query, row_query, earlier, level, new_factors = lax.optimization_barrier(
        (slots, prompt_query, row_query, earlier, level, new_factors)
    )
    others = lax.ppermute(slots, "core", [(0, 1), (1, 0)])

    spare, spare_new = lax.cond(
        fits[0, 0] == 1,
        lambda *unused: tuple(
            pl.pallas_call(
                empty_kernel,
                out_shape=[shaped((KEYS, KVW), bf16), shaped((128, KVW), bf16)],
                out_specs=[anywhere] * 2,
                name="no_keys",
            )()
        ),
        dense_keys,
        token_ids,
        place,
        embed_table,
        down,
        latent_gain,
        cache_length,
    )

    near = pl.pallas_call(
        near_kernel,
        out_shape=VMEM((KEYS + 128, WIDE), bf16),
        in_specs=[scalars, whole, whole],
        out_specs=whole,
        scratch_shapes=[VMEM((1024, SIDE), bf16)],
        compiler_params=params(12),
        cost_estimate=pl.CostEstimate(flops=2 * 10**9, bytes_accessed=10**6, transcendentals=0),
        name="near_keys",
    )(place, slots, columns)
    factors = jnp.asarray(rope_factors(np.arange(1024, dtype=np.float32)))
    decoded = pl.pallas_call(
        decode_kernel,
        out_shape=pltpu.HBM((128, 4096), bf16),
        in_specs=[scalars] * 2 + [whole] * 4 + [anywhere] * 6,
        out_specs=anywhere,
        scratch_shapes=[
            VMEM((128, 4096), bf16),
            VMEM((1024, 128), f32),
            VMEM((1024, KVW), bf16),
            VMEM((1024, LAT), bf16),
            VMEM((1024, 128), f32),
            VMEM((KEYS + 128, KVW), bf16),
            VMEM((1024, SIDE), bf16),
            VMEM((1024, 128), f32),
            VMEM((1024, 128), f32),
            VMEM((1024, LAT), f32),
            pltpu.SemaphoreType.DMA,
            pltpu.SemaphoreType.DMA((4,)),
            pltpu.SemaphoreType.DMA((8,)),
        ],
        compiler_params=params(24),
        cost_estimate=pl.CostEstimate(flops=5 * 10**9, bytes_accessed=7 * 10**6, transcendentals=10**6),
        name="decode_rows",
    )(
        place, fits, in_vmem(near), in_vmem(others), columns, new_factors, in_hbm(factors),
        in_hbm(row_query), in_hbm(earlier), in_hbm(level), in_hbm(spare), in_hbm(spare_new),
    )
    turned = lax.all_to_all(decoded.reshape(8, 16, 4096), TP, 0, 0, tiled=True).reshape(128, 4096)
    prefilled = pl.pallas_call(
        prefill_kernel,
        out_shape=pltpu.HBM((128, 4096), bf16),
        in_specs=[scalars] * 2 + [whole] * 5 + [anywhere],
        out_specs=whole,
        scratch_shapes=[
            VMEM((1024, KVW), bf16),
            VMEM((1024, SIDE), bf16),
            VMEM((4, 1024, 128), f32),
            VMEM((4, 128, 128), f32),
            pltpu.SemaphoreType.DMA,
        ],
        compiler_params=params(20),
        cost_estimate=pl.CostEstimate(flops=7 * 10**9, bytes_accessed=7 * 10**6, transcendentals=10**6),
        name="prefill_rows",
    )(place, fits, in_vmem(near), in_vmem(others), columns, in_vmem(factors), in_vmem(prompt_query), in_hbm(spare))
    out = pl.pallas_call(
        join_kernel,
        out_shape=pltpu.HBM((128, 4096), bf16),
        in_specs=[scalars] + [anywhere] * 2,
        out_specs=anywhere,
        scratch_shapes=[pltpu.SemaphoreType.DMA((4,))],
        input_output_aliases={1: 0},
        compiler_params=params(4),
        name="join_rows",
    )(place, in_hbm(prefilled), turned)
    return out[None]


def solution(mesh):
    fine_mesh = Mesh(mesh.devices.reshape(2, 8, 4, 2, 2), ("ylo", "z", "x", "core", "role"))
    ctx, tp = ("ylo", "z"), ("x", "core")
    in_specs = (
        P("role", ctx),
        P(ctx + ("role",), tp),
        P(tp, None),
        P(),
        P(ctx, tp, None),
        P(ctx + tp, None, None, None),
        P(ctx + tp, None, None),
        P(ctx + tp),
        P(),
    )
    out_specs = P("role", ctx, tp)
    return jax.shard_map(shards, mesh=fine_mesh, in_specs=in_specs, out_specs=out_specs, check_vma=False)
```
